128 devices in a mesh: ctx: 16 (over y, z_hi, core), tp: 8 (over x, z_lo).
Axes of the slice: x: 4, y: 4, z: 4 (z_hi: 2, z_lo: 2; z = z_hi * 2 + z_lo), core: 2. Of those that a mesh axis runs over, the one named last changes fastest.
Arguments:
- query: bfloat16 [4096, 5120], P('ctx', 'tp'), may hold values from -6 to 6
- key_projected: bfloat16 [4096, 1024], P('ctx', 'tp'), may hold values from -6 to 6
- value: bfloat16 [4096, 1024], P('ctx', 'tp'), may hold values from -6 to 6
- attention_output: bfloat16 [4096, 5120], P('ctx', 'tp'), may hold values from -6 to 6
- output_gradient: bfloat16 [4096, 5120], P('ctx', 'tp'), may hold values from -6 to 6
- lse: float32 [40, 4096], P('tp', 'ctx'), may hold values from 4 to 7
- block_mask: int32 [32, 32], replicated, may hold values from 0 to 1, as said below
- positions: int32 [4096], P('ctx'), may hold values from 0 to 1023, as said below
- segments: int32 [4096], replicated, may hold values from 0 to 63, as said below
- w_query: bfloat16 [5120, 5120], P(None, 'tp'), may hold values from -0.078125 to 0.078125
- key_weight: bfloat16 [5120, 1024], P(None, 'tp'), may hold values from -0.078125 to 0.078125
- value_weight: bfloat16 [5120, 1024], P(None, 'tp'), may hold values from -0.078125 to 0.078125
Outputs:
- input_grad_t: bfloat16 [5120, 4096], P('tp', 'ctx')
The draws below stay inside these ranges and needn't reach their ends.
Inputs may be any that keep to these rules, and one draw needn't show every extreme that they name: block_mask[a, b] is 1 exactly when tile b is tile a or an ancestor of tile a in a forest of tiles in which every tile's parent is an earlier tile. `positions`: a token's position is 128 times its tile's number of ancestors plus its offset from the first token of its segment within the tile. `segments`: never falling along the tokens; one segment a tile, except that a tile that is no other tile's ancestor may hold two, the second beginning inside it.
All inputs are finite; a program needn't handle non-finite values.
Results may differ from the reference program's by a relative error of at most 0.0065.
The reference program's roundings to bfloat16 on the way count: a program that leaves them out, or rounds other values in their place, can miss the bound.
Values may be sent and summed in bfloat16 or wider, within the bound.
No kernel may reach another device: no remote copies, remote signals or barrier semaphores. Data moves between devices by JAX's collectives and lax.ppermute only.
A program may use at most 128 MiB of HBM per device.

```python
import jax
import jax.numpy as jnp
from jax import lax

MODEL_WIDTH = 5120
QUERY_HEADS = 40
KEY_VALUE_HEADS = 8
HEAD_SIZE = 128
TILE = 128
PACKED_TOKENS = 4096


def tree_parts(key):
    tiles = PACKED_TOKENS // TILE
    levels = 8
    first, second, third = jax.random.split(key, 3)
    index = jnp.arange(tiles).astype(jnp.int32)
    raw = jax.random.randint(first, (tiles,), 0, 1 << 30)
    choices_count = jnp.maximum(index - 1, 0) // levels + 1
    parent = index - 1 - levels * (raw % choices_count)
    parent = jnp.where(index % levels == 0, index, parent).astype(jnp.int32)
    ancestors = ((index[None, :] == parent[:, None]) | (index[None, :] == index[:, None])).astype(jnp.int32)
    for _ in range(int(tiles).bit_length() + 1):
        ancestors = (jnp.dot(ancestors, ancestors) > 0).astype(jnp.int32)
    has_child = jnp.zeros((tiles,), jnp.int32).at[parent].max(jnp.where(parent != index, 1, 0).astype(jnp.int32))
    cut_point = jax.random.randint(second, (tiles,), 1, TILE)
    split_tile = (jax.random.randint(third, (tiles,), 0, 2) == 1) & (has_child == 0) & (index != levels - 1)
    split_tile = split_tile | (index == tiles - 1)
    depth = jnp.sum(ancestors, axis=1) - 1
    offset = jnp.arange(TILE).astype(jnp.int32)
    later = split_tile[:, None] & (offset[None, :] >= cut_point[:, None])
    seg_ids = (2 * index[:, None] + later.astype(jnp.int32)).reshape(-1)
    pos_ids = (TILE * depth[:, None] + jnp.where(later, offset[None, :] - cut_point[:, None], offset[None, :])).reshape(-1)
    return (ancestors.astype(jnp.int32), pos_ids.astype(jnp.int32), seg_ids.astype(jnp.int32))


def draw_block_mask(key, part):
    ancestors, pos_ids, seg_ids = tree_parts(key)
    return ancestors


def draw_positions(key, part):
    ancestors, pos_ids, seg_ids = tree_parts(key)
    return pos_ids


def draw_segments(key, part):
    ancestors, pos_ids, seg_ids = tree_parts(key)
    return seg_ids


def block_scale(rng, shape, shards, low, largest):
    def one(axis_at, shards_of):
        heights = jax.random.uniform(jax.random.fold_in(jax.random.fold_in(rng, 6), axis_at), (shards_of,), jnp.float32, low / len(shards), largest / len(shards))
        return jnp.repeat(jnp.exp(heights), shape[axis_at] // shards_of).reshape((-1,) + (1,) * (len(shape) - axis_at - 1))

    factor_of = one(*shards[0])
    for cut in shards[1:]:
        factor_of = factor_of * one(*cut)
    return factor_of


def gaussian(stream_key, shape, deviation, bound, pieces=(), held_as=jnp.bfloat16):
    values = jax.random.normal(stream_key, shape, jnp.float32) * deviation
    if len(pieces) > 0:
        values = block_scale(stream_key, shape, pieces, -0.22, 0.18) * values
    return jnp.clip(values, min=-bound, max=bound).astype(held_as)


def setup_inputs(seed: int = 0) -> dict:
    arg_keys = jax.random.split(jax.random.key(seed), 13)
    return {
        "query": gaussian(arg_keys[0], (PACKED_TOKENS, QUERY_HEADS * HEAD_SIZE), 1.0, 6.0, ((0, 16), (1, 8))),
        "key_projected": gaussian(arg_keys[1], (PACKED_TOKENS, KEY_VALUE_HEADS * HEAD_SIZE), 1.0, 6.0, ((0, 16), (1, 8))),
        "value": gaussian(arg_keys[2], (PACKED_TOKENS, KEY_VALUE_HEADS * HEAD_SIZE), 1.0, 6.0, ((0, 16), (1, 8))),
        "attention_output": gaussian(arg_keys[3], (PACKED_TOKENS, QUERY_HEADS * HEAD_SIZE), 1.0, 6.0, ((0, 16), (1, 8))),
        "output_gradient": gaussian(arg_keys[4], (PACKED_TOKENS, QUERY_HEADS * HEAD_SIZE), 1.0, 6.0, ((0, 16), (1, 8))),
        "lse": jnp.clip(4.0 + 3.0 * jax.random.uniform(arg_keys[5], (QUERY_HEADS, PACKED_TOKENS), jnp.float32) ** block_scale(arg_keys[5], (QUERY_HEADS, PACKED_TOKENS), ((0, 8), (1, 16)), -0.2, 0.2), 4.0, 7.0),
        "block_mask": draw_block_mask(jax.random.fold_in(arg_keys[12], 71), 0),
        "positions": draw_positions(jax.random.fold_in(arg_keys[12], 71), 0),
        "segments": draw_segments(jax.random.fold_in(arg_keys[12], 71), 0),
        "w_query": gaussian(arg_keys[9], (MODEL_WIDTH, QUERY_HEADS * HEAD_SIZE), MODEL_WIDTH ** -0.5, 0.078125, ((1, 8),)),
        "key_weight": gaussian(arg_keys[10], (MODEL_WIDTH, KEY_VALUE_HEADS * HEAD_SIZE), MODEL_WIDTH ** -0.5, 0.078125, ((1, 8),)),
        "value_weight": gaussian(arg_keys[11], (MODEL_WIDTH, KEY_VALUE_HEADS * HEAD_SIZE), MODEL_WIDTH ** -0.5, 0.078125, ((1, 8),)),
    }


rope_base = 1000000.0


def rope_tables(positions, head_dim):
    half = head_dim // 2
    exponent = jnp.arange(half).astype(jnp.float32) * (2.0 / head_dim)
    inverse = jnp.power(jnp.float32(rope_base), -exponent)
    angles = positions.astype(jnp.float32)[:, None] * inverse[None, :]
    cosine_table = jnp.cos(angles)
    sine_table = jnp.sin(angles)
    return jnp.concatenate([cosine_table, cosine_table], 1), jnp.concatenate([sine_table, sine_table], 1)


def rotate_forward(values, cosine_table, sine_table):
    half = values.shape[-1] // 2
    turned = jnp.concatenate([-values[..., half:], values[..., :half]], -1)
    return values * cosine_table[:, None, :] + turned * sine_table[:, None, :]


def unrotate_halves(grads, cosine_table, sine_table):
    half = grads.shape[-1] // 2
    scaled = grads * sine_table[:, None, :]
    turned = jnp.concatenate([scaled[..., half:], -scaled[..., :half]], -1)
    return grads * cosine_table[:, None, :] + turned


def pair_mask(block_mask, segments, q_start, q_count, k_start, k_count, tile):
    q_start = jnp.asarray(q_start).astype(jnp.int32)
    k_start = jnp.asarray(k_start).astype(jnp.int32)
    table = lax.dynamic_slice(block_mask, (q_start // tile, k_start // tile), (q_count // tile, k_count // tile))
    wide = jnp.broadcast_to(table[:, None, :, None], (q_count // tile, tile, k_count // tile, tile)).reshape(q_count, k_count) > 0
    q_index = q_start + jnp.arange(q_count).astype(jnp.int32)
    k_index = k_start + jnp.arange(k_count).astype(jnp.int32)
    seg_query = lax.dynamic_slice_in_dim(segments, q_start, q_count)
    seg_key = lax.dynamic_slice_in_dim(segments, k_start, k_count)
    same_tile = (q_index[:, None] // tile) == (k_index[None, :] // tile)
    inner = (k_index[None, :] <= q_index[:, None]) & (seg_query[:, None] == seg_key[None, :])
    return wide & (jnp.logical_not(same_tile) | inner)


def reference(query, key_projected, value, attention_output, output_gradient, lse, block_mask, positions, segments, w_query, key_weight, value_weight):
    grand_total = PACKED_TOKENS
    query_groups = QUERY_HEADS // KEY_VALUE_HEADS
    logit_scale = HEAD_SIZE ** -0.5
    cosine_table, sine_table = rope_tables(positions, HEAD_SIZE)
    query_rotated = rotate_forward(query.astype(jnp.float32).reshape(grand_total, QUERY_HEADS, HEAD_SIZE), cosine_table, sine_table).astype(jnp.bfloat16)
    query_rotated = query_rotated.reshape(grand_total, KEY_VALUE_HEADS, query_groups, HEAD_SIZE)
    key_rotated = rotate_forward(key_projected.astype(jnp.float32).reshape(grand_total, KEY_VALUE_HEADS, HEAD_SIZE), cosine_table, sine_table).astype(jnp.bfloat16)
    head_gradient = output_gradient.reshape(grand_total, KEY_VALUE_HEADS, query_groups, HEAD_SIZE)
    row_dot_delta = jnp.sum(head_gradient.astype(jnp.float32) * attention_output.reshape(grand_total, KEY_VALUE_HEADS, query_groups, HEAD_SIZE).astype(jnp.float32), -1)
    row_logsumexp = lse.T.reshape(grand_total, KEY_VALUE_HEADS, query_groups)
    key_float = key_rotated.astype(jnp.float32)
    value_single = value.reshape(grand_total, KEY_VALUE_HEADS, HEAD_SIZE).astype(jnp.float32)

    def step(carry, index):
        start = (index * TILE).astype(jnp.int32)
        query_blk = lax.dynamic_slice_in_dim(query_rotated, start, TILE, 0).astype(jnp.float32)
        grad_blk = lax.dynamic_slice_in_dim(head_gradient, start, TILE, 0).astype(jnp.float32)
        lse_blk = lax.dynamic_slice_in_dim(row_logsumexp, start, TILE, 0)
        delta_blk = lax.dynamic_slice_in_dim(row_dot_delta, start, TILE, 0)
        allowed = pair_mask(block_mask, segments, start, TILE, 0, grand_total, TILE)
        scores = jnp.einsum('tkgd,skd->tkgs', query_blk, key_float) * logit_scale
        probs = jnp.where(allowed[:, None, None, :], jnp.exp(scores - lse_blk[..., None]), 0.0)
        dprobs = jnp.einsum('tkgd,skd->tkgs', grad_blk, value_single)
        dscore = probs * (dprobs - delta_blk[..., None])
        probs_bf = lax.optimization_barrier(probs.astype(jnp.bfloat16)).astype(jnp.float32)
        dscore_bf = lax.optimization_barrier(dscore.astype(jnp.bfloat16)).astype(jnp.float32)
        query_part = jnp.einsum('tkgs,skd->tkgd', dscore_bf, key_float) * logit_scale
        key_accumulator = carry[0] + jnp.einsum('tkgs,tkgd->skd', dscore_bf, query_blk)
        value_accumulator = carry[1] + jnp.einsum('tkgs,tkgd->skd', probs_bf, grad_blk)
        return (key_accumulator, value_accumulator), query_part

    zero_filled = jnp.zeros((grand_total, KEY_VALUE_HEADS, HEAD_SIZE), jnp.float32)
    (key_accumulator, value_accumulator), query_parts = lax.scan(step, (zero_filled, zero_filled), jnp.arange(grand_total // TILE).astype(jnp.int32))
    query_rot_grad = query_parts.reshape(grand_total, QUERY_HEADS, HEAD_SIZE)
    query_grad = unrotate_halves(query_rot_grad, cosine_table, sine_table).astype(jnp.bfloat16).reshape(grand_total, QUERY_HEADS * HEAD_SIZE)
    key_gradient = unrotate_halves(key_accumulator * logit_scale, cosine_table, sine_table).astype(jnp.bfloat16).reshape(grand_total, KEY_VALUE_HEADS * HEAD_SIZE)
    value_gradient = value_accumulator.astype(jnp.bfloat16).reshape(grand_total, KEY_VALUE_HEADS * HEAD_SIZE)
    result = jnp.dot(w_query, query_grad.T, preferred_element_type=jnp.float32)
    result = result + jnp.dot(key_weight, key_gradient.T, preferred_element_type=jnp.float32)
    result = result + jnp.dot(value_weight, value_gradient.T, preferred_element_type=jnp.float32)
    return result.astype(jnp.bfloat16)
```

```python
import numpy as np
import jax
import jax.numpy as jnp
from jax import lax
from jax.experimental import pallas as pl
from jax.experimental.pallas import tpu as pltpu
from jax.sharding import Mesh, PartitionSpec as P

HEAD = 128
TILE = 128
GROUPS = 5
TOK = 256
TILES = 32
ROWS = GROUPS * TILE
SCALE = HEAD**-0.5
ROPE_BASE = 1000000.0
CTX = ("y", "zh", "core")
TP = ("x", "zl")
SLOTS = ((0, 0), (0, 1), (1, 0), (3, 0), (2, 0), (1, 1), (3, 1), (2, 1))

f32 = jnp.float32
bf16 = jnp.bfloat16


def shift(x, axes, sizes, offs):
    perm = []
    for source in np.ndindex(*sizes):
        dest = tuple((a + o) % s for a, o, s in zip(source, offs, sizes))
        perm.append(
            (int(np.ravel_multi_index(source, sizes)), int(np.ravel_multi_index(dest, sizes)))
        )
    return lax.ppermute(x, axes, perm)


def shift_y(x, k):
    return shift(x, ("y",), (4,), (k % 4,))


def swap_zh(x):
    return shift(x, ("zh",), (2,), (1,))


def swap_core(x):
    return shift(x, ("core",), (2,), (1,))


def rope_tables(positions):
    half = HEAD // 2
    exponent = jnp.arange(half).astype(f32) * (2.0 / HEAD)
    inverse = jnp.power(f32(ROPE_BASE), -exponent)
    angles = positions.astype(f32)[:, None] * inverse[None, :]
    cosine, sine = jnp.cos(angles), jnp.sin(angles)
    return jnp.concatenate([cosine, cosine], 1), jnp.concatenate([sine, sine], 1)


def half_sign(shape, axis):
    return jnp.where(lax.broadcasted_iota(jnp.int32, shape, axis) < HEAD // 2, -1.0, 1.0).astype(f32)


def prep_kernel(query, grad, att, cos, sin, q_rows, q_cols, g_rows, g_cols, delta):
    sign = half_sign((TILE, HEAD), 1)
    for t in range(2):
        tok = pl.ds(t * TILE, TILE)
        c, s = cos[tok, :], sin[tok, :] * sign
        for h in range(GROUPS):
            feat = pl.ds(h * HEAD, HEAD)
            lane = pl.ds(h * TILE, TILE)
            x = query[tok, feat].astype(f32)
            rot = (x * c + pltpu.roll(x, HEAD // 2, 1) * s).astype(bf16)
            q_rows[t, lane, :] = rot
            q_cols[t, :, lane] = rot.T
            g = grad[tok, feat]
            g_rows[t, lane, :] = g
            g_cols[t, :, lane] = g.T
            prod = g.astype(f32) * att[tok, feat].astype(f32)
            delta[t, :, lane] = jnp.sum(prod.T, axis=0, keepdims=True)


def attention_kernel(
    mask, info, seg, lse, delta, cos, sin, q_rows, q_cols, g_rows, g_cols, kv_mine, kv_other,
    dkv_mine, dkv_other, qg, kv, dkv, acc, dq, sem,
):
    first = pltpu.make_async_copy(kv_mine, kv.at[pl.ds(0, 8 * TOK)], sem.at[0])
    second = pltpu.make_async_copy(kv_other, kv.at[pl.ds(8 * TOK, 8 * TOK)], sem.at[1])
    first.start()
    second.start()
    dq[...] = jnp.zeros_like(dq)
    first.wait()
    second.wait()
    q_tile = info[TILES]

    def pair(t, start, allowed):
        keys = kv[pl.ds(start, TILE), :HEAD]
        vals = kv[pl.ds(start, TILE), HEAD:]
        keys_t = keys.T
        scores = jnp.dot(keys, q_cols[t], preferred_element_type=f32)
        probs = jnp.exp(scores * SCALE - lse[t])
        if allowed is not None:
            probs = jnp.where(allowed, probs, 0.0)
        dprobs = jnp.dot(vals, g_cols[t], preferred_element_type=f32)
        dscore = (probs * (dprobs - delta[t])).astype(bf16)
        probs = probs.astype(bf16)
        dq[t] += jnp.dot(keys_t, dscore, preferred_element_type=f32)
        acc[:, :HEAD] += jnp.dot(dscore, q_rows[t], preferred_element_type=f32)
        acc[:, HEAD:] += jnp.dot(probs, g_rows[t], preferred_element_type=f32)

    def step(j, carry):
        tile = info[j]
        need0 = mask[q_tile, tile] > 0
        need1 = mask[q_tile + 1, tile] > 0
        start = pl.multiple_of(j * TILE, TILE)

        @pl.when(need0 | need1)
        def _():
            acc[...] = jnp.zeros_like(acc)
            for t, need in ((0, need0), (1, need1)):
                diagonal = need & (tile == q_tile + t)

                @pl.when(need & jnp.logical_not(diagonal))
                def _():
                    pair(t, start, None)

                @pl.when(diagonal)
                def _():
                    row = jnp.broadcast_to(seg[t], (TILE, TILE))
                    causal = lax.broadcasted_iota(jnp.int32, (TILE, TILE), 0) <= (
                        lax.broadcasted_iota(jnp.int32, (TILE, TILE), 1)
                    )
                    one = jnp.where((row.T == row) & causal, 1.0, 0.0)
                    pair(t, start, jnp.concatenate([one] * GROUPS, 1) > 0.5)

            dkv[pl.ds(start, TILE), :] = acc[...].astype(bf16)

        @pl.when(jnp.logical_not(need0 | need1))
        def _():
            dkv[pl.ds(start, TILE), :] = jnp.zeros((TILE, 2 * HEAD), bf16)

        return carry

    lax.fori_loop(0, TILES, step, 0)
    first = pltpu.make_async_copy(dkv.at[pl.ds(0, 8 * TOK)], dkv_mine, sem.at[0])
    second = pltpu.make_async_copy(dkv.at[pl.ds(8 * TOK, 8 * TOK)], dkv_other, sem.at[1])
    second.start()
    first.start()
    sign = half_sign((HEAD, TILE), 0)
    for t in range(2):
        tok = pl.ds(t * TILE, TILE)
        c, s = cos[tok, :].T, sin[tok, :].T
        for h in range(GROUPS):
            g = dq[t, :, pl.ds(h * TILE, TILE)] * SCALE
            u = g * s
            half = HEAD // 2
            turned = jnp.concatenate([u[half:], -u[:half]], 0)
            qg[pl.ds(h * HEAD, HEAD), tok] = (g * c + turned).astype(bf16)
    first.wait()
    second.wait()


def vmem(n):
    return [pl.BlockSpec(memory_space=pltpu.VMEM)] * n


def prep(query, grad, att, cos, sin):
    s = jax.ShapeDtypeStruct
    return pl.pallas_call(
        prep_kernel,
        out_shape=(
            s((2, ROWS, HEAD), bf16),
            s((2, HEAD, ROWS), bf16),
            s((2, ROWS, HEAD), bf16),
            s((2, HEAD, ROWS), bf16),
            s((2, 1, ROWS), f32),
        ),
        in_specs=vmem(5),
        out_specs=tuple(vmem(5)),
        compiler_params=pltpu.CompilerParams(vmem_limit_bytes=32 << 20),
        cost_estimate=pl.CostEstimate(flops=10000000, bytes_accessed=3000000, transcendentals=0),
        name="prep",
    )(query, grad, att, cos, sin)


def attention(mask, info, seg, lse, delta, cos, sin, q_rows, q_cols, g_rows, g_cols, mine, other):
    s = jax.ShapeDtypeStruct
    smem = [pl.BlockSpec(memory_space=pltpu.SMEM)] * 2
    hbm = [pl.BlockSpec(memory_space=pl.ANY)] * 2
    return pl.pallas_call(
        attention_kernel,
        out_shape=(
            s((8 * TOK, 2 * HEAD), bf16),
            s((8 * TOK, 2 * HEAD), bf16),
            s((ROWS, TOK), bf16),
        ),
        in_specs=smem + vmem(9) + hbm,
        out_specs=tuple(hbm + vmem(1)),
        scratch_shapes=[
            pltpu.VMEM((16 * TOK, 2 * HEAD), bf16),
            pltpu.VMEM((16 * TOK, 2 * HEAD), bf16),
            pltpu.VMEM((TILE, 2 * HEAD), f32),
            pltpu.VMEM((2, HEAD, ROWS), f32),
            pltpu.SemaphoreType.DMA((2,)),
        ],
        compiler_params=pltpu.CompilerParams(vmem_limit_bytes=48 << 20),
        cost_estimate=pl.CostEstimate(
            flops=2000000000, bytes_accessed=8000000, transcendentals=1000000
        ),
        name="attention",
    )(mask, info, seg, lse, delta, cos, sin, q_rows, q_cols, g_rows, g_cols, mine, other)


def local(
    query, key, value, att, grad, lse, block_mask, positions, segments, w_query, key_weight,
    value_weight,
):
    y, zh, core = lax.axis_index("y"), lax.axis_index("zh"), lax.axis_index("core")
    me = lax.axis_index(CTX)
    cos, sin = rope_tables(positions)
    half = HEAD // 2
    key_f = key.astype(f32)
    turned = jnp.concatenate([-key_f[:, half:], key_f[:, :half]], 1)
    key_rot = (key_f * cos + turned * sin).astype(bf16)
    block = jnp.concatenate([key_rot, value], 1)

    across = swap_zh(block)
    near = [shift_y(block, k) for k in (1, 3, 2)]
    far = [shift_y(across, k) for k in (1, 3, 2)]
    q_rows, q_cols, g_rows, g_cols, delta = prep(query, grad, att, cos, sin)
    mine = jnp.concatenate([block, across] + near + far, 0)
    other = swap_core(mine)

    owners = [
        ((y - dy) % 4) * 4 + ((zh - dz) % 2) * 2 + (core + dc) % 2
        for dc in (0, 1)
        for dy, dz in SLOTS
    ]
    tiles = (2 * jnp.stack(owners)[:, None] + jnp.arange(2)[None, :]).reshape(-1)
    info = jnp.concatenate([tiles, 2 * me[None]]).astype(jnp.int32)
    seg = lax.dynamic_slice_in_dim(segments, me * TOK, TOK).astype(f32).reshape(2, 1, TILE)
    lse_rows = lse.reshape(GROUPS, 2, TILE).transpose(1, 0, 2).reshape(2, 1, ROWS)
    dkv_mine, dkv_other, query_grad = attention(
        block_mask, info, seg, lse_rows, delta, cos, sin, q_rows, q_cols, g_rows, g_cols, mine, other
    )

    summed = dkv_mine.astype(f32) + swap_core(dkv_other).astype(f32)
    parts = lax.optimization_barrier(summed.astype(bf16)).reshape(8, TOK, 2 * HEAD)
    far = [shift_y(parts[5 + i], -k) for i, k in enumerate((1, 3, 2))]
    near = [shift_y(parts[2 + i], -k) for i, k in enumerate((1, 3, 2))]
    across = parts[1].astype(f32) + sum(p.astype(f32) for p in far)
    across = swap_zh(lax.optimization_barrier(across.astype(bf16)))
    total = parts[0].astype(f32) + across.astype(f32) + sum(p.astype(f32) for p in near)

    key_rot_grad = total[:, :HEAD] * SCALE
    u = key_rot_grad * sin
    key_grad = (
        key_rot_grad * cos + jnp.concatenate([u[:, half:], -u[:, :half]], 1)
    ).astype(bf16)
    value_grad = total[:, HEAD:].astype(bf16)

    result = jnp.dot(w_query, query_grad, preferred_element_type=f32)
    contract = (((1,), (1,)), ((), ()))
    result = result + lax.dot_general(key_weight, key_grad, contract, preferred_element_type=f32)
    result = result + lax.dot_general(
        value_weight, value_grad, contract, preferred_element_type=f32
    )
    send = lax.optimization_barrier(result.astype(bf16)).reshape(8, 640, TOK)
    got = lax.all_to_all(send, TP, 0, 0)
    return jnp.sum(got.astype(f32), 0).astype(bf16)


def solution(mesh):
    fine = Mesh(mesh.devices.reshape(4, 2, 2, 4, 2), ("y", "zh", "core", "x", "zl"))
    in_specs = (
        P(CTX, TP),
        P(CTX, TP),
        P(CTX, TP),
        P(CTX, TP),
        P(CTX, TP),
        P(TP, CTX),
        P(),
        P(CTX),
        P(),
        P(None, TP),
        P(None, TP),
        P(None, TP),
    )
    return jax.shard_map(
        local, mesh=fine, in_specs=in_specs, out_specs=P(TP, CTX), check_vma=False
    )
```

```python
import numpy as np
import jax
import jax.numpy as jnp
from jax import lax
from jax.experimental import pallas as pl
from jax.experimental.pallas import tpu as pltpu
from jax.sharding import Mesh, PartitionSpec as P

HEAD = 128
TILE = 128
GROUPS = 5
TOK = 256
TILES = 32
ROWS = GROUPS * TILE
SCALE = HEAD**-0.5
ROPE_BASE = 1000000.0
CTX = ("y", "zh", "core")
TP = ("x", "zl")

f32 = jnp.float32
bf16 = jnp.bfloat16


def shift(x, axes, sizes, offs):
    perm = []
    for source in np.ndindex(*sizes):
        dest = tuple((a + o) % s for a, o, s in zip(source, offs, sizes))
        perm.append(
            (int(np.ravel_multi_index(source, sizes)), int(np.ravel_multi_index(dest, sizes)))
        )
    return lax.ppermute(x, axes, perm)


def shift_y(x, k):
    return shift(x, ("y",), (4,), (k % 4,))


def swap_zh(x):
    return shift(x, ("zh",), (2,), (1,))


def swap_core(x):
    return shift(x, ("core",), (2,), (1,))


INVERSE = np.power(np.float64(ROPE_BASE), -np.arange(HEAD // 2) * (2.0 / HEAD)).astype(np.float32)


def half_sign(shape, axis):
    return jnp.where(lax.broadcasted_iota(jnp.int32, shape, axis) < HEAD // 2, -1.0, 1.0).astype(f32)


def block_kernel(key, value, positions, inverse, cos, sin, block):
    sign = half_sign((TILE, HEAD), 1)
    for t in range(2):
        tok = pl.ds(t * TILE, TILE)
        place = jnp.broadcast_to(positions[t], (TILE, TILE)).T
        angles = place * inverse[...]
        c, s = jnp.cos(angles), jnp.sin(angles)
        cos[tok, :] = c
        sin[tok, :] = s
        x = key[tok, :].astype(f32)
        block[tok, :HEAD] = (x * c + pltpu.roll(x, HEAD // 2, 1) * (s * sign)).astype(bf16)
        block[tok, HEAD:] = value[tok, :]


def prep_kernel(query, grad, att, cos, sin, q_rows, q_cols, g_rows, g_cols, delta):
    sign = half_sign((TILE, HEAD), 1)
    for t in range(2):
        tok = pl.ds(t * TILE, TILE)
        c, s = cos[tok, :], sin[tok, :] * sign
        for h in range(GROUPS):
            feat = pl.ds(h * HEAD, HEAD)
            lane = pl.ds(h * TILE, TILE)
            x = query[tok, feat].astype(f32)
            rot = (x * c + pltpu.roll(x, HEAD // 2, 1) * s).astype(bf16)
            q_rows[t, lane, :] = rot
            q_cols[t, :, lane] = rot.T
            g = grad[tok, feat]
            g_rows[t, lane, :] = g
            g_cols[t, :, lane] = g.T
            prod = g.astype(f32) * att[tok, feat].astype(f32)
            delta[t, :, lane] = jnp.sum(prod.T, axis=0, keepdims=True)


def attention_kernel(
    mask, info, seg, lse, delta, cos, sin, q_rows, q_cols, g_rows, g_cols, kv_mine, kv_other,
    dkv_mine, dkv_other, qg, kv, dkv, acc, dq, sem,
):
    first = pltpu.make_async_copy(kv_mine, kv.at[pl.ds(0, 8 * TOK)], sem.at[0])
    second = pltpu.make_async_copy(kv_other, kv.at[pl.ds(8 * TOK, 8 * TOK)], sem.at[1])
    first.start()
    second.start()
    dq[...] = jnp.zeros_like(dq)
    first.wait()
    second.wait()
    me = info[0]
    q_tile = 2 * me

    def pair(t, start, allowed):
        keys = kv[pl.ds(start, TILE), :HEAD]
        vals = kv[pl.ds(start, TILE), HEAD:]
        keys_t = keys.T
        scores = jnp.dot(keys, q_cols[t], preferred_element_type=f32)
        probs = jnp.exp(scores * SCALE - lse[t])
        if allowed is not None:
            probs = jnp.where(allowed, probs, 0.0)
        dprobs = jnp.dot(vals, g_cols[t], preferred_element_type=f32)
        dscore = (probs * (dprobs - delta[t])).astype(bf16)
        probs = probs.astype(bf16)
        dq[t] += jnp.dot(keys_t, dscore, preferred_element_type=f32)
        acc[:, :HEAD] += jnp.dot(dscore, q_rows[t], preferred_element_type=f32)
        acc[:, HEAD:] += jnp.dot(probs, g_rows[t], preferred_element_type=f32)

    def step(j, carry):
        slot = lax.shift_right_logical(j, 1)
        back_y = (lax.shift_right_logical(me, 2) - slot) & 3
        back_rest = (me ^ (lax.shift_right_logical(slot, 1) & 2)) & 2
        back_core = (me ^ lax.shift_right_logical(slot, 3)) & 1
        tile = 2 * (4 * back_y + back_rest + back_core) + (j & 1)
        need0 = mask[q_tile, tile] > 0
        need1 = mask[q_tile + 1, tile] > 0
        start = pl.multiple_of(j * TILE, TILE)

        @pl.when(need0 | need1)
        def _():
            acc[...] = jnp.zeros_like(acc)
            for t, need in ((0, need0), (1, need1)):
                diagonal = need & (tile == q_tile + t)

                @pl.when(need & jnp.logical_not(diagonal))
                def _():
                    pair(t, start, None)

                @pl.when(diagonal)
                def _():
                    row = jnp.broadcast_to(seg[t], (TILE, TILE))
                    causal = lax.broadcasted_iota(jnp.int32, (TILE, TILE), 0) <= (
                        lax.broadcasted_iota(jnp.int32, (TILE, TILE), 1)
                    )
                    one = jnp.where((row.T == row) & causal, 1.0, 0.0)
                    pair(t, start, jnp.concatenate([one] * GROUPS, 1) > 0.5)

            dkv[pl.ds(start, TILE), :] = acc[...].astype(bf16)

        @pl.when(jnp.logical_not(need0 | need1))
        def _():
            dkv[pl.ds(start, TILE), :] = jnp.zeros((TILE, 2 * HEAD), bf16)

        return carry

    lax.fori_loop(0, TILES, step, 0)
    first = pltpu.make_async_copy(dkv.at[pl.ds(0, 8 * TOK)], dkv_mine, sem.at[0])
    second = pltpu.make_async_copy(dkv.at[pl.ds(8 * TOK, 8 * TOK)], dkv_other, sem.at[1])
    second.start()
    first.start()
    sign = half_sign((HEAD, TILE), 0)
    for t in range(2):
        tok = pl.ds(t * TILE, TILE)
        c, s = cos[tok, :].T, sin[tok, :].T
        for h in range(GROUPS):
            g = dq[t, :, pl.ds(h * TILE, TILE)] * SCALE
            u = g * s
            half = HEAD // 2
            turned = jnp.concatenate([u[half:], -u[:half]], 0)
            qg[pl.ds(h * HEAD, HEAD), tok] = (g * c + turned).astype(bf16)
    first.wait()
    second.wait()


def vmem(n):
    return [pl.BlockSpec(memory_space=pltpu.VMEM)] * n


def prep(query, grad, att, cos, sin):
    s = jax.ShapeDtypeStruct
    return pl.pallas_call(
        prep_kernel,
        out_shape=(
            s((2, ROWS, HEAD), bf16),
            s((2, HEAD, ROWS), bf16),
            s((2, ROWS, HEAD), bf16),
            s((2, HEAD, ROWS), bf16),
            s((2, 1, ROWS), f32),
        ),
        in_specs=vmem(5),
        out_specs=tuple(vmem(5)),
        compiler_params=pltpu.CompilerParams(vmem_limit_bytes=32 << 20),
        cost_estimate=pl.CostEstimate(flops=10000000, bytes_accessed=3000000, transcendentals=0),
        name="prep",
    )(query, grad, att, cos, sin)


def attention(mask, info, seg, lse, delta, cos, sin, q_rows, q_cols, g_rows, g_cols, mine, other):
    s = jax.ShapeDtypeStruct
    smem = [pl.BlockSpec(memory_space=pltpu.SMEM)] * 2
    hbm = [pl.BlockSpec(memory_space=pl.ANY)] * 2
    return pl.pallas_call(
        attention_kernel,
        out_shape=(
            s((8 * TOK, 2 * HEAD), bf16),
            s((8 * TOK, 2 * HEAD), bf16),
            s((ROWS, TOK), bf16),
        ),
        in_specs=smem + vmem(9) + hbm,
        out_specs=tuple(hbm + vmem(1)),
        scratch_shapes=[
            pltpu.VMEM((16 * TOK, 2 * HEAD), bf16),
            pltpu.VMEM((16 * TOK, 2 * HEAD), bf16),
            pltpu.VMEM((TILE, 2 * HEAD), f32),
            pltpu.VMEM((2, HEAD, ROWS), f32),
            pltpu.SemaphoreType.DMA((2,)),
        ],
        compiler_params=pltpu.CompilerParams(vmem_limit_bytes=48 << 20),
        cost_estimate=pl.CostEstimate(
            flops=2000000000, bytes_accessed=8000000, transcendentals=1000000
        ),
        name="attention",
    )(mask, info, seg, lse, delta, cos, sin, q_rows, q_cols, g_rows, g_cols, mine, other)


def make_block(key, value, positions):
    s = jax.ShapeDtypeStruct
    inverse = jnp.asarray(np.concatenate([INVERSE, INVERSE])[None, :])
    return pl.pallas_call(
        block_kernel,
        out_shape=(s((TOK, HEAD), f32), s((TOK, HEAD), f32), s((TOK, 2 * HEAD), bf16)),
        in_specs=vmem(4),
        out_specs=tuple(vmem(3)),
        cost_estimate=pl.CostEstimate(flops=5000000, bytes_accessed=700000, transcendentals=60000),
        name="block",
    )(key, value, positions.astype(f32).reshape(2, 1, TILE), inverse)


WIDTH = 5120
STEP_ROWS = 640


def project_kernel(
    own, across, near1, near2, near3, cos, sin, qg, wq, wk, wv, out, kg, vg
):
    @pl.when(pl.program_id(0) == 0)
    def _():
        total = own[...].astype(f32) + across[...].astype(f32)
        total += near1[...].astype(f32) + near2[...].astype(f32) + near3[...].astype(f32)
        sign = half_sign((TOK, HEAD), 1)
        g = total[:, :HEAD] * SCALE
        key_grad = g * cos[...] - pltpu.roll(g * sin[...], HEAD // 2, 1) * sign
        kg[...] = key_grad.T.astype(bf16)
        vg[...] = total[:, HEAD:].T.astype(bf16)

    result = jnp.dot(wq[...], qg[...], preferred_element_type=f32)
    result += jnp.dot(wk[...], kg[...], preferred_element_type=f32)
    result += jnp.dot(wv[...], vg[...], preferred_element_type=f32)
    out[...] = result.astype(bf16)


def project(own, across, near, cos, sin, qg, wq, wk, wv):
    def whole(shape):
        return pl.BlockSpec(shape, lambda i: (0, 0))

    def rows(width):
        return pl.BlockSpec((STEP_ROWS, width), lambda i: (i, 0))

    return pl.pallas_call(
        project_kernel,
        grid=(WIDTH // STEP_ROWS,),
        out_shape=jax.ShapeDtypeStruct((WIDTH, TOK), bf16),
        in_specs=[whole((TOK, 2 * HEAD))] * 5
        + [whole((TOK, HEAD))] * 2
        + [whole((ROWS, TOK)), rows(ROWS), rows(HEAD), rows(HEAD)],
        out_specs=rows(TOK),
        scratch_shapes=[pltpu.VMEM((HEAD, TOK), bf16), pltpu.VMEM((HEAD, TOK), bf16)],
        compiler_params=pltpu.CompilerParams(vmem_limit_bytes=32 << 20),
        cost_estimate=pl.CostEstimate(
            flops=2350000000, bytes_accessed=12000000, transcendentals=0
        ),
        name="project",
    )(own, across, *near, cos, sin, qg, wq, wk, wv)


def last_kernel(parts, out):
    total = parts[0].astype(f32)
    for i in range(1, 8):
        total += parts[i].astype(f32)
    out[...] = total.astype(bf16)


def last_sum(parts):
    return pl.pallas_call(
        last_kernel,
        grid=(5,),
        out_shape=jax.ShapeDtypeStruct((640, TOK), bf16),
        in_specs=[pl.BlockSpec((8, 128, TOK), lambda i: (0, i, 0))],
        out_specs=pl.BlockSpec((128, TOK), lambda i: (i, 0)),
        cost_estimate=pl.CostEstimate(flops=1300000, bytes_accessed=3000000, transcendentals=0),
        name="last_sum",
    )(parts)


def local(
    query, key, value, att, grad, lse, block_mask, positions, segments, w_query, key_weight,
    value_weight,
):
    me = lax.axis_index(CTX)
    cos, sin, block = make_block(key, value, positions)

    across = swap_zh(block)
    near = [shift_y(block, k) for k in (1, 2, 3)]
    info = me.reshape(1)
    seg = lax.dynamic_slice_in_dim(segments, me * TOK, TOK).astype(f32).reshape(2, 1, TILE)
    lse_rows = lse.reshape(GROUPS, 2, TILE).transpose(1, 0, 2).reshape(2, 1, ROWS)
    ready = (info, seg, lse_rows, *prep(query, grad, att, cos, sin))
    across, ready = lax.optimization_barrier((across, ready))
    info, seg, lse_rows, q_rows, q_cols, g_rows, g_cols, delta = ready
    far = [shift_y(across, k) for k in (1, 2, 3)]
    mine = jnp.concatenate([block] + near + [across] + far, 0)
    other = swap_core(mine)

    dkv_mine, dkv_other, query_grad = attention(
        block_mask, info, seg, lse_rows, delta, cos, sin, q_rows, q_cols, g_rows, g_cols, mine, other
    )

    summed = dkv_mine.astype(f32) + swap_core(dkv_other).astype(f32)
    parts = lax.optimization_barrier(summed.astype(bf16)).reshape(8, TOK, 2 * HEAD)
    far = [shift_y(parts[4 + k], -k) for k in (1, 2, 3)]
    near = [shift_y(parts[k], -k) for k in (1, 2, 3)]
    across = parts[4].astype(f32) + sum(p.astype(f32) for p in far)
    across = swap_zh(lax.optimization_barrier(across.astype(bf16)))
    send = project(
        parts[0], across, near, cos, sin, query_grad, w_query, key_weight, value_weight
    )
    return last_sum(lax.all_to_all(send.reshape(8, 640, TOK), TP, 0, 0))


def solution(mesh):
    fine = Mesh(mesh.devices.reshape(4, 2, 2, 4, 2), ("y", "zh", "core", "x", "zl"))
    in_specs = (
        P(CTX, TP),
        P(CTX, TP),
        P(CTX, TP),
        P(CTX, TP),
        P(CTX, TP),
        P(TP, CTX),
        P(),
        P(CTX),
        P(),
        P(None, TP),
        P(None, TP),
        P(None, TP),
    )
    return jax.shard_map(
        local, mesh=fine, in_specs=in_specs, out_specs=P(TP, CTX), check_vma=False
    )
```

```python
import numpy as np
import jax
import jax.numpy as jnp
from jax import lax
from jax.experimental import pallas as pl
from jax.experimental.pallas import tpu as pltpu
from jax.sharding import Mesh, PartitionSpec as P

HEAD = 128
TILE = 128
GROUPS = 5
TOK = 256
TILES = 32
ROWS = GROUPS * TILE
SCALE = HEAD**-0.5
ROPE_BASE = 1000000.0
CTX = ("y", "zh", "core")
TP = ("x", "zl")

f32 = jnp.float32
bf16 = jnp.bfloat16


def shift(x, axes, sizes, offs):
    perm = []
    for source in np.ndindex(*sizes):
        dest = tuple((a + o) % s for a, o, s in zip(source, offs, sizes))
        perm.append(
            (int(np.ravel_multi_index(source, sizes)), int(np.ravel_multi_index(dest, sizes)))
        )
    return lax.ppermute(x, axes, perm)


def shift_y(x, k):
    return shift(x, ("y",), (4,), (k % 4,))


def swap_zh(x):
    return shift(x, ("zh",), (2,), (1,))


def swap_core(x):
    return shift(x, ("core",), (2,), (1,))


INVERSE = np.power(np.float64(ROPE_BASE), -np.arange(HEAD // 2) * (2.0 / HEAD)).astype(np.float32)


def half_sign(shape, axis):
    return jnp.where(lax.broadcasted_iota(jnp.int32, shape, axis) < HEAD // 2, -1.0, 1.0).astype(f32)


def block_kernel(key, value, positions, inverse, cos, sin, block):
    sign = half_sign((TILE, HEAD), 1)
    for t in range(2):
        tok = pl.ds(t * TILE, TILE)
        place = jnp.broadcast_to(positions[t].astype(f32), (TILE, TILE)).T
        angles = place * inverse[...]
        c, s = jnp.cos(angles), jnp.sin(angles)
        cos[tok, :] = c
        sin[tok, :] = s
        x = key[tok, :].astype(f32)
        block[tok, :HEAD] = (x * c + pltpu.roll(x, HEAD // 2, 1) * (s * sign)).astype(bf16)
        block[tok, HEAD:] = value[tok, :]


def prep_kernel(joined, cos, sin, block, q_rows, q_cols, g_rows, g_cols, delta, again):
    again[...] = block[...]
    sign = half_sign((TILE, HEAD), 1)
    for t in range(2):
        tok = pl.ds(t * TILE, TILE)
        c, s = cos[tok, :], sin[tok, :] * sign
        for h in range(GROUPS):
            feat = pl.ds(h * HEAD, HEAD)
            lane = pl.ds(h * TILE, TILE)
            x = joined[tok, feat].astype(f32)
            rot = (x * c + pltpu.roll(x, HEAD // 2, 1) * s).astype(bf16)
            q_rows[t, lane, :] = rot
            q_cols[t, :, lane] = rot.T
            g = joined[tok, pl.ds(ROWS + h * HEAD, HEAD)]
            g_rows[t, lane, :] = g
            g_cols[t, :, lane] = g.T
            prod = g.astype(f32) * joined[tok, pl.ds(2 * ROWS + h * HEAD, HEAD)].astype(f32)
            delta[t, :, lane] = jnp.sum(prod.T, axis=0, keepdims=True)


def attention_kernel(
    mask, info, seg, lse, delta, cos, sin, q_rows, q_cols, g_rows, g_cols, kv_mine, kv_other,
    dkv_mine, dkv_other, qg, acc, dq, lse_rows,
):
    dq[...] = jnp.zeros_like(dq)
    for t in range(2):
        for h in range(GROUPS):
            lse_rows[t, :, pl.ds(h * TILE, TILE)] = lse[h : h + 1, t * TILE : (t + 1) * TILE]
    me = info[0]
    q_tile = 2 * me

    def pair(t, keys, vals, allowed):
        keys_t = keys.T
        scores = jnp.dot(keys, q_cols[t], preferred_element_type=f32)
        probs = jnp.exp(scores * SCALE - lse_rows[t])
        if allowed is not None:
            probs = jnp.where(allowed, probs, 0.0)
        dprobs = jnp.dot(vals, g_cols[t], preferred_element_type=f32)
        dscore = (probs * (dprobs - delta[t])).astype(bf16)
        probs = probs.astype(bf16)
        dq[t] += jnp.dot(keys_t, dscore, preferred_element_type=f32)
        acc[:, :HEAD] += jnp.dot(dscore, q_rows[t], preferred_element_type=f32)
        acc[:, HEAD:] += jnp.dot(probs, g_rows[t], preferred_element_type=f32)

    def tiles_of(kv, dkv, away):
        def step(j, carry):
            slot = lax.shift_right_logical(j, 1)
            back_y = (lax.shift_right_logical(me, 2) - slot) & 3
            back_zh = (me ^ (lax.shift_right_logical(slot, 1) & 2)) & 2
            tile = 2 * (4 * back_y + back_zh + ((me ^ away) & 1)) + (j & 1)
            need0 = mask[q_tile, tile] > 0
            need1 = mask[q_tile + 1, tile] > 0
            here = pl.ds(pl.multiple_of(j * TILE, TILE), TILE)

            @pl.when(need0 | need1)
            def _():
                acc[...] = jnp.zeros_like(acc)
                keys, vals = kv[here, :HEAD], kv[here, HEAD:]
                for t, need in ((0, need0), (1, need1)):
                    diagonal = need & (tile == q_tile + t)

                    @pl.when(need & jnp.logical_not(diagonal))
                    def _():
                        pair(t, keys, vals, None)

                    if away == 0:

                        @pl.when(diagonal)
                        def _():
                            row = jnp.broadcast_to(seg[tile], (TILE, TILE)).astype(f32)
                            causal = lax.broadcasted_iota(jnp.int32, (TILE, TILE), 0) <= (
                                lax.broadcasted_iota(jnp.int32, (TILE, TILE), 1)
                            )
                            one = jnp.where((row.T == row) & causal, 1.0, 0.0)
                            pair(t, keys, vals, jnp.concatenate([one] * GROUPS, 1) > 0.5)

                dkv[here, :] = acc[...].astype(bf16)

            @pl.when(jnp.logical_not(need0 | need1))
            def _():
                dkv[here, :] = jnp.zeros((TILE, 2 * HEAD), bf16)

            return carry

        lax.fori_loop(0, TILES // 2, step, 0)

    tiles_of(kv_mine, dkv_mine, 0)
    tiles_of(kv_other, dkv_other, 1)
    for t in range(2):
        tok = pl.ds(t * TILE, TILE)
        c, s = cos[tok, :].T, sin[tok, :].T
        for h in range(GROUPS):
            g = dq[t, :, pl.ds(h * TILE, TILE)] * SCALE
            u = g * s
            half = HEAD // 2
            turned = jnp.concatenate([u[half:], -u[:half]], 0)
            qg[pl.ds(h * HEAD, HEAD), tok] = (g * c + turned).astype(bf16)


def vmem(n):
    return [pl.BlockSpec(memory_space=pltpu.VMEM)] * n


def prep(joined, cos, sin, block):
    s = jax.ShapeDtypeStruct
    return pl.pallas_call(
        prep_kernel,
        out_shape=(
            s((2, ROWS, HEAD), bf16),
            s((2, HEAD, ROWS), bf16),
            s((2, ROWS, HEAD), bf16),
            s((2, HEAD, ROWS), bf16),
            s((2, 1, ROWS), f32),
            s((TOK, 2 * HEAD), bf16),
        ),
        in_specs=vmem(4),
        out_specs=tuple(vmem(6)),
        compiler_params=pltpu.CompilerParams(vmem_limit_bytes=32 << 20),
        cost_estimate=pl.CostEstimate(flops=10000000, bytes_accessed=3000000, transcendentals=0),
        name="prep",
    )(joined, cos, sin, block)


def attention(mask, info, seg, lse, delta, cos, sin, q_rows, q_cols, g_rows, g_cols, mine, other):
    s = jax.ShapeDtypeStruct
    smem = [pl.BlockSpec(memory_space=pltpu.SMEM)] * 2
    return pl.pallas_call(
        attention_kernel,
        out_shape=(
            s((8 * TOK, 2 * HEAD), bf16),
            s((8 * TOK, 2 * HEAD), bf16),
            s((ROWS, TOK), bf16),
        ),
        in_specs=smem + vmem(11),
        out_specs=tuple(vmem(3)),
        scratch_shapes=[
            pltpu.VMEM((TILE, 2 * HEAD), f32),
            pltpu.VMEM((2, HEAD, ROWS), f32),
            pltpu.VMEM((2, 1, ROWS), f32),
        ],
        compiler_params=pltpu.CompilerParams(vmem_limit_bytes=48 << 20),
        cost_estimate=pl.CostEstimate(
            flops=2000000000, bytes_accessed=8000000, transcendentals=1000000
        ),
        name="attention",
    )(mask, info, seg, lse, delta, cos, sin, q_rows, q_cols, g_rows, g_cols, mine, other)


def make_block(key, value, positions):
    s = jax.ShapeDtypeStruct
    inverse = jnp.asarray(np.concatenate([INVERSE, INVERSE])[None, :])
    return pl.pallas_call(
        block_kernel,
        out_shape=(s((TOK, HEAD), f32), s((TOK, HEAD), f32), s((TOK, 2 * HEAD), bf16)),
        in_specs=vmem(4),
        out_specs=tuple(vmem(3)),
        cost_estimate=pl.CostEstimate(flops=5000000, bytes_accessed=700000, transcendentals=60000),
        name="block",
    )(key, value, positions.reshape(2, 1, TILE), inverse)


WIDTH = 5120
STEP_ROWS = 640


def project_kernel(
    own, across, near1, near2, near3, cos, sin, qg, wq, wk, wv, out, kg, vg
):
    total = own[...].astype(f32) + across[...].astype(f32)
    total += near1[...].astype(f32) + near2[...].astype(f32) + near3[...].astype(f32)
    sign = half_sign((TOK, HEAD), 1)
    g = total[:, :HEAD] * SCALE
    key_grad = g * cos[...] - pltpu.roll(g * sin[...], HEAD // 2, 1) * sign
    kg[...] = key_grad.T.astype(bf16)
    vg[...] = total[:, HEAD:].T.astype(bf16)

    def step(i, carry):
        rows = pl.ds(pl.multiple_of(i * STEP_ROWS, STEP_ROWS), STEP_ROWS)
        result = jnp.dot(wq[rows, :], qg[...], preferred_element_type=f32)
        result += jnp.dot(wk[rows, :], kg[...], preferred_element_type=f32)
        result += jnp.dot(wv[rows, :], vg[...], preferred_element_type=f32)
        out[rows, :] = result.astype(bf16)
        return carry

    lax.fori_loop(0, WIDTH // STEP_ROWS, step, 0)


def project(own, across, near, cos, sin, qg, wq, wk, wv):
    return pl.pallas_call(
        project_kernel,
        out_shape=jax.ShapeDtypeStruct((WIDTH, TOK), bf16),
        in_specs=vmem(11),
        out_specs=vmem(1)[0],
        scratch_shapes=[pltpu.VMEM((HEAD, TOK), bf16), pltpu.VMEM((HEAD, TOK), bf16)],
        compiler_params=pltpu.CompilerParams(vmem_limit_bytes=40 << 20),
        cost_estimate=pl.CostEstimate(
            flops=2350000000, bytes_accessed=12000000, transcendentals=0
        ),
        name="project",
    )(own, across, *near, cos, sin, qg, wq, wk, wv)


def last_kernel(parts, out):
    def step(i, carry):
        rows = pl.ds(pl.multiple_of(i * TILE, TILE), TILE)
        total = parts[0, rows, :].astype(f32)
        for k in range(1, 8):
            total += parts[k, rows, :].astype(f32)
        out[rows, :] = total.astype(bf16)
        return carry

    lax.fori_loop(0, 5, step, 0)


def last_sum(parts):
    return pl.pallas_call(
        last_kernel,
        out_shape=jax.ShapeDtypeStruct((640, TOK), bf16),
        in_specs=vmem(1),
        out_specs=vmem(1)[0],
        compiler_params=pltpu.CompilerParams(vmem_limit_bytes=16 << 20),
        cost_estimate=pl.CostEstimate(flops=1300000, bytes_accessed=3000000, transcendentals=0),
        name="last_sum",
    )(parts)


def local(
    query, key, value, att, grad, lse, block_mask, positions, segments, w_query, key_weight,
    value_weight,
):
    me = lax.axis_index(CTX)
    cos, sin, block = make_block(key, value, positions)

    across = swap_zh(block)
    q_rows, q_cols, g_rows, g_cols, delta, again = prep(
        jnp.concatenate([query, grad, att], 1), cos, sin, block
    )
    near = [shift_y(again, k) for k in (1, 2, 3)]
    far = [shift_y(across, k) for k in (1, 2, 3)]
    mine = jnp.concatenate([block] + near + [across] + far, 0)
    other = swap_core(mine)

    dkv_mine, dkv_other, query_grad = attention(
        block_mask, me.reshape(1), segments.reshape(TILES, 1, TILE), lse, delta, cos, sin, q_rows,
        q_cols, g_rows, g_cols, mine, other,
    )

    summed = dkv_mine.astype(f32) + swap_core(dkv_other).astype(f32)
    parts = lax.optimization_barrier(summed.astype(bf16)).reshape(8, TOK, 2 * HEAD)
    far = [shift_y(parts[4 + k], -k) for k in (1, 2, 3)]
    across = parts[4].astype(f32) + sum(p.astype(f32) for p in far)
    across, rest = lax.optimization_barrier(
        (across.astype(bf16), (parts[1], parts[2], parts[3]))
    )
    near = [shift_y(rest[k - 1], -k) for k in (1, 2, 3)]
    across = swap_zh(across)
    send = project(
        parts[0], across, near, cos, sin, query_grad, w_query, key_weight, value_weight
    )
    return last_sum(lax.all_to_all(send.reshape(8, 640, TOK), TP, 0, 0))


def solution(mesh):
    fine = Mesh(mesh.devices.reshape(4, 2, 2, 4, 2), ("y", "zh", "core", "x", "zl"))
    in_specs = (
        P(CTX, TP),
        P(CTX, TP),
        P(CTX, TP),
        P(CTX, TP),
        P(CTX, TP),
        P(TP, CTX),
        P(),
        P(CTX),
        P(),
        P(None, TP),
        P(None, TP),
        P(None, TP),
    )
    return jax.shard_map(
        local, mesh=fine, in_specs=in_specs, out_specs=P(TP, CTX), check_vma=False
    )
```

```python
import functools

import numpy as np
import jax
import jax.numpy as jnp
from jax import lax
from jax.experimental import pallas as pl
from jax.experimental.pallas import tpu as pltpu
from jax.sharding import Mesh, PartitionSpec as P

HEAD = 128
TILE = 128
GROUPS = 5
TOK = 256
TILES = 32
ROWS = GROUPS * TILE
SCALE = HEAD**-0.5
ROPE_BASE = 1000000.0
CTX = ("y", "zh", "core")
TP = ("x", "zl")

f32 = jnp.float32
bf16 = jnp.bfloat16


def shift(x, axes, sizes, offs):
    perm = []
    for source in np.ndindex(*sizes):
        dest = tuple((a + o) % s for a, o, s in zip(source, offs, sizes))
        perm.append(
            (int(np.ravel_multi_index(source, sizes)), int(np.ravel_multi_index(dest, sizes)))
        )
    return lax.ppermute(x, axes, perm)


def shift_y(x, k):
    return shift(x, ("y",), (4,), (k % 4,))


def swap_zh(x):
    return shift(x, ("zh",), (2,), (1,))


def swap_core(x):
    return shift(x, ("core",), (2,), (1,))


INVERSE = np.power(np.float64(ROPE_BASE), -np.arange(HEAD // 2) * (2.0 / HEAD)).astype(np.float32)


def half_sign(shape, axis):
    return jnp.where(lax.broadcasted_iota(jnp.int32, shape, axis) < HEAD // 2, -1.0, 1.0).astype(f32)


def block_kernel(key, value, positions, inverse, cos, sin, block):
    sign = half_sign((TILE, HEAD), 1)
    for t in range(2):
        tok = pl.ds(t * TILE, TILE)
        place = jnp.broadcast_to(positions[t].astype(f32), (TILE, TILE)).T
        angles = place * inverse[...]
        c, s = jnp.cos(angles), jnp.sin(angles)
        cos[tok, :] = c
        sin[tok, :] = s
        x = key[tok, :].astype(f32)
        block[tok, :HEAD] = (x * c + pltpu.roll(x, HEAD // 2, 1) * (s * sign)).astype(bf16)
        block[tok, HEAD:] = value[tok, :]


def prep_kernel(joined, cos, sin, q_rows, q_cols, g_rows, g_cols, delta):
    sign = half_sign((TILE, HEAD), 1)
    for t in range(2):
        tok = pl.ds(t * TILE, TILE)
        c, s = cos[tok, :], sin[tok, :] * sign
        for h in range(GROUPS):
            feat = pl.ds(h * HEAD, HEAD)
            lane = pl.ds(h * TILE, TILE)
            x = joined[tok, feat].astype(f32)
            rot = (x * c + pltpu.roll(x, HEAD // 2, 1) * s).astype(bf16)
            q_rows[t, lane, :] = rot
            q_cols[t, :, lane] = rot.T
            g = joined[tok, pl.ds(ROWS + h * HEAD, HEAD)]
            g_rows[t, lane, :] = g
            g_cols[t, :, lane] = g.T
            prod = g.astype(f32) * joined[tok, pl.ds(2 * ROWS + h * HEAD, HEAD)].astype(f32)
            delta[t, :, lane] = jnp.sum(prod.T, axis=0, keepdims=True)


EARLY = 5


def attention_kernel(early, *refs):
    mask, info, seg, lse, delta, q_rows, q_cols, g_rows, g_cols, kv_mine, kv_other = refs[:11]
    if early:
        dkv_mine, dkv_other, dq, acc, lse_rows = refs[11:]
        dq[...] = jnp.zeros_like(dq)
    else:
        dq_in, cos, sin, dkv_mine, dkv_other, qg, acc, lse_rows, dq = refs[11:]
        dq[...] = dq_in[...]
    for t in range(2):
        for h in range(GROUPS):
            lse_rows[t, :, pl.ds(h * TILE, TILE)] = lse[h : h + 1, t * TILE : (t + 1) * TILE]
    me = info[0]
    q_tile = 2 * me
    first_slot = 0 if early else EARLY
    slots = EARLY if early else 8 - EARLY

    def pair(t, keys, vals, allowed):
        keys_t = keys.T
        scores = jnp.dot(keys, q_cols[t], preferred_element_type=f32)
        probs = jnp.exp(scores * SCALE - lse_rows[t])
        if allowed is not None:
            probs = jnp.where(allowed, probs, 0.0)
        dprobs = jnp.dot(vals, g_cols[t], preferred_element_type=f32)
        dscore = (probs * (dprobs - delta[t])).astype(bf16)
        probs = probs.astype(bf16)
        dq[t] += jnp.dot(keys_t, dscore, preferred_element_type=f32)
        acc[:, :HEAD] += jnp.dot(dscore, q_rows[t], preferred_element_type=f32)
        acc[:, HEAD:] += jnp.dot(probs, g_rows[t], preferred_element_type=f32)

    def tiles_of(kv, dkv, away):
        def step(j, carry):
            slot = lax.shift_right_logical(j, 1) + first_slot
            back_y = (lax.shift_right_logical(me, 2) - slot) & 3
            back_zh = (me ^ (lax.shift_right_logical(slot, 1) & 2)) & 2
            tile = 2 * (4 * back_y + back_zh + ((me ^ away) & 1)) + (j & 1)
            need0 = mask[q_tile, tile] > 0
            need1 = mask[q_tile + 1, tile] > 0
            here = pl.ds(pl.multiple_of(j * TILE, TILE), TILE)

            @pl.when(need0 | need1)
            def _():
                acc[...] = jnp.zeros_like(acc)
                keys, vals = kv[here, :HEAD], kv[here, HEAD:]
                for t, need in ((0, need0), (1, need1)):
                    diagonal = need & (tile == q_tile + t)

                    @pl.when(need & jnp.logical_not(diagonal))
                    def _():
                        pair(t, keys, vals, None)

                    if early and away == 0:

                        @pl.when(diagonal)
                        def _():
                            row = jnp.broadcast_to(seg[tile], (TILE, TILE)).astype(f32)
                            causal = lax.broadcasted_iota(jnp.int32, (TILE, TILE), 0) <= (
                                lax.broadcasted_iota(jnp.int32, (TILE, TILE), 1)
                            )
                            one = jnp.where((row.T == row) & causal, 1.0, 0.0)
                            pair(t, keys, vals, jnp.concatenate([one] * GROUPS, 1) > 0.5)

                dkv[here, :] = acc[...].astype(bf16)

            @pl.when(jnp.logical_not(need0 | need1))
            def _():
                dkv[here, :] = jnp.zeros((TILE, 2 * HEAD), bf16)

            return carry

        lax.fori_loop(0, 2 * slots, step, 0)

    tiles_of(kv_mine, dkv_mine, 0)
    tiles_of(kv_other, dkv_other, 1)
    if early:
        return
    for t in range(2):
        tok = pl.ds(t * TILE, TILE)
        c, s = cos[tok, :].T, sin[tok, :].T
        for h in range(GROUPS):
            g = dq[t, :, pl.ds(h * TILE, TILE)] * SCALE
            u = g * s
            half = HEAD // 2
            turned = jnp.concatenate([u[half:], -u[:half]], 0)
            qg[pl.ds(h * HEAD, HEAD), tok] = (g * c + turned).astype(bf16)


def vmem(n):
    return [pl.BlockSpec(memory_space=pltpu.VMEM)] * n


def prep(joined, cos, sin):
    s = jax.ShapeDtypeStruct
    return pl.pallas_call(
        prep_kernel,
        out_shape=(
            s((2, ROWS, HEAD), bf16),
            s((2, HEAD, ROWS), bf16),
            s((2, ROWS, HEAD), bf16),
            s((2, HEAD, ROWS), bf16),
            s((2, 1, ROWS), f32),
        ),
        in_specs=vmem(3),
        out_specs=tuple(vmem(5)),
        compiler_params=pltpu.CompilerParams(vmem_limit_bytes=32 << 20),
        cost_estimate=pl.CostEstimate(flops=1000000, bytes_accessed=10000, transcendentals=0),
        name="prep",
    )(joined, cos, sin)


def attention(early, mask, info, *operands):
    s = jax.ShapeDtypeStruct
    rows = (EARLY if early else 8 - EARLY) * TOK
    dq = (2, HEAD, ROWS)
    scratch = [pltpu.VMEM((TILE, 2 * HEAD), f32), pltpu.VMEM((2, 1, ROWS), f32)]
    return pl.pallas_call(
        functools.partial(attention_kernel, early),
        out_shape=(
            s((rows, 2 * HEAD), bf16),
            s((rows, 2 * HEAD), bf16),
            s(dq, f32) if early else s((ROWS, TOK), bf16),
        ),
        in_specs=[pl.BlockSpec(memory_space=pltpu.SMEM)] * 2 + vmem(len(operands)),
        out_specs=tuple(vmem(3)),
        scratch_shapes=scratch if early else scratch + [pltpu.VMEM(dq, f32)],
        compiler_params=pltpu.CompilerParams(vmem_limit_bytes=32 << 20),
        cost_estimate=pl.CostEstimate(flops=1000000, bytes_accessed=10000, transcendentals=0),
        name="early" if early else "late",
    )(mask, info, *operands)


def make_block(key, value, positions):
    s = jax.ShapeDtypeStruct
    inverse = jnp.asarray(np.concatenate([INVERSE, INVERSE])[None, :])
    return pl.pallas_call(
        block_kernel,
        out_shape=(s((TOK, HEAD), f32), s((TOK, HEAD), f32), s((TOK, 2 * HEAD), bf16)),
        in_specs=vmem(4),
        out_specs=tuple(vmem(3)),
        cost_estimate=pl.CostEstimate(flops=5000000, bytes_accessed=700000, transcendentals=60000),
        name="block",
    )(key, value, positions.reshape(2, 1, TILE), inverse)


def combine_kernel(early_mine, early_other, late_mine, late_other, own, across, *parts):
    def early(k):
        rows = pl.ds(k * TOK, TOK)
        return early_mine[rows, :].astype(f32) + early_other[rows, :].astype(f32)

    own[...] = early(0)
    across[...] = early(4)
    for k in range(3):
        rows = pl.ds(k * TOK, TOK)
        parts[k][:TOK, :] = early(k + 1).astype(bf16)
        late = late_mine[rows, :].astype(f32) + late_other[rows, :].astype(f32)
        parts[k][TOK:, :] = late.astype(bf16)


def combine(early_mine, early_other, late_mine, late_other):
    s = jax.ShapeDtypeStruct
    return pl.pallas_call(
        combine_kernel,
        out_shape=(
            [s((TOK, 2 * HEAD), f32)] * 2 + [s((2 * TOK, 2 * HEAD), bf16)] * 3
        ),
        in_specs=vmem(4),
        out_specs=vmem(5),
        cost_estimate=pl.CostEstimate(flops=1000000, bytes_accessed=10000, transcendentals=0),
        name="combine",
    )(early_mine, early_other, late_mine, late_other)


WIDTH = 5120
STEP_ROWS = 640


def project_kernel(
    own, across, near1, near2, near3, cos, sin, qg, wq, wk, wv, out, grads
):
    total = own[...].astype(f32) + across[...].astype(f32)
    for near in (near1, near2, near3):
        total += near[:TOK, :].astype(f32)
    sign = half_sign((TOK, HEAD), 1)
    g = total[:, :HEAD] * SCALE
    key_grad = g * cos[...] - pltpu.roll(g * sin[...], HEAD // 2, 1) * sign
    grads[:ROWS, :] = qg[...]
    grads[ROWS : ROWS + HEAD, :] = key_grad.T.astype(bf16)
    grads[ROWS + HEAD :, :] = total[:, HEAD:].T.astype(bf16)

    def step(i, carry):
        rows = pl.ds(pl.multiple_of(i * STEP_ROWS, STEP_ROWS), STEP_ROWS)
        weights = jnp.concatenate([wq[rows, :], wk[rows, :], wv[rows, :]], 1)
        result = jnp.dot(weights, grads[...], preferred_element_type=f32)
        out[rows, :] = result.astype(bf16)
        return carry

    lax.fori_loop(0, WIDTH // STEP_ROWS, step, 0)


def project(own, across, near, cos, sin, qg, wq, wk, wv):
    return pl.pallas_call(
        project_kernel,
        out_shape=jax.ShapeDtypeStruct((WIDTH, TOK), bf16),
        in_specs=vmem(11),
        out_specs=vmem(1)[0],
        scratch_shapes=[pltpu.VMEM((ROWS + 2 * HEAD, TOK), bf16)],
        compiler_params=pltpu.CompilerParams(vmem_limit_bytes=40 << 20),
        cost_estimate=pl.CostEstimate(
            flops=2350000000, bytes_accessed=12000000, transcendentals=0
        ),
        name="project",
    )(own, across, *near, cos, sin, qg, wq, wk, wv)


def last_kernel(parts, out):
    def step(i, carry):
        rows = pl.ds(pl.multiple_of(i * TILE, TILE), TILE)
        total = parts[0, rows, :].astype(f32)
        for k in range(1, 8):
            total += parts[k, rows, :].astype(f32)
        out[rows, :] = total.astype(bf16)
        return carry

    lax.fori_loop(0, 5, step, 0)


def last_sum(parts):
    return pl.pallas_call(
        last_kernel,
        out_shape=jax.ShapeDtypeStruct((640, TOK), bf16),
        in_specs=vmem(1),
        out_specs=vmem(1)[0],
        compiler_params=pltpu.CompilerParams(vmem_limit_bytes=16 << 20),
        cost_estimate=pl.CostEstimate(flops=1300000, bytes_accessed=3000000, transcendentals=0),
        name="last_sum",
    )(parts)


def local(
    query, key, value, att, grad, lse, block_mask, positions, segments, w_query, key_weight,
    value_weight,
):
    me = lax.axis_index(CTX)
    cos, sin, block = make_block(key, value, positions)

    across = swap_zh(block)
    joined = jnp.concatenate([query, grad, att], 1)
    joined, again = lax.optimization_barrier((joined, block))
    near = [shift_y(again, k) for k in (1, 2, 3)]
    across, joined = lax.optimization_barrier((across, joined))
    far = [shift_y(across, k) for k in (1, 2, 3)]
    ready, near = lax.optimization_barrier((prep(joined, cos, sin), near))
    q_rows, q_cols, g_rows, g_cols, delta = ready
    common = (
        block_mask, me.reshape(1), segments.reshape(TILES, 1, TILE), lse, delta, q_rows, q_cols,
        g_rows, g_cols,
    )

    mine = jnp.concatenate([block] + near + [across], 0)
    early_mine, early_other, dq = attention(True, *common, mine, swap_core(mine))
    dq, far = lax.optimization_barrier((dq, far))
    mine = jnp.concatenate(far, 0)
    late_mine, late_other, query_grad = attention(
        False, *common, mine, swap_core(mine), dq, cos, sin
    )

    own, across, *parts = combine(
        early_mine, swap_core(early_other), late_mine, swap_core(late_other)
    )
    got = [shift_y(parts[k - 1], -k) for k in (1, 2, 3)]
    across = across + sum(p[TOK:].astype(f32) for p in got)
    across = swap_zh(lax.optimization_barrier(across.astype(bf16)))
    send = project(own, across, got, cos, sin, query_grad, w_query, key_weight, value_weight)
    return last_sum(lax.all_to_all(send.reshape(8, 640, TOK), TP, 0, 0))


def solution(mesh):
    fine = Mesh(mesh.devices.reshape(4, 2, 2, 4, 2), ("y", "zh", "core", "x", "zl"))
    in_specs = (
        P(CTX, TP),
        P(CTX, TP),
        P(CTX, TP),
        P(CTX, TP),
        P(CTX, TP),
        P(TP, CTX),
        P(),
        P(CTX),
        P(),
        P(None, TP),
        P(None, TP),
        P(None, TP),
    )
    return jax.shard_map(
        local, mesh=fine, in_specs=in_specs, out_specs=P(TP, CTX), check_vma=False
    )
```

```python
import numpy as np
import jax
import jax.numpy as jnp
from jax import lax
from jax.experimental import pallas as pl
from jax.experimental.pallas import tpu as pltpu
from jax.sharding import Mesh, PartitionSpec as P

HEAD = 128
TILE = 128
GROUPS = 5
TOK = 256
TILES = 32
ROWS = GROUPS * TILE
SCALE = HEAD**-0.5
ROPE_BASE = 1000000.0
CTX = ("y", "zh", "core")
TP = ("x", "zl")

f32 = jnp.float32
bf16 = jnp.bfloat16


def shift(x, axes, sizes, offs):
    perm = []
    for source in np.ndindex(*sizes):
        dest = tuple((a + o) % s for a, o, s in zip(source, offs, sizes))
        perm.append(
            (int(np.ravel_multi_index(source, sizes)), int(np.ravel_multi_index(dest, sizes)))
        )
    return lax.ppermute(x, axes, perm)


def shift_y(x, k):
    return shift(x, ("y",), (4,), (k % 4,))


def swap_zh(x):
    return shift(x, ("zh",), (2,), (1,))


def swap_core(x):
    return shift(x, ("core",), (2,), (1,))


INVERSE = np.power(np.float64(ROPE_BASE), -np.arange(HEAD // 2) * (2.0 / HEAD)).astype(np.float32)


def half_sign(shape, axis):
    return jnp.where(lax.broadcasted_iota(jnp.int32, shape, axis) < HEAD // 2, -1.0, 1.0).astype(f32)


def block_kernel(key, value, positions, inverse, cos, sin, block):
    sign = half_sign((TILE, HEAD), 1)
    for t in range(2):
        tok = pl.ds(t * TILE, TILE)
        place = jnp.broadcast_to(positions[t].astype(f32), (TILE, TILE)).T
        angles = place * inverse[...]
        c, s = jnp.cos(angles), jnp.sin(angles)
        cos[tok, :] = c
        sin[tok, :] = s
        x = key[tok, :].astype(f32)
        block[tok, :HEAD] = (x * c + pltpu.roll(x, HEAD // 2, 1) * (s * sign)).astype(bf16)
        block[tok, HEAD:] = value[tok, :]


def prep_kernel(joined, cos, sin, q_rows, q_cols, g_rows, g_cols, delta):
    sign = half_sign((TILE, HEAD), 1)
    for t in range(2):
        tok = pl.ds(t * TILE, TILE)
        c, s = cos[tok, :], sin[tok, :] * sign
        for h in range(GROUPS):
            feat = pl.ds(h * HEAD, HEAD)
            lane = pl.ds(h * TILE, TILE)
            x = joined[tok, feat].astype(f32)
            rot = (x * c + pltpu.roll(x, HEAD // 2, 1) * s).astype(bf16)
            q_rows[t, lane, :] = rot
            q_cols[t, :, lane] = rot.T
            g = joined[tok, pl.ds(ROWS + h * HEAD, HEAD)]
            g_rows[t, lane, :] = g
            g_cols[t, :, lane] = g.T
            prod = g.astype(f32) * joined[tok, pl.ds(2 * ROWS + h * HEAD, HEAD)].astype(f32)
            delta[t, :, lane] = jnp.sum(prod.T, axis=0, keepdims=True)


EARLY = 5


def attention_kernel(
    mask, info, seg, lse, delta, cos, sin, q_rows, q_cols, g_rows, g_cols,
    early_mine, early_other, late_mine, late_other,
    d_early_mine, d_early_other, d_late_mine, d_late_other, qg, acc, dq, lse_rows,
):
    dq[...] = jnp.zeros_like(dq)
    for t in range(2):
        for h in range(GROUPS):
            lse_rows[t, :, pl.ds(h * TILE, TILE)] = lse[h : h + 1, t * TILE : (t + 1) * TILE]
    me = info[0]
    q_tile = 2 * me

    def pair(t, keys, vals, allowed):
        keys_t = keys.T
        scores = jnp.dot(keys, q_cols[t], preferred_element_type=f32)
        probs = jnp.exp(scores * SCALE - lse_rows[t])
        if allowed is not None:
            probs = jnp.where(allowed, probs, 0.0)
        dprobs = jnp.dot(vals, g_cols[t], preferred_element_type=f32)
        dscore = (probs * (dprobs - delta[t])).astype(bf16)
        probs = probs.astype(bf16)
        dq[t] += jnp.dot(keys_t, dscore, preferred_element_type=f32)
        acc[:, :HEAD] += jnp.dot(dscore, q_rows[t], preferred_element_type=f32)
        acc[:, HEAD:] += jnp.dot(probs, g_rows[t], preferred_element_type=f32)

    def tiles_of(kv, dkv, away, first_slot, slots):
        def step(j, carry):
            slot = lax.shift_right_logical(j, 1) + first_slot
            back_y = (lax.shift_right_logical(me, 2) - slot) & 3
            back_zh = (me ^ (lax.shift_right_logical(slot, 1) & 2)) & 2
            tile = 2 * (4 * back_y + back_zh + ((me ^ away) & 1)) + (j & 1)
            need0 = mask[q_tile, tile] > 0
            need1 = mask[q_tile + 1, tile] > 0
            here = pl.ds(pl.multiple_of(j * TILE, TILE), TILE)

            @pl.when(need0 | need1)
            def _():
                acc[...] = jnp.zeros_like(acc)
                keys, vals = kv[here, :HEAD], kv[here, HEAD:]
                for t, need in ((0, need0), (1, need1)):
                    diagonal = need & (tile == q_tile + t)

                    @pl.when(need & jnp.logical_not(diagonal))
                    def _():
                        pair(t, keys, vals, None)

                    if away == 0 and first_slot == 0:

                        @pl.when(diagonal)
                        def _():
                            row = jnp.broadcast_to(seg[tile], (TILE, TILE)).astype(f32)
                            causal = lax.broadcasted_iota(jnp.int32, (TILE, TILE), 0) <= (
                                lax.broadcasted_iota(jnp.int32, (TILE, TILE), 1)
                            )
                            one = jnp.where((row.T == row) & causal, 1.0, 0.0)
                            pair(t, keys, vals, jnp.concatenate([one] * GROUPS, 1) > 0.5)

                dkv[here, :] = acc[...].astype(bf16)

            @pl.when(jnp.logical_not(need0 | need1))
            def _():
                dkv[here, :] = jnp.zeros((TILE, 2 * HEAD), bf16)

            return carry

        lax.fori_loop(0, 2 * slots, step, 0)

    tiles_of(early_mine, d_early_mine, 0, 0, EARLY)
    tiles_of(early_other, d_early_other, 1, 0, EARLY)
    tiles_of(late_mine, d_late_mine, 0, EARLY, 8 - EARLY)
    tiles_of(late_other, d_late_other, 1, EARLY, 8 - EARLY)
    for t in range(2):
        tok = pl.ds(t * TILE, TILE)
        c, s = cos[tok, :].T, sin[tok, :].T
        for h in range(GROUPS):
            g = dq[t, :, pl.ds(h * TILE, TILE)] * SCALE
            u = g * s
            half = HEAD // 2
            turned = jnp.concatenate([u[half:], -u[:half]], 0)
            qg[pl.ds(h * HEAD, HEAD), tok] = (g * c + turned).astype(bf16)


def vmem(n):
    return [pl.BlockSpec(memory_space=pltpu.VMEM)] * n


def prep(joined, cos, sin):
    s = jax.ShapeDtypeStruct
    return pl.pallas_call(
        prep_kernel,
        out_shape=(
            s((2, ROWS, HEAD), bf16),
            s((2, HEAD, ROWS), bf16),
            s((2, ROWS, HEAD), bf16),
            s((2, HEAD, ROWS), bf16),
            s((2, 1, ROWS), f32),
        ),
        in_specs=vmem(3),
        out_specs=tuple(vmem(5)),
        compiler_params=pltpu.CompilerParams(vmem_limit_bytes=12 << 20),
        cost_estimate=pl.CostEstimate(flops=1000000, bytes_accessed=10000, transcendentals=0),
        name="prep",
    )(joined, cos, sin)


def attention(mask, info, *operands):
    s = jax.ShapeDtypeStruct
    early, late = (s((n * TOK, 2 * HEAD), bf16) for n in (EARLY, 8 - EARLY))
    return pl.pallas_call(
        attention_kernel,
        out_shape=(early, early, late, late, s((ROWS, TOK), bf16)),
        in_specs=[pl.BlockSpec(memory_space=pltpu.SMEM)] * 2 + vmem(len(operands)),
        out_specs=tuple(vmem(5)),
        scratch_shapes=[
            pltpu.VMEM((TILE, 2 * HEAD), f32),
            pltpu.VMEM((2, HEAD, ROWS), f32),
            pltpu.VMEM((2, 1, ROWS), f32),
        ],
        compiler_params=pltpu.CompilerParams(vmem_limit_bytes=16 << 20),
        cost_estimate=pl.CostEstimate(
            flops=2000000000, bytes_accessed=8000000, transcendentals=1000000
        ),
        name="attention",
    )(mask, info, *operands)


def make_block(key, value, positions):
    s = jax.ShapeDtypeStruct
    inverse = jnp.asarray(np.concatenate([INVERSE, INVERSE])[None, :])
    return pl.pallas_call(
        block_kernel,
        out_shape=(s((TOK, HEAD), f32), s((TOK, HEAD), f32), s((TOK, 2 * HEAD), bf16)),
        in_specs=vmem(4),
        out_specs=tuple(vmem(3)),
        cost_estimate=pl.CostEstimate(flops=5000000, bytes_accessed=700000, transcendentals=60000),
        name="block",
    )(key, value, positions.reshape(2, 1, TILE), inverse)


WIDTH = 5120
STEP_ROWS = 640


def project_kernel(
    own, across, near1, near2, near3, cos, sin, qg, wq, wk, wv, out, grads
):
    total = own[...].astype(f32) + across[...].astype(f32)
    for near in (near1, near2, near3):
        total += near[...].astype(f32)
    sign = half_sign((TOK, HEAD), 1)
    g = total[:, :HEAD] * SCALE
    key_grad = g * cos[...] - pltpu.roll(g * sin[...], HEAD // 2, 1) * sign
    grads[:ROWS, :] = qg[...]
    grads[ROWS : ROWS + HEAD, :] = key_grad.T.astype(bf16)
    grads[ROWS + HEAD :, :] = total[:, HEAD:].T.astype(bf16)

    def step(i, carry):
        rows = pl.ds(pl.multiple_of(i * STEP_ROWS, STEP_ROWS), STEP_ROWS)
        weights = jnp.concatenate([wq[rows, :], wk[rows, :], wv[rows, :]], 1)
        result = jnp.dot(weights, grads[...], preferred_element_type=f32)
        out[rows, :] = result.astype(bf16)
        return carry

    lax.fori_loop(0, WIDTH // STEP_ROWS, step, 0)


def project(own, across, near, cos, sin, qg, wq, wk, wv):
    return pl.pallas_call(
        project_kernel,
        out_shape=jax.ShapeDtypeStruct((WIDTH, TOK), bf16),
        in_specs=vmem(11),
        out_specs=vmem(1)[0],
        scratch_shapes=[pltpu.VMEM((ROWS + 2 * HEAD, TOK), bf16)],
        compiler_params=pltpu.CompilerParams(vmem_limit_bytes=16 << 20),
        cost_estimate=pl.CostEstimate(
            flops=2350000000, bytes_accessed=12000000, transcendentals=0
        ),
        name="project",
    )(own, across, *near, cos, sin, qg, wq, wk, wv)


def last_kernel(parts, out):
    def step(i, carry):
        rows = pl.ds(pl.multiple_of(i * TILE, TILE), TILE)
        total = parts[0, rows, :].astype(f32)
        for k in range(1, 8):
            total += parts[k, rows, :].astype(f32)
        out[rows, :] = total.astype(bf16)
        return carry

    lax.fori_loop(0, 5, step, 0)


def last_sum(parts):
    return pl.pallas_call(
        last_kernel,
        out_shape=jax.ShapeDtypeStruct((640, TOK), bf16),
        in_specs=vmem(1),
        out_specs=vmem(1)[0],
        compiler_params=pltpu.CompilerParams(vmem_limit_bytes=16 << 20),
        cost_estimate=pl.CostEstimate(flops=1300000, bytes_accessed=3000000, transcendentals=0),
        name="last_sum",
    )(parts)


def local(
    query, key, value, att, grad, lse, block_mask, positions, segments, w_query, key_weight,
    value_weight,
):
    me = lax.axis_index(CTX)
    cos, sin, block = make_block(key, value, positions)

    across = swap_zh(block)
    joined = jnp.concatenate([query, grad, att], 1)
    joined, again = lax.optimization_barrier((joined, block))
    near = [shift_y(again, k) for k in (1, 2, 3)]
    across, joined = lax.optimization_barrier((across, joined))
    far = [shift_y(across, k) for k in (1, 2, 3)]
    q_rows, q_cols, g_rows, g_cols, delta = prep(joined, cos, sin)
    early = jnp.concatenate([block] + near + [across], 0)
    late = jnp.concatenate(far, 0)

    early_mine, early_other, late_mine, late_other, query_grad = attention(
        block_mask, me.reshape(1), segments.reshape(TILES, 1, TILE), lse, delta, cos, sin, q_rows,
        q_cols, g_rows, g_cols, early, swap_core(early), late, swap_core(late),
    )

    late = late_mine.astype(f32) + swap_core(late_other).astype(f32)
    early = early_mine.astype(f32) + swap_core(early_other).astype(f32)
    own, across = early[:TOK], early[4 * TOK :]
    parts = [early[k * TOK : (k + 1) * TOK].astype(bf16) for k in (1, 2, 3)]
    parts += [late[k * TOK : (k + 1) * TOK].astype(bf16) for k in range(3)]
    own, across, parts = lax.optimization_barrier((own, across, parts))
    far = [shift_y(parts[2 + k], -k) for k in (1, 2, 3)]
    near = [shift_y(parts[k - 1], -k) for k in (1, 2, 3)]
    across = across + sum(p.astype(f32) for p in far)
    across = swap_zh(lax.optimization_barrier(across.astype(bf16)))
    send = project(own, across, near, cos, sin, query_grad, w_query, key_weight, value_weight)
    return last_sum(lax.all_to_all(send.reshape(8, 640, TOK), TP, 0, 0))


def solution(mesh):
    fine = Mesh(mesh.devices.reshape(4, 2, 2, 4, 2), ("y", "zh", "core", "x", "zl"))
    in_specs = (
        P(CTX, TP),
        P(CTX, TP),
        P(CTX, TP),
        P(CTX, TP),
        P(CTX, TP),
        P(TP, CTX),
        P(),
        P(CTX),
        P(),
        P(None, TP),
        P(None, TP),
        P(None, TP),
    )
    return jax.shard_map(
        local, mesh=fine, in_specs=in_specs, out_specs=P(TP, CTX), check_vma=False
    )
```

```python
import numpy as np
import jax
import jax.numpy as jnp
from jax import lax
from jax.experimental import pallas as pl
from jax.experimental.pallas import tpu as pltpu
from jax.sharding import Mesh, PartitionSpec as P

HEAD = 128
TILE = 128
GROUPS = 5
TOK = 256
TILES = 32
ROWS = GROUPS * TILE
SCALE = HEAD**-0.5
ROPE_BASE = 1000000.0
LOG2E = 1.4426950408889634
CTX = ("y", "zh", "core")
TP = ("x", "zl")

f32 = jnp.float32
bf16 = jnp.bfloat16


def shift(x, axes, sizes, offs):
    perm = []
    for source in np.ndindex(*sizes):
        dest = tuple((a + o) % s for a, o, s in zip(source, offs, sizes))
        perm.append(
            (int(np.ravel_multi_index(source, sizes)), int(np.ravel_multi_index(dest, sizes)))
        )
    return lax.ppermute(x, axes, perm)


def shift_y(x, k):
    return shift(x, ("y",), (4,), (k % 4,))


def swap_zh(x):
    return shift(x, ("zh",), (2,), (1,))


def swap_core(x):
    return shift(x, ("core",), (2,), (1,))


INVERSE = np.power(np.float64(ROPE_BASE), -np.arange(HEAD // 2) * (2.0 / HEAD)).astype(np.float32)


def half_sign(shape, axis):
    return jnp.where(lax.broadcasted_iota(jnp.int32, shape, axis) < HEAD // 2, -1.0, 1.0).astype(f32)


def block_kernel(key, value, positions, inverse, cos, sin, block):
    sign = half_sign((TILE, HEAD), 1)
    for t in range(2):
        tok = pl.ds(t * TILE, TILE)
        place = jnp.broadcast_to(positions[t].astype(f32), (TILE, TILE)).T
        angles = place * inverse[...]
        c, s = jnp.cos(angles), jnp.sin(angles)
        cos[tok, :] = c
        sin[tok, :] = s
        x = key[tok, :].astype(f32)
        block[tok, :HEAD] = (x * c + pltpu.roll(x, HEAD // 2, 1) * (s * sign)).astype(bf16)
        block[tok, HEAD:] = value[tok, :]


def prep_kernel(joined, cos, sin, q_rows, q_cols, g_rows, g_cols, delta):
    sign = half_sign((TILE, HEAD), 1)
    for t in range(2):
        tok = pl.ds(t * TILE, TILE)
        c, s = cos[tok, :], sin[tok, :] * sign
        for h in range(GROUPS):
            feat = pl.ds(h * HEAD, HEAD)
            lane = pl.ds(h * TILE, TILE)
            x = joined[tok, feat].astype(f32)
            rot = (x * c + pltpu.roll(x, HEAD // 2, 1) * s).astype(bf16)
            q_rows[t, lane, :] = rot
            q_cols[t, :, lane] = rot.T
            g = joined[tok, pl.ds(ROWS + h * HEAD, HEAD)]
            g_rows[t, lane, :] = g
            g_cols[t, :, lane] = g.T
            prod = g.astype(f32) * joined[tok, pl.ds(2 * ROWS + h * HEAD, HEAD)].astype(f32)
            delta[t, :, lane] = jnp.sum(prod.T, axis=0, keepdims=True)


EARLY = 5


def attention_kernel(
    mask, info, seg, lse, delta, cos, sin, q_rows, q_cols, g_rows, g_cols,
    early_mine, early_other, late_mine, late_other,
    d_early_mine, d_early_other, d_late_mine, d_late_other, qg,
    kv, dkv, dq, lse_rows, lists, counts, flags,
):
    dq[...] = jnp.zeros_like(dq)
    for t in range(2):
        for h in range(GROUPS):
            row = lse[h : h + 1, t * TILE : (t + 1) * TILE]
            lse_rows[t, :, pl.ds(h * TILE, TILE)] = row * LOG2E
    me = info[0]
    q_tile = 2 * me
    groups = (
        (early_mine, d_early_mine, 0, 0, EARLY),
        (early_other, d_early_other, 1, 0, EARLY),
        (late_mine, d_late_mine, 0, EARLY, 8 - EARLY),
        (late_other, d_late_other, 1, EARLY, 8 - EARLY),
    )
    starts = (0, 2 * EARLY, 4 * EARLY, 4 * EARLY + 2 * (8 - EARLY))

    def needs(j, away, first_slot):
        slot = lax.shift_right_logical(j, 1) + first_slot
        back_y = (lax.shift_right_logical(me, 2) - slot) & 3
        back_zh = (me ^ (lax.shift_right_logical(slot, 1) & 2)) & 2
        tile = 2 * (4 * back_y + back_zh + ((me ^ away) & 1)) + (j & 1)
        return mask[q_tile, tile] > 0, mask[q_tile + 1, tile] > 0

    for t in range(2):
        lists[t, 0] = t
        counts[t] = 1
    kv[pl.ds(TILES * TILE, TILE), :] = jnp.zeros((TILE, 2 * HEAD), bf16)
    dkv[pl.ds(TILES * TILE, TILE), :] = jnp.zeros((TILE, 2 * HEAD), f32)
    for (source, dest, away, first_slot, slots), start in zip(groups, starts):

        def collect(j, carry):
            needed = needs(j, away, first_slot)
            flags[start + j] = jnp.where(needed[0] | needed[1], 1, 0)
            here = pl.ds(pl.multiple_of(j * TILE, TILE), TILE)
            there = pl.ds(pl.multiple_of((start + j) * TILE, TILE), TILE)

            @pl.when(needed[0] | needed[1])
            def _():
                kv[there, :] = source[here, :]
                dkv[there, :] = jnp.zeros((TILE, 2 * HEAD), f32)

            @pl.when(jnp.logical_not(needed[0] | needed[1]))
            def _():
                dest[here, :] = jnp.zeros((TILE, 2 * HEAD), bf16)

            for t in range(2):
                add = needed[t]
                if start == 0:
                    add = add & (j != t)

                @pl.when(add)
                def _():
                    count = counts[t]
                    lists[t, count] = start + j
                    counts[t] = count + 1

            return carry

        lax.fori_loop(0, 2 * slots, collect, 0)

    def two_tiles(t, first, second, allowed):
        ones = pl.ds(pl.multiple_of(first * TILE, TILE), TILE)
        twos = pl.ds(pl.multiple_of(second * TILE, TILE), TILE)
        keys = jnp.concatenate([kv[ones, :HEAD], kv[twos, :HEAD]], 0)
        vals = jnp.concatenate([kv[ones, HEAD:], kv[twos, HEAD:]], 0)
        scores = jnp.dot(keys, q_cols[t], preferred_element_type=f32)
        probs = jnp.exp2(scores * (SCALE * LOG2E) - lse_rows[t])
        if allowed is not None:
            probs = jnp.concatenate([jnp.where(allowed, probs[:TILE], 0.0), probs[TILE:]], 0)
        dprobs = jnp.dot(vals, g_cols[t], preferred_element_type=f32)
        dscore = (probs * (dprobs - delta[t])).astype(bf16)
        probs = probs.astype(bf16)
        dkeys = jnp.dot(dscore, q_rows[t], preferred_element_type=f32)
        dvals = jnp.dot(probs, g_rows[t], preferred_element_type=f32)
        dqs = jnp.dot(keys.T, dscore, preferred_element_type=f32)
        return t, ones, twos, dkeys, dvals, dqs

    def add(t, ones, twos, dkeys, dvals, dqs):
        dq[t] += dqs
        dkv[ones, :HEAD] += dkeys[:TILE]
        dkv[ones, HEAD:] += dvals[:TILE]
        dkv[twos, :HEAD] += dkeys[TILE:]
        dkv[twos, HEAD:] += dvals[TILE:]

    most = jnp.maximum(counts[0], counts[1])

    def fill(i, carry):
        for t in range(2):

            @pl.when(i >= counts[t])
            def _():
                lists[t, i] = TILES

        return carry

    lax.fori_loop(jnp.minimum(counts[0], counts[1]), most + 1, fill, 0)
    causal = lax.broadcasted_iota(jnp.int32, (TILE, TILE), 0) <= (
        lax.broadcasted_iota(jnp.int32, (TILE, TILE), 1)
    )
    terms = []
    for t in range(2):
        row = jnp.broadcast_to(seg[q_tile + t], (TILE, TILE)).astype(f32)
        listed = jnp.where(mask[q_tile + t, q_tile + t] > 0, 1.0, 0.0)
        one = jnp.where((row.T == row) & causal, 1.0, 0.0) * listed
        terms.append(two_tiles(t, t, lists[t, 1], jnp.concatenate([one] * GROUPS, 1) > 0.5))
    for term in terms:
        add(*term)

    def rest(i, carry):
        terms = [two_tiles(t, lists[t, 2 * i], lists[t, 2 * i + 1], None) for t in range(2)]
        for term in terms:
            add(*term)
        return carry

    lax.fori_loop(1, lax.shift_right_logical(most + 1, 1), rest, 0)

    for (source, dest, away, first_slot, slots), start in zip(groups, starts):

        def give(j, carry):
            @pl.when(flags[start + j] > 0)
            def _():
                here = pl.ds(pl.multiple_of(j * TILE, TILE), TILE)
                there = pl.ds(pl.multiple_of((start + j) * TILE, TILE), TILE)
                dest[here, :] = dkv[there, :].astype(bf16)

            return carry

        lax.fori_loop(0, 2 * slots, give, 0)

    for t in range(2):
        tok = pl.ds(t * TILE, TILE)
        c, s = cos[tok, :].T, sin[tok, :].T
        for h in range(GROUPS):
            g = dq[t, :, pl.ds(h * TILE, TILE)] * SCALE
            u = g * s
            half = HEAD // 2
            turned = jnp.concatenate([u[half:], -u[:half]], 0)
            qg[pl.ds(h * HEAD, HEAD), tok] = (g * c + turned).astype(bf16)


def vmem(n):
    return [pl.BlockSpec(memory_space=pltpu.VMEM)] * n


def prep(joined, cos, sin):
    s = jax.ShapeDtypeStruct
    return pl.pallas_call(
        prep_kernel,
        out_shape=(
            s((2, ROWS, HEAD), bf16),
            s((2, HEAD, ROWS), bf16),
            s((2, ROWS, HEAD), bf16),
            s((2, HEAD, ROWS), bf16),
            s((2, 1, ROWS), f32),
        ),
        in_specs=vmem(3),
        out_specs=tuple(vmem(5)),
        compiler_params=pltpu.CompilerParams(vmem_limit_bytes=12 << 20),
        cost_estimate=pl.CostEstimate(flops=1000000, bytes_accessed=10000, transcendentals=0),
        name="prep",
    )(joined, cos, sin)


def attention(mask, info, *operands):
    s = jax.ShapeDtypeStruct
    early, late = (s((n * TOK, 2 * HEAD), bf16) for n in (EARLY, 8 - EARLY))
    return pl.pallas_call(
        attention_kernel,
        out_shape=(early, early, late, late, s((ROWS, TOK), bf16)),
        in_specs=[pl.BlockSpec(memory_space=pltpu.SMEM)] * 2 + vmem(len(operands)),
        out_specs=tuple(vmem(5)),
        scratch_shapes=[
            pltpu.VMEM(((TILES + 1) * TILE, 2 * HEAD), bf16),
            pltpu.VMEM(((TILES + 1) * TILE, 2 * HEAD), f32),
            pltpu.VMEM((2, HEAD, ROWS), f32),
            pltpu.VMEM((2, 1, ROWS), f32),
            pltpu.SMEM((2, TILES + 1), jnp.int32),
            pltpu.SMEM((2,), jnp.int32),
            pltpu.SMEM((TILES,), jnp.int32),
        ],
        compiler_params=pltpu.CompilerParams(vmem_limit_bytes=16 << 20),
        cost_estimate=pl.CostEstimate(
            flops=2000000000, bytes_accessed=8000000, transcendentals=1000000
        ),
        name="attention",
    )(mask, info, *operands)


def make_block(key, value, positions):
    s = jax.ShapeDtypeStruct
    inverse = jnp.asarray(np.concatenate([INVERSE, INVERSE])[None, :])
    return pl.pallas_call(
        block_kernel,
        out_shape=(s((TOK, HEAD), f32), s((TOK, HEAD), f32), s((TOK, 2 * HEAD), bf16)),
        in_specs=vmem(4),
        out_specs=tuple(vmem(3)),
        cost_estimate=pl.CostEstimate(flops=5000000, bytes_accessed=700000, transcendentals=60000),
        name="block",
    )(key, value, positions.reshape(2, 1, TILE), inverse)


WIDTH = 5120
STEP_ROWS = 640


def project_kernel(
    own, across, near1, near2, near3, cos, sin, qg, wq, wk, wv, out, grads
):
    total = own[...].astype(f32) + across[...].astype(f32)
    for near in (near1, near2, near3):
        total += near[...].astype(f32)
    sign = half_sign((TOK, HEAD), 1)
    g = total[:, :HEAD] * SCALE
    key_grad = g * cos[...] - pltpu.roll(g * sin[...], HEAD // 2, 1) * sign
    grads[:ROWS, :] = qg[...]
    grads[ROWS : ROWS + HEAD, :] = key_grad.T.astype(bf16)
    grads[ROWS + HEAD :, :] = total[:, HEAD:].T.astype(bf16)

    def step(i, carry):
        rows = pl.ds(pl.multiple_of(i * STEP_ROWS, STEP_ROWS), STEP_ROWS)
        weights = jnp.concatenate([wq[rows, :], wk[rows, :], wv[rows, :]], 1)
        result = jnp.dot(weights, grads[...], preferred_element_type=f32)
        out[rows, :] = result.astype(bf16)
        return carry

    lax.fori_loop(0, WIDTH // STEP_ROWS, step, 0)


def project(own, across, near, cos, sin, qg, wq, wk, wv):
    return pl.pallas_call(
        project_kernel,
        out_shape=jax.ShapeDtypeStruct((WIDTH, TOK), bf16),
        in_specs=vmem(11),
        out_specs=vmem(1)[0],
        scratch_shapes=[pltpu.VMEM((ROWS + 2 * HEAD, TOK), bf16)],
        compiler_params=pltpu.CompilerParams(vmem_limit_bytes=16 << 20),
        cost_estimate=pl.CostEstimate(
            flops=2350000000, bytes_accessed=12000000, transcendentals=0
        ),
        name="project",
    )(own, across, *near, cos, sin, qg, wq, wk, wv)


def last_kernel(parts, out):
    def step(i, carry):
        rows = pl.ds(pl.multiple_of(i * TILE, TILE), TILE)
        total = parts[0, rows, :].astype(f32)
        for k in range(1, 8):
            total += parts[k, rows, :].astype(f32)
        out[rows, :] = total.astype(bf16)
        return carry

    lax.fori_loop(0, 5, step, 0)


def last_sum(parts):
    return pl.pallas_call(
        last_kernel,
        out_shape=jax.ShapeDtypeStruct((640, TOK), bf16),
        in_specs=vmem(1),
        out_specs=vmem(1)[0],
        compiler_params=pltpu.CompilerParams(vmem_limit_bytes=16 << 20),
        cost_estimate=pl.CostEstimate(flops=1300000, bytes_accessed=3000000, transcendentals=0),
        name="last_sum",
    )(parts)


def local(
    query, key, value, att, grad, lse, block_mask, positions, segments, w_query, key_weight,
    value_weight,
):
    me = lax.axis_index(CTX)
    cos, sin, block = make_block(key, value, positions)

    across = swap_zh(block)
    joined = jnp.concatenate([query, grad, att], 1)
    joined, again = lax.optimization_barrier((joined, block))
    near = [shift_y(again, k) for k in (1, 2, 3)]
    across, joined = lax.optimization_barrier((across, joined))
    far = [shift_y(across, k) for k in (1, 2, 3)]
    q_rows, q_cols, g_rows, g_cols, delta = prep(joined, cos, sin)
    early = jnp.concatenate([block] + near + [across], 0)
    late = jnp.concatenate(far, 0)

    early_mine, early_other, late_mine, late_other, query_grad = attention(
        block_mask, me.reshape(1), segments.reshape(TILES, 1, TILE), lse, delta, cos, sin, q_rows,
        q_cols, g_rows, g_cols, early, swap_core(early), late, swap_core(late),
    )

    late = late_mine.astype(f32) + swap_core(late_other).astype(f32)
    early = early_mine.astype(f32) + swap_core(early_other).astype(f32)
    own, across = early[:TOK], early[4 * TOK :]
    parts = [early[k * TOK : (k + 1) * TOK].astype(bf16) for k in (1, 2, 3)]
    parts += [late[k * TOK : (k + 1) * TOK].astype(bf16) for k in range(3)]
    own, across, parts = lax.optimization_barrier((own, across, parts))
    far = [shift_y(parts[2 + k], -k) for k in (1, 2, 3)]
    near = [shift_y(parts[k - 1], -k) for k in (1, 2, 3)]
    across = across + sum(p.astype(f32) for p in far)
    across = swap_zh(lax.optimization_barrier(across.astype(bf16)))
    send = project(own, across, near, cos, sin, query_grad, w_query, key_weight, value_weight)
    return last_sum(lax.all_to_all(send.reshape(8, 640, TOK), TP, 0, 0))


def solution(mesh):
    fine = Mesh(mesh.devices.reshape(4, 2, 2, 4, 2), ("y", "zh", "core", "x", "zl"))
    in_specs = (
        P(CTX, TP),
        P(CTX, TP),
        P(CTX, TP),
        P(CTX, TP),
        P(CTX, TP),
        P(TP, CTX),
        P(),
        P(CTX),
        P(),
        P(None, TP),
        P(None, TP),
        P(None, TP),
    )
    return jax.shard_map(
        local, mesh=fine, in_specs=in_specs, out_specs=P(TP, CTX), check_vma=False
    )
```

```python
import numpy as np
import jax
import jax.numpy as jnp
from jax import lax
from jax.experimental import pallas as pl
from jax.experimental.pallas import tpu as pltpu
from jax.sharding import Mesh, PartitionSpec as P

HEAD = 128
TILE = 128
GROUPS = 5
TOK = 256
TILES = 32
ROWS = GROUPS * TILE
SCALE = HEAD**-0.5
ROPE_BASE = 1000000.0
LOG2E = 1.4426950408889634
CTX = ("y", "zh", "core")
TP = ("x", "zl")

f32 = jnp.float32
bf16 = jnp.bfloat16


def shift(x, axes, sizes, offs):
    perm = []
    for source in np.ndindex(*sizes):
        dest = tuple((a + o) % s for a, o, s in zip(source, offs, sizes))
        perm.append(
            (int(np.ravel_multi_index(source, sizes)), int(np.ravel_multi_index(dest, sizes)))
        )
    return lax.ppermute(x, axes, perm)


def shift_y(x, k):
    return shift(x, ("y",), (4,), (k % 4,))


def swap_zh(x):
    return shift(x, ("zh",), (2,), (1,))


def swap_core(x):
    return shift(x, ("core",), (2,), (1,))


INVERSE = np.power(np.float64(ROPE_BASE), -np.arange(HEAD // 2) * (2.0 / HEAD)).astype(np.float32)


def half_sign(shape, axis):
    return jnp.where(lax.broadcasted_iota(jnp.int32, shape, axis) < HEAD // 2, -1.0, 1.0).astype(f32)


def block_kernel(key, value, positions, inverse, cos, sin, block):
    sign = half_sign((TILE, HEAD), 1)
    for t in range(2):
        tok = pl.ds(t * TILE, TILE)
        place = jnp.broadcast_to(positions[t].astype(f32), (TILE, TILE)).T
        angles = place * inverse[...]
        c, s = jnp.cos(angles), jnp.sin(angles)
        cos[tok, :] = c
        sin[tok, :] = s
        x = key[tok, :].astype(f32)
        block[tok, :HEAD] = (x * c + pltpu.roll(x, HEAD // 2, 1) * (s * sign)).astype(bf16)
        block[tok, HEAD:] = value[tok, :]


def prep_kernel(joined, cos, sin, q_rows, q_cols, g_rows, g_cols, delta):
    sign = half_sign((TILE, HEAD), 1)
    for t in range(2):
        tok = pl.ds(t * TILE, TILE)
        c, s = cos[tok, :], sin[tok, :] * sign
        for h in range(GROUPS):
            feat = pl.ds(h * HEAD, HEAD)
            lane = pl.ds(h * TILE, TILE)
            x = joined[tok, feat].astype(f32)
            rot = (x * c + pltpu.roll(x, HEAD // 2, 1) * s).astype(bf16)
            q_rows[t, lane, :] = rot
            q_cols[t, :, lane] = rot.T
            g = joined[tok, pl.ds(ROWS + h * HEAD, HEAD)]
            g_rows[t, lane, :] = g
            g_cols[t, :, lane] = g.T
            prod = g.astype(f32) * joined[tok, pl.ds(2 * ROWS + h * HEAD, HEAD)].astype(f32)
            delta[t, :, lane] = jnp.sum(prod.T, axis=0, keepdims=True)


EARLY = 5


def attention_kernel(
    mask, info, seg, lse, delta, cos, sin, q_rows, q_cols, g_rows, g_cols,
    early_mine, early_other, late_mine, late_other,
    d_early_mine, d_early_other, d_late_mine, d_late_other, qg,
    kv, dkv, dq, lse_rows, lists, counts, flags,
):
    dq[...] = jnp.zeros_like(dq)
    for t in range(2):
        for h in range(GROUPS):
            row = lse[h : h + 1, t * TILE : (t + 1) * TILE]
            lse_rows[t, :, pl.ds(h * TILE, TILE)] = row * LOG2E
    me = info[0]
    q_tile = 2 * me
    groups = (
        (early_mine, d_early_mine, 0, 0, EARLY),
        (early_other, d_early_other, 1, 0, EARLY),
        (late_mine, d_late_mine, 0, EARLY, 8 - EARLY),
        (late_other, d_late_other, 1, EARLY, 8 - EARLY),
    )
    starts = (0, 2 * EARLY, 4 * EARLY, 4 * EARLY + 2 * (8 - EARLY))

    def needs(j, away, first_slot):
        slot = lax.shift_right_logical(j, 1) + first_slot
        back_y = (lax.shift_right_logical(me, 2) - slot) & 3
        back_zh = (me ^ (lax.shift_right_logical(slot, 1) & 2)) & 2
        tile = 2 * (4 * back_y + back_zh + ((me ^ away) & 1)) + (j & 1)
        return mask[q_tile, tile] > 0, mask[q_tile + 1, tile] > 0

    for t in range(2):
        lists[t, 0] = t
        counts[t] = 1
    kv[pl.ds(TILES * TILE, TILE), :] = jnp.zeros((TILE, 2 * HEAD), bf16)
    dkv[pl.ds(TILES * TILE, TILE), :] = jnp.zeros((TILE, 2 * HEAD), f32)
    for (source, dest, away, first_slot, slots), start in zip(groups, starts):

        def collect(j, carry):
            needed = needs(j, away, first_slot)
            flags[start + j] = jnp.where(needed[0] | needed[1], 1, 0)
            here = pl.ds(pl.multiple_of(j * TILE, TILE), TILE)
            there = pl.ds(pl.multiple_of((start + j) * TILE, TILE), TILE)

            @pl.when(needed[0] | needed[1])
            def _():
                kv[there, :] = source[here, :]
                dkv[there, :] = jnp.zeros((TILE, 2 * HEAD), f32)

            @pl.when(jnp.logical_not(needed[0] | needed[1]))
            def _():
                dest[here, :] = jnp.zeros((TILE, 2 * HEAD), bf16)

            for t in range(2):
                add = needed[t]
                if start == 0:
                    add = add & (j != t)

                @pl.when(add)
                def _():
                    count = counts[t]
                    lists[t, count] = start + j
                    counts[t] = count + 1

            return carry

        lax.fori_loop(0, 2 * slots, collect, 0)

    def two_tiles(t, first, second, allowed):
        ones = pl.ds(pl.multiple_of(first * TILE, TILE), TILE)
        twos = pl.ds(pl.multiple_of(second * TILE, TILE), TILE)
        keys = jnp.concatenate([kv[ones, :HEAD], kv[twos, :HEAD]], 0)
        vals = jnp.concatenate([kv[ones, HEAD:], kv[twos, HEAD:]], 0)
        scores = jnp.dot(keys, q_cols[t], preferred_element_type=f32)
        probs = jnp.exp2(scores * (SCALE * LOG2E) - lse_rows[t])
        if allowed is not None:
            probs = jnp.concatenate([jnp.where(allowed, probs[:TILE], 0.0), probs[TILE:]], 0)
        dprobs = jnp.dot(vals, g_cols[t], preferred_element_type=f32)
        dscore = (probs * (dprobs - delta[t])).astype(bf16)
        probs = probs.astype(bf16)
        dkeys = jnp.dot(dscore, q_rows[t], preferred_element_type=f32)
        dvals = jnp.dot(probs, g_rows[t], preferred_element_type=f32)
        dqs = jnp.dot(keys.T, dscore, preferred_element_type=f32)
        return t, ones, twos, dkeys, dvals, dqs

    def add(t, ones, twos, dkeys, dvals, dqs):
        dq[t] += dqs
        dkv[ones, :HEAD] += dkeys[:TILE]
        dkv[ones, HEAD:] += dvals[:TILE]
        dkv[twos, :HEAD] += dkeys[TILE:]
        dkv[twos, HEAD:] += dvals[TILE:]

    most = jnp.maximum(counts[0], counts[1])

    def fill(i, carry):
        for t in range(2):

            @pl.when(i >= counts[t])
            def _():
                lists[t, i] = TILES

        return carry

    lax.fori_loop(jnp.minimum(counts[0], counts[1]), most + 1, fill, 0)
    causal = lax.broadcasted_iota(jnp.int32, (TILE, TILE), 0) <= (
        lax.broadcasted_iota(jnp.int32, (TILE, TILE), 1)
    )
    terms = []
    for t in range(2):
        row = jnp.broadcast_to(seg[q_tile + t], (TILE, TILE)).astype(f32)
        listed = jnp.where(mask[q_tile + t, q_tile + t] > 0, 1.0, 0.0)
        one = jnp.where((row.T == row) & causal, 1.0, 0.0) * listed
        terms.append(two_tiles(t, t, lists[t, 1], jnp.concatenate([one] * GROUPS, 1) > 0.5))
    for term in terms:
        add(*term)

    def rest(i, carry):
        terms = [two_tiles(t, lists[t, 2 * i], lists[t, 2 * i + 1], None) for t in range(2)]
        for term in terms:
            add(*term)
        return carry

    lax.fori_loop(1, lax.shift_right_logical(most + 1, 1), rest, 0)

    for (source, dest, away, first_slot, slots), start in zip(groups, starts):

        def give(j, carry):
            @pl.when(flags[start + j] > 0)
            def _():
                here = pl.ds(pl.multiple_of(j * TILE, TILE), TILE)
                there = pl.ds(pl.multiple_of((start + j) * TILE, TILE), TILE)
                dest[here, :] = dkv[there, :].astype(bf16)

            return carry

        lax.fori_loop(0, 2 * slots, give, 0)

    for t in range(2):
        tok = pl.ds(t * TILE, TILE)
        c, s = cos[tok, :].T, sin[tok, :].T
        for h in range(GROUPS):
            g = dq[t, :, pl.ds(h * TILE, TILE)] * SCALE
            u = g * s
            half = HEAD // 2
            turned = jnp.concatenate([u[half:], -u[:half]], 0)
            qg[pl.ds(h * HEAD, HEAD), tok] = (g * c + turned).astype(bf16)


def vmem(n):
    return [pl.BlockSpec(memory_space=pltpu.VMEM)] * n


def prep(joined, cos, sin):
    s = jax.ShapeDtypeStruct
    return pl.pallas_call(
        prep_kernel,
        out_shape=(
            s((2, ROWS, HEAD), bf16),
            s((2, HEAD, ROWS), bf16),
            s((2, ROWS, HEAD), bf16),
            s((2, HEAD, ROWS), bf16),
            s((2, 1, ROWS), f32),
        ),
        in_specs=vmem(3),
        out_specs=tuple(vmem(5)),
        compiler_params=pltpu.CompilerParams(vmem_limit_bytes=12 << 20),
        cost_estimate=pl.CostEstimate(flops=1000000, bytes_accessed=10000, transcendentals=0),
        name="prep",
    )(joined, cos, sin)


def attention(mask, info, *operands):
    s = jax.ShapeDtypeStruct
    early, late = (s((n * TOK, 2 * HEAD), bf16) for n in (EARLY, 8 - EARLY))
    return pl.pallas_call(
        attention_kernel,
        out_shape=(early, early, late, late, s((ROWS, TOK), bf16)),
        in_specs=[pl.BlockSpec(memory_space=pltpu.SMEM)] * 2 + vmem(len(operands)),
        out_specs=tuple(vmem(5)),
        scratch_shapes=[
            pltpu.VMEM(((TILES + 1) * TILE, 2 * HEAD), bf16),
            pltpu.VMEM(((TILES + 1) * TILE, 2 * HEAD), f32),
            pltpu.VMEM((2, HEAD, ROWS), f32),
            pltpu.VMEM((2, 1, ROWS), f32),
            pltpu.SMEM((2, TILES + 1), jnp.int32),
            pltpu.SMEM((2,), jnp.int32),
            pltpu.SMEM((TILES,), jnp.int32),
        ],
        compiler_params=pltpu.CompilerParams(vmem_limit_bytes=16 << 20),
        cost_estimate=pl.CostEstimate(
            flops=2000000000, bytes_accessed=8000000, transcendentals=1000000
        ),
        name="attention",
    )(mask, info, *operands)


def make_block(key, value, positions):
    s = jax.ShapeDtypeStruct
    inverse = jnp.asarray(np.concatenate([INVERSE, INVERSE])[None, :])
    return pl.pallas_call(
        block_kernel,
        out_shape=(s((TOK, HEAD), f32), s((TOK, HEAD), f32), s((TOK, 2 * HEAD), bf16)),
        in_specs=vmem(4),
        out_specs=tuple(vmem(3)),
        cost_estimate=pl.CostEstimate(flops=5000000, bytes_accessed=700000, transcendentals=60000),
        name="block",
    )(key, value, positions.reshape(2, 1, TILE), inverse)


STEP_ROWS = 640


ORDERS = (
    ((0, 1), (1, 1), (2, 1), (3, 1), (0, 0), (1, 0), (2, 0), (3, 0)),
    ((1, 0), (1, 1), (3, 0), (3, 1), (0, 0), (0, 1), (2, 0), (2, 1)),
)


def by_core(offsets):
    pairs = []
    for core, offset in enumerate(offsets):
        if offset is not None:
            for x in range(4):
                for zl in range(2):
                    to = (core * 4 + (x + offset[0]) % 4) * 2 + (zl + offset[1]) % 2
                    pairs.append(((core * 4 + x) * 2 + zl, to))
    return pairs


def send(x, *offsets):
    return lax.ppermute(x, ("core", "x", "zl"), by_core(offsets))


def make_blocks(tp, core, first, count, grads, wq, wk, wv, put):
    x, zl = lax.shift_right_logical(tp[0], 1), tp[0] & 1
    for i in range(count):
        (x0, z0), (x1, z1) = ORDERS[0][first + i], ORDERS[1][first + i]
        to_x = (x + jnp.where(core[0] == 0, x0, x1)) & 3
        to_z = zl ^ jnp.where(core[0] == 0, z0, z1)
        rows = pl.ds(pl.multiple_of((2 * to_x + to_z) * STEP_ROWS, STEP_ROWS), STEP_ROWS)
        weights = jnp.concatenate([wq[rows, :], wk[rows, :], wv[rows, :]], 1)
        put(i, jnp.dot(weights, grads[...], preferred_element_type=f32))


def first_kernel(
    tp, core, own, across, near1, near2, near3, cos, sin, qg, wq, wk, wv, out1, out2, out3, grads
):
    total = own[...].astype(f32) + across[...].astype(f32)
    for near in (near1, near2, near3):
        total += near[...].astype(f32)
    sign = half_sign((TOK, HEAD), 1)
    g = total[:, :HEAD] * SCALE
    key_grad = g * cos[...] - pltpu.roll(g * sin[...], HEAD // 2, 1) * sign
    grads[:ROWS, :] = qg[...]
    grads[ROWS : ROWS + HEAD, :] = key_grad.T.astype(bf16)
    grads[ROWS + HEAD :, :] = total[:, HEAD:].T.astype(bf16)

    def put_in(out):
        def put(i, block):
            out[i] = block.astype(bf16)

        return put

    make_blocks(tp, core, 0, 2, grads, wq, wk, wv, put_in(out1))
    make_blocks(tp, core, 2, 2, grads, wq, wk, wv, put_in(out2))

    @pl.when(core[0] != 0)
    def _():
        make_blocks(tp, core, 6, 2, grads, wq, wk, wv, put_in(out3))


def kept_kernel(tp, core, grads, wq, wk, wv, kept):
    def put(i, block):
        kept[i] = block

    def put_more(i, block):
        kept[2 + i] = block

    make_blocks(tp, core, 4, 2, grads, wq, wk, wv, put)

    @pl.when(core[0] == 0)
    def _():
        make_blocks(tp, core, 6, 2, grads, wq, wk, wv, put_more)


def middle_kernel(core, kept, got1, got2, got3, base, out1, out2, out3):
    @pl.when(core[0] == 0)
    def _():
        base[...] = kept[0] + got1[0].astype(f32)
        out1[...] = (kept[1] + got1[1].astype(f32)).astype(bf16)
        out2[...] = (kept[2] + got2[0].astype(f32)).astype(bf16)
        out3[...] = (kept[3] + got2[1].astype(f32)).astype(bf16)

    @pl.when(core[0] != 0)
    def _():
        total = [
            kept[i] + got1[i].astype(f32) + got2[i].astype(f32) + got3[i].astype(f32)
            for i in range(2)
        ]
        base[...] = total[0]
        out1[...] = total[1].astype(bf16)
        out2[...] = jnp.zeros_like(out2)
        out3[...] = jnp.zeros_like(out3)


def last_kernel(core, base, got1, got2, got3, out):
    @pl.when(core[0] == 0)
    def _():
        total = base[...] + got1[...].astype(f32) + got2[...].astype(f32)
        out[...] = (total + got3[...].astype(f32)).astype(bf16)

    @pl.when(core[0] != 0)
    def _():
        out[...] = (base[...] + got1[...].astype(f32)).astype(bf16)


def whole_call(kernel, name, flops, outs, scalars, *operands):
    outs = tuple(jax.ShapeDtypeStruct(shape, dtype) for shape, dtype in outs)
    return pl.pallas_call(
        kernel,
        out_shape=outs,
        in_specs=[pl.BlockSpec(memory_space=pltpu.SMEM)] * len(scalars) + vmem(len(operands)),
        out_specs=tuple(vmem(len(outs))),
        compiler_params=pltpu.CompilerParams(vmem_limit_bytes=16 << 20),
        cost_estimate=pl.CostEstimate(flops=flops, bytes_accessed=10000, transcendentals=0),
        name=name,
    )(*scalars, *operands)


def project_and_sum(own, across, near, cos, sin, qg, wq, wk, wv):
    tp = lax.axis_index(TP).reshape(1)
    core = lax.axis_index("core").reshape(1)
    one, two, four = ((n, STEP_ROWS, TOK) for n in (1, 2, 4))
    one = one[1:]
    first, second, third, grads = whole_call(
        first_kernel,
        "first",
        1000000,
        [(two, bf16), (two, bf16), (two, bf16), ((ROWS + 2 * HEAD, TOK), bf16)],
        (tp, core),
        own, across, *near, cos, sin, qg, wq, wk, wv,
    )
    got1 = send(first, (0, 1), (1, 0))
    got2 = send(second, (0, 1), (3, 0))
    got3 = send(third, None, (2, 0))
    got1, grads = lax.optimization_barrier((got1, grads))
    (kept,) = whole_call(
        kept_kernel, "kept", 1000000, [(four, f32)], (tp, core), grads, wq, wk, wv
    )
    base, out1, out2, out3 = whole_call(
        middle_kernel,
        "middle",
        1000000,
        [(one, f32), (one, bf16), (one, bf16), (one, bf16)],
        (core,),
        kept, got1, got2, got3,
    )
    got1 = send(out1, (1, 0), (0, 1))
    got2 = send(out2, (2, 0), None)
    got3 = send(out3, (3, 0), None)
    return whole_call(last_kernel, "last", 1000000, [(one, bf16)], (core,), base, got1, got2, got3)[0]


def local(
    query, key, value, att, grad, lse, block_mask, positions, segments, w_query, key_weight,
    value_weight,
):
    me = lax.axis_index(CTX)
    cos, sin, block = make_block(key, value, positions)

    across = swap_zh(block)
    joined = jnp.concatenate([query, grad, att], 1)
    joined, again = lax.optimization_barrier((joined, block))
    near = [shift_y(again, k) for k in (1, 2, 3)]
    across, joined = lax.optimization_barrier((across, joined))
    far = [shift_y(across, k) for k in (1, 2, 3)]
    q_rows, q_cols, g_rows, g_cols, delta = prep(joined, cos, sin)
    early = jnp.concatenate([block] + near + [across], 0)
    late = jnp.concatenate(far, 0)

    early_mine, early_other, late_mine, late_other, query_grad = attention(
        block_mask, me.reshape(1), segments.reshape(TILES, 1, TILE), lse, delta, cos, sin, q_rows,
        q_cols, g_rows, g_cols, early, swap_core(early), late, swap_core(late),
    )

    late = late_mine.astype(f32) + swap_core(late_other).astype(f32)
    early = early_mine.astype(f32) + swap_core(early_other).astype(f32)
    own, across = early[:TOK], early[4 * TOK :]
    parts = [early[k * TOK : (k + 1) * TOK].astype(bf16) for k in (1, 2, 3)]
    parts += [late[k * TOK : (k + 1) * TOK].astype(bf16) for k in range(3)]
    own, across, parts = lax.optimization_barrier((own, across, parts))
    far = [shift_y(parts[2 + k], -k) for k in (1, 2, 3)]
    near = [shift_y(parts[k - 1], -k) for k in (1, 2, 3)]
    across = across + sum(p.astype(f32) for p in far)
    across = swap_zh(lax.optimization_barrier(across.astype(bf16)))
    return project_and_sum(
        own, across, near, cos, sin, query_grad, w_query, key_weight, value_weight
    )


def solution(mesh):
    fine = Mesh(mesh.devices.reshape(4, 2, 2, 4, 2), ("y", "zh", "core", "x", "zl"))
    in_specs = (
        P(CTX, TP),
        P(CTX, TP),
        P(CTX, TP),
        P(CTX, TP),
        P(CTX, TP),
        P(TP, CTX),
        P(),
        P(CTX),
        P(),
        P(None, TP),
        P(None, TP),
        P(None, TP),
    )
    return jax.shard_map(
        local, mesh=fine, in_specs=in_specs, out_specs=P(TP, CTX), check_vma=False
    )
```

```python
import numpy as np
import jax
import jax.numpy as jnp
from jax import lax
from jax.experimental import pallas as pl
from jax.experimental.pallas import tpu as pltpu
from jax.sharding import Mesh, PartitionSpec as P

HEAD = 128
TILE = 128
GROUPS = 5
TOK = 256
TILES = 32
ROWS = GROUPS * TILE
SCALE = HEAD**-0.5
ROPE_BASE = 1000000.0
LOG2E = 1.4426950408889634
CTX = ("y", "zh", "core")
TP = ("x", "zl")

f32 = jnp.float32
bf16 = jnp.bfloat16


def shift(x, axes, sizes, offs):
    perm = []
    for source in np.ndindex(*sizes):
        dest = tuple((a + o) % s for a, o, s in zip(source, offs, sizes))
        perm.append(
            (int(np.ravel_multi_index(source, sizes)), int(np.ravel_multi_index(dest, sizes)))
        )
    return lax.ppermute(x, axes, perm)


def shift_y(x, k):
    return shift(x, ("y",), (4,), (k % 4,))


def swap_zh(x):
    return shift(x, ("zh",), (2,), (1,))


def swap_core(x):
    return shift(x, ("core",), (2,), (1,))


INVERSE = np.power(np.float64(ROPE_BASE), -np.arange(HEAD // 2) * (2.0 / HEAD)).astype(np.float32)


def half_sign(shape, axis):
    return jnp.where(lax.broadcasted_iota(jnp.int32, shape, axis) < HEAD // 2, -1.0, 1.0).astype(f32)


def block_kernel(key, value, positions, inverse, cos, sin, block):
    sign = half_sign((TILE, HEAD), 1)
    for t in range(2):
        tok = pl.ds(t * TILE, TILE)
        place = jnp.broadcast_to(positions[t].astype(f32), (TILE, TILE)).T
        angles = place * inverse[...]
        c, s = jnp.cos(angles), jnp.sin(angles)
        cos[tok, :] = c
        sin[tok, :] = s
        x = key[tok, :].astype(f32)
        block[tok, :HEAD] = (x * c + pltpu.roll(x, HEAD // 2, 1) * (s * sign)).astype(bf16)
        block[tok, HEAD:] = value[tok, :]


def prep_kernel(joined, cos, sin, q_rows, q_cols, g_rows, g_cols, delta):
    sign = half_sign((TILE, HEAD), 1)
    for t in range(2):
        tok = pl.ds(t * TILE, TILE)
        c, s = cos[tok, :], sin[tok, :] * sign
        for h in range(GROUPS):
            feat = pl.ds(h * HEAD, HEAD)
            lane = pl.ds(h * TILE, TILE)
            x = joined[tok, feat].astype(f32)
            rot = (x * c + pltpu.roll(x, HEAD // 2, 1) * s).astype(bf16)
            q_rows[t, lane, :] = rot
            q_cols[t, :, lane] = rot.T
            g = joined[tok, pl.ds(ROWS + h * HEAD, HEAD)]
            g_rows[t, lane, :] = g
            g_cols[t, :, lane] = g.T
            prod = g.astype(f32) * joined[tok, pl.ds(2 * ROWS + h * HEAD, HEAD)].astype(f32)
            delta[t, :, lane] = jnp.sum(prod.T, axis=0, keepdims=True)


EARLY = 5


def attention_kernel(
    mask, info, seg, lse, delta, cos, sin, q_rows, q_cols, g_rows, g_cols,
    early_mine, early_other, late_mine, late_other,
    d_early_mine, d_early_other, d_late_mine, d_late_other, qg,
    kv, dkv, dq, lse_rows, lists, counts, flags,
):
    dq[...] = jnp.zeros_like(dq)
    for t in range(2):
        for h in range(GROUPS):
            row = lse[h : h + 1, t * TILE : (t + 1) * TILE]
            lse_rows[t, :, pl.ds(h * TILE, TILE)] = row * LOG2E
    me = info[0]
    q_tile = 2 * me
    groups = (
        (early_mine, d_early_mine, 0, 0, EARLY),
        (early_other, d_early_other, 1, 0, EARLY),
        (late_mine, d_late_mine, 0, EARLY, 8 - EARLY),
        (late_other, d_late_other, 1, EARLY, 8 - EARLY),
    )
    starts = (0, 2 * EARLY, 4 * EARLY, 4 * EARLY + 2 * (8 - EARLY))

    def needs(j, away, first_slot):
        slot = lax.shift_right_logical(j, 1) + first_slot
        back_y = (lax.shift_right_logical(me, 2) - slot) & 3
        back_zh = (me ^ (lax.shift_right_logical(slot, 1) & 2)) & 2
        tile = 2 * (4 * back_y + back_zh + ((me ^ away) & 1)) + (j & 1)
        return mask[q_tile, tile] > 0, mask[q_tile + 1, tile] > 0

    for t in range(2):
        lists[t, 0] = t
        counts[t] = 1
    kv[pl.ds(TILES * TILE, TILE), :] = jnp.zeros((TILE, 2 * HEAD), bf16)
    dkv[pl.ds(TILES * TILE, TILE), :] = jnp.zeros((TILE, 2 * HEAD), f32)
    for (source, dest, away, first_slot, slots), start in zip(groups, starts):

        def collect(j, carry):
            needed = needs(j, away, first_slot)
            flags[start + j] = jnp.where(needed[0] | needed[1], 1, 0)
            here = pl.ds(pl.multiple_of(j * TILE, TILE), TILE)
            there = pl.ds(pl.multiple_of((start + j) * TILE, TILE), TILE)

            @pl.when(needed[0] | needed[1])
            def _():
                kv[there, :] = source[here, :]
                dkv[there, :] = jnp.zeros((TILE, 2 * HEAD), f32)

            @pl.when(jnp.logical_not(needed[0] | needed[1]))
            def _():
                dest[here, :] = jnp.zeros((TILE, 2 * HEAD), bf16)

            for t in range(2):
                add = needed[t]
                if start == 0:
                    add = add & (j != t)

                @pl.when(add)
                def _():
                    count = counts[t]
                    lists[t, count] = start + j
                    counts[t] = count + 1

            return carry

        lax.fori_loop(0, 2 * slots, collect, 0)

    def two_tiles(t, first, second, allowed):
        ones = pl.ds(pl.multiple_of(first * TILE, TILE), TILE)
        twos = pl.ds(pl.multiple_of(second * TILE, TILE), TILE)
        keys = jnp.concatenate([kv[ones, :HEAD], kv[twos, :HEAD]], 0)
        vals = jnp.concatenate([kv[ones, HEAD:], kv[twos, HEAD:]], 0)
        scores = jnp.dot(keys, q_cols[t], preferred_element_type=f32)
        probs = jnp.exp2(scores * (SCALE * LOG2E) - lse_rows[t])
        if allowed is not None:
            probs = jnp.concatenate([jnp.where(allowed, probs[:TILE], 0.0), probs[TILE:]], 0)
        dprobs = jnp.dot(vals, g_cols[t], preferred_element_type=f32)
        dscore = (probs * (dprobs - delta[t])).astype(bf16)
        probs = probs.astype(bf16)
        dkeys = jnp.dot(dscore, q_rows[t], preferred_element_type=f32)
        dvals = jnp.dot(probs, g_rows[t], preferred_element_type=f32)
        dqs = jnp.dot(keys.T, dscore, preferred_element_type=f32)
        return t, ones, twos, dkeys, dvals, dqs

    def add(t, ones, twos, dkeys, dvals, dqs):
        dq[t] += dqs
        dkv[ones, :HEAD] += dkeys[:TILE]
        dkv[ones, HEAD:] += dvals[:TILE]
        dkv[twos, :HEAD] += dkeys[TILE:]
        dkv[twos, HEAD:] += dvals[TILE:]

    most = jnp.maximum(counts[0], counts[1])

    def fill(i, carry):
        for t in range(2):

            @pl.when(i >= counts[t])
            def _():
                lists[t, i] = TILES

        return carry

    lax.fori_loop(jnp.minimum(counts[0], counts[1]), most + 1, fill, 0)
    causal = lax.broadcasted_iota(jnp.int32, (TILE, TILE), 0) <= (
        lax.broadcasted_iota(jnp.int32, (TILE, TILE), 1)
    )
    terms = []
    for t in range(2):
        row = jnp.broadcast_to(seg[q_tile + t], (TILE, TILE)).astype(f32)
        listed = jnp.where(mask[q_tile + t, q_tile + t] > 0, 1.0, 0.0)
        one = jnp.where((row.T == row) & causal, 1.0, 0.0) * listed
        terms.append(two_tiles(t, t, lists[t, 1], jnp.concatenate([one] * GROUPS, 1) > 0.5))
    for term in terms:
        add(*term)

    def rest(i, carry):
        terms = [two_tiles(t, lists[t, 2 * i], lists[t, 2 * i + 1], None) for t in range(2)]
        for term in terms:
            add(*term)
        return carry

    lax.fori_loop(1, lax.shift_right_logical(most + 1, 1), rest, 0)

    for (source, dest, away, first_slot, slots), start in zip(groups, starts):

        def give(j, carry):
            @pl.when(flags[start + j] > 0)
            def _():
                here = pl.ds(pl.multiple_of(j * TILE, TILE), TILE)
                there = pl.ds(pl.multiple_of((start + j) * TILE, TILE), TILE)
                dest[here, :] = dkv[there, :].astype(bf16)

            return carry

        lax.fori_loop(0, 2 * slots, give, 0)

    for t in range(2):
        tok = pl.ds(t * TILE, TILE)
        c, s = cos[tok, :].T, sin[tok, :].T
        for h in range(GROUPS):
            g = dq[t, :, pl.ds(h * TILE, TILE)] * SCALE
            u = g * s
            half = HEAD // 2
            turned = jnp.concatenate([u[half:], -u[:half]], 0)
            qg[pl.ds(h * HEAD, HEAD), tok] = (g * c + turned).astype(bf16)


def vmem(n):
    return [pl.BlockSpec(memory_space=pltpu.VMEM)] * n


def prep(joined, cos, sin):
    s = jax.ShapeDtypeStruct
    return pl.pallas_call(
        prep_kernel,
        out_shape=(
            s((2, ROWS, HEAD), bf16),
            s((2, HEAD, ROWS), bf16),
            s((2, ROWS, HEAD), bf16),
            s((2, HEAD, ROWS), bf16),
            s((2, 1, ROWS), f32),
        ),
        in_specs=vmem(3),
        out_specs=tuple(vmem(5)),
        compiler_params=pltpu.CompilerParams(vmem_limit_bytes=6 << 20),
        cost_estimate=pl.CostEstimate(flops=1000000, bytes_accessed=10000, transcendentals=0),
        name="prep",
    )(joined, cos, sin)


def attention(mask, info, *operands):
    s = jax.ShapeDtypeStruct
    early, late = (s((n * TOK, 2 * HEAD), bf16) for n in (EARLY, 8 - EARLY))
    return pl.pallas_call(
        attention_kernel,
        out_shape=(early, early, late, late, s((ROWS, TOK), bf16)),
        in_specs=[pl.BlockSpec(memory_space=pltpu.SMEM)] * 2 + vmem(len(operands)),
        out_specs=tuple(vmem(5)),
        scratch_shapes=[
            pltpu.VMEM(((TILES + 1) * TILE, 2 * HEAD), bf16),
            pltpu.VMEM(((TILES + 1) * TILE, 2 * HEAD), f32),
            pltpu.VMEM((2, HEAD, ROWS), f32),
            pltpu.VMEM((2, 1, ROWS), f32),
            pltpu.SMEM((2, TILES + 1), jnp.int32),
            pltpu.SMEM((2,), jnp.int32),
            pltpu.SMEM((TILES,), jnp.int32),
        ],
        compiler_params=pltpu.CompilerParams(vmem_limit_bytes=16 << 20),
        cost_estimate=pl.CostEstimate(
            flops=2000000000, bytes_accessed=8000000, transcendentals=1000000
        ),
        name="attention",
    )(mask, info, *operands)


def make_block(key, value, positions):
    s = jax.ShapeDtypeStruct
    inverse = jnp.asarray(np.concatenate([INVERSE, INVERSE])[None, :])
    return pl.pallas_call(
        block_kernel,
        out_shape=(s((TOK, HEAD), f32), s((TOK, HEAD), f32), s((TOK, 2 * HEAD), bf16)),
        in_specs=vmem(4),
        out_specs=tuple(vmem(3)),
        cost_estimate=pl.CostEstimate(flops=5000000, bytes_accessed=700000, transcendentals=60000),
        name="block",
    )(key, value, positions.reshape(2, 1, TILE), inverse)


STEP_ROWS = 640


ORDERS = (
    ((0, 1), (1, 1), (2, 1), (3, 1), (0, 0), (1, 0), (2, 0), (3, 0)),
    ((1, 0), (1, 1), (3, 0), (3, 1), (0, 0), (0, 1), (2, 0), (2, 1)),
)


def by_core(offsets):
    pairs = []
    for core, offset in enumerate(offsets):
        if offset is not None:
            for x in range(4):
                for zl in range(2):
                    to = (core * 4 + (x + offset[0]) % 4) * 2 + (zl + offset[1]) % 2
                    pairs.append(((core * 4 + x) * 2 + zl, to))
    return pairs


def send(x, *offsets):
    return lax.ppermute(x, ("core", "x", "zl"), by_core(offsets))


def first_kernel(
    tp, core, own, across, near1, near2, near3, cos, sin, qg, wq, wk, wv,
    out1, out2, out3, kept, grads, weights, sem,
):
    x, zl = lax.shift_right_logical(tp[0], 1), tp[0] & 1

    def fetch(i):
        (x0, z0), (x1, z1) = ORDERS[0][i], ORDERS[1][i]
        to_x = (x + jnp.where(core[0] == 0, x0, x1)) & 3
        to_z = zl ^ jnp.where(core[0] == 0, z0, z1)
        rows = pl.ds(pl.multiple_of((2 * to_x + to_z) * STEP_ROWS, STEP_ROWS), STEP_ROWS)
        slot = i % 3
        return [
            pltpu.make_async_copy(
                source.at[rows, :],
                weights.at[slot, :, pl.ds(start, source.shape[1])],
                sem.at[slot, k],
            )
            for k, (source, start) in enumerate(((wq, 0), (wk, ROWS), (wv, ROWS + HEAD)))
        ]

    flights = [fetch(i) for i in range(8)]
    for flight in flights[:3]:
        for copy in flight:
            copy.start()
    total = own[...].astype(f32) + across[...].astype(f32)
    for near in (near1, near2, near3):
        total += near[...].astype(f32)
    sign = half_sign((TOK, HEAD), 1)
    g = total[:, :HEAD] * SCALE
    key_grad = g * cos[...] - pltpu.roll(g * sin[...], HEAD // 2, 1) * sign
    grads[:ROWS, :] = qg[...]
    grads[ROWS : ROWS + HEAD, :] = key_grad.T.astype(bf16)
    grads[ROWS + HEAD :, :] = total[:, HEAD:].T.astype(bf16)
    for i in range(8):
        for copy in flights[i]:
            copy.wait()
        block = jnp.dot(weights[i % 3], grads[...], preferred_element_type=f32)
        if i < 4:
            (out1, out2)[i // 2][i % 2] = block.astype(bf16)
        else:
            kept[i - 4] = block
        if i >= 6:
            out3[i - 6] = block.astype(bf16)
        if i + 3 < 8:
            for copy in flights[i + 3]:
                copy.start()


def middle_kernel(core, kept, got1, got2, got3, base, out1, out2, out3):
    @pl.when(core[0] == 0)
    def _():
        base[...] = kept[0] + got1[0].astype(f32)
        out1[...] = (kept[1] + got1[1].astype(f32)).astype(bf16)
        out2[...] = (kept[2] + got2[0].astype(f32)).astype(bf16)
        out3[...] = (kept[3] + got2[1].astype(f32)).astype(bf16)

    @pl.when(core[0] != 0)
    def _():
        total = [
            kept[i] + got1[i].astype(f32) + got2[i].astype(f32) + got3[i].astype(f32)
            for i in range(2)
        ]
        base[...] = total[0]
        out1[...] = total[1].astype(bf16)
        out2[...] = jnp.zeros_like(out2)
        out3[...] = jnp.zeros_like(out3)


def last_kernel(core, base, got1, got2, got3, out):
    @pl.when(core[0] == 0)
    def _():
        total = base[...] + got1[...].astype(f32) + got2[...].astype(f32)
        out[...] = (total + got3[...].astype(f32)).astype(bf16)

    @pl.when(core[0] != 0)
    def _():
        out[...] = (base[...] + got1[...].astype(f32)).astype(bf16)


def whole_call(kernel, name, outs, scalars, *operands, large=(), scratch=()):
    outs = tuple(jax.ShapeDtypeStruct(shape, dtype) for shape, dtype in outs)
    return pl.pallas_call(
        kernel,
        out_shape=outs,
        in_specs=[pl.BlockSpec(memory_space=pltpu.SMEM)] * len(scalars)
        + vmem(len(operands))
        + [pl.BlockSpec(memory_space=pl.ANY)] * len(large),
        out_specs=tuple(vmem(len(outs))),
        scratch_shapes=scratch,
        compiler_params=pltpu.CompilerParams(vmem_limit_bytes=(48 if large else 10) << 20),
        cost_estimate=pl.CostEstimate(flops=1000000, bytes_accessed=10000, transcendentals=0),
        name=name,
    )(*scalars, *operands, *large)


def project_and_sum(own, across, near, cos, sin, qg, wq, wk, wv):
    tp = lax.axis_index(TP).reshape(1)
    core = lax.axis_index("core").reshape(1)
    one, two, four = ((n, STEP_ROWS, TOK) for n in (1, 2, 4))
    one = one[1:]
    first, second, third, kept = whole_call(
        first_kernel,
        "first",
        [(two, bf16), (two, bf16), (two, bf16), (four, f32)],
        (tp, core),
        own, across, *near, cos, sin, qg,
        large=(wq, wk, wv),
        scratch=[
            pltpu.VMEM((ROWS + 2 * HEAD, TOK), bf16),
            pltpu.VMEM((3, STEP_ROWS, ROWS + 2 * HEAD), bf16),
            pltpu.SemaphoreType.DMA((3, 3)),
        ],
    )
    got1 = send(first, (0, 1), (1, 0))
    got2 = send(second, (0, 1), (3, 0))
    got3 = send(third, None, (2, 0))
    base, out1, out2, out3 = whole_call(
        middle_kernel,
        "middle",
        [(one, f32), (one, bf16), (one, bf16), (one, bf16)],
        (core,),
        kept, got1, got2, got3,
    )
    got1 = send(out1, (1, 0), (0, 1))
    got2 = send(out2, (2, 0), None)
    got3 = send(out3, (3, 0), None)
    return whole_call(last_kernel, "last", [(one, bf16)], (core,), base, got1, got2, got3)[0]


def local(
    query, key, value, att, grad, lse, block_mask, positions, segments, w_query, key_weight,
    value_weight,
):
    me = lax.axis_index(CTX)
    cos, sin, block = make_block(key, value, positions)

    across = swap_zh(block)
    joined = jnp.concatenate([query, grad, att], 1)
    joined, again = lax.optimization_barrier((joined, block))
    near = [shift_y(again, k) for k in (1, 2, 3)]
    across, joined = lax.optimization_barrier((across, joined))
    far = [shift_y(across, k) for k in (1, 2, 3)]
    q_rows, q_cols, g_rows, g_cols, delta = prep(joined, cos, sin)
    early = jnp.concatenate([block] + near + [across], 0)
    late = jnp.concatenate(far, 0)

    early_mine, early_other, late_mine, late_other, query_grad = attention(
        block_mask, me.reshape(1), segments.reshape(TILES, 1, TILE), lse, delta, cos, sin, q_rows,
        q_cols, g_rows, g_cols, early, swap_core(early), late, swap_core(late),
    )

    late = late_mine.astype(f32) + swap_core(late_other).astype(f32)
    early = early_mine.astype(f32) + swap_core(early_other).astype(f32)
    own, across = early[:TOK], early[4 * TOK :]
    parts = [early[k * TOK : (k + 1) * TOK].astype(bf16) for k in (1, 2, 3)]
    parts += [late[k * TOK : (k + 1) * TOK].astype(bf16) for k in range(3)]
    own, across, parts = lax.optimization_barrier((own, across, parts))
    far = [shift_y(parts[2 + k], -k) for k in (1, 2, 3)]
    near = [shift_y(parts[k - 1], -k) for k in (1, 2, 3)]
    across = across + sum(p.astype(f32) for p in far)
    across = swap_zh(lax.optimization_barrier(across.astype(bf16)))
    return project_and_sum(
        own, across, near, cos, sin, query_grad, w_query, key_weight, value_weight
    )


def solution(mesh):
    fine = Mesh(mesh.devices.reshape(4, 2, 2, 4, 2), ("y", "zh", "core", "x", "zl"))
    in_specs = (
        P(CTX, TP),
        P(CTX, TP),
        P(CTX, TP),
        P(CTX, TP),
        P(CTX, TP),
        P(TP, CTX),
        P(),
        P(CTX),
        P(),
        P(None, TP),
        P(None, TP),
        P(None, TP),
    )
    return jax.shard_map(
        local, mesh=fine, in_specs=in_specs, out_specs=P(TP, CTX), check_vma=False
    )
```

```python
import numpy as np
import jax
import jax.numpy as jnp
from jax import lax
from jax.experimental import pallas as pl
from jax.experimental.pallas import tpu as pltpu
from jax.sharding import Mesh, PartitionSpec as P

HEAD = 128
TILE = 128
GROUPS = 5
TOK = 256
TILES = 32
ROWS = GROUPS * TILE
SCALE = HEAD**-0.5
ROPE_BASE = 1000000.0
LOG2E = 1.4426950408889634
CTX = ("y", "zh", "core")
TP = ("x", "zl")

f32 = jnp.float32
bf16 = jnp.bfloat16


def shift(x, axes, sizes, offs):
    perm = []
    for source in np.ndindex(*sizes):
        dest = tuple((a + o) % s for a, o, s in zip(source, offs, sizes))
        perm.append(
            (int(np.ravel_multi_index(source, sizes)), int(np.ravel_multi_index(dest, sizes)))
        )
    return lax.ppermute(x, axes, perm)


def shift_y(x, k):
    return shift(x, ("y",), (4,), (k % 4,))


def swap_zh(x):
    return shift(x, ("zh",), (2,), (1,))


def swap_core(x):
    return shift(x, ("core",), (2,), (1,))


INVERSE = np.power(np.float64(ROPE_BASE), -np.arange(HEAD // 2) * (2.0 / HEAD)).astype(np.float32)


def half_sign(shape, axis):
    return jnp.where(lax.broadcasted_iota(jnp.int32, shape, axis) < HEAD // 2, -1.0, 1.0).astype(f32)


def block_kernel(key, value, positions, inverse, cos, sin, block):
    sign = half_sign((TILE, HEAD), 1)
    for t in range(2):
        tok = pl.ds(t * TILE, TILE)
        place = jnp.broadcast_to(positions[t].astype(f32), (TILE, TILE)).T
        angles = place * inverse[...]
        c, s = jnp.cos(angles), jnp.sin(angles)
        cos[tok, :] = c
        sin[tok, :] = s
        x = key[tok, :].astype(f32)
        block[tok, :HEAD] = (x * c + pltpu.roll(x, HEAD // 2, 1) * (s * sign)).astype(bf16)
        block[tok, HEAD:] = value[tok, :]


def prep_kernel(joined, cos, sin, q_rows, q_cols, g_rows, g_cols, delta):
    sign = half_sign((TILE, HEAD), 1)
    for t in range(2):
        tok = pl.ds(t * TILE, TILE)
        c, s = cos[tok, :], sin[tok, :] * sign
        for h in range(GROUPS):
            feat = pl.ds(h * HEAD, HEAD)
            lane = pl.ds(h * TILE, TILE)
            x = joined[tok, feat].astype(f32)
            rot = (x * c + pltpu.roll(x, HEAD // 2, 1) * s).astype(bf16)
            q_rows[t, lane, :] = rot
            q_cols[t, :, lane] = rot.T
            g = joined[tok, pl.ds(ROWS + h * HEAD, HEAD)]
            g_rows[t, lane, :] = g
            g_cols[t, :, lane] = g.T
            prod = g.astype(f32) * joined[tok, pl.ds(2 * ROWS + h * HEAD, HEAD)].astype(f32)
            delta[t, :, lane] = jnp.sum(prod.T, axis=0, keepdims=True)


EARLY = 5


def attention_kernel(
    mask, info, seg, lse, delta, cos, sin, q_rows, q_cols, g_rows, g_cols,
    early_mine, early_other, late_mine, late_other,
    d_early_mine, d_early_other, d_late_mine, d_late_other, qg,
    kv, dkv, dq, lse_rows, lists, counts, flags,
):
    dq[...] = jnp.zeros_like(dq)
    for t in range(2):
        for h in range(GROUPS):
            row = lse[h : h + 1, t * TILE : (t + 1) * TILE]
            lse_rows[t, :, pl.ds(h * TILE, TILE)] = row * LOG2E
    me = info[0]
    q_tile = 2 * me
    groups = (
        (early_mine, d_early_mine, 0, 0, EARLY),
        (early_other, d_early_other, 1, 0, EARLY),
        (late_mine, d_late_mine, 0, EARLY, 8 - EARLY),
        (late_other, d_late_other, 1, EARLY, 8 - EARLY),
    )
    starts = (0, 2 * EARLY, 4 * EARLY, 4 * EARLY + 2 * (8 - EARLY))

    def needs(j, away, first_slot):
        slot = lax.shift_right_logical(j, 1) + first_slot
        back_y = (lax.shift_right_logical(me, 2) - slot) & 3
        back_zh = (me ^ (lax.shift_right_logical(slot, 1) & 2)) & 2
        tile = 2 * (4 * back_y + back_zh + ((me ^ away) & 1)) + (j & 1)
        return mask[q_tile, tile] > 0, mask[q_tile + 1, tile] > 0

    for t in range(2):
        lists[t, 0] = t
        counts[t] = 1
    kv[pl.ds(TILES * TILE, TILE), :] = jnp.zeros((TILE, 2 * HEAD), bf16)
    dkv[pl.ds(TILES * TILE, TILE), :] = jnp.zeros((TILE, 2 * HEAD), f32)
    for (source, dest, away, first_slot, slots), start in zip(groups, starts):

        def collect(j, carry):
            needed = needs(j, away, first_slot)
            flags[start + j] = jnp.where(needed[0] | needed[1], 1, 0)
            here = pl.ds(pl.multiple_of(j * TILE, TILE), TILE)
            there = pl.ds(pl.multiple_of((start + j) * TILE, TILE), TILE)

            @pl.when(needed[0] | needed[1])
            def _():
                kv[there, :] = source[here, :]
                dkv[there, :] = jnp.zeros((TILE, 2 * HEAD), f32)

            @pl.when(jnp.logical_not(needed[0] | needed[1]))
            def _():
                dest[here, :] = jnp.zeros((TILE, 2 * HEAD), bf16)

            for t in range(2):
                add = needed[t]
                if start == 0:
                    add = add & (j != t)

                @pl.when(add)
                def _():
                    count = counts[t]
                    lists[t, count] = start + j
                    counts[t] = count + 1

            return carry

        lax.fori_loop(0, 2 * slots, collect, 0)

    def two_tiles(t, first, second, allowed):
        ones = pl.ds(pl.multiple_of(first * TILE, TILE), TILE)
        twos = pl.ds(pl.multiple_of(second * TILE, TILE), TILE)
        keys = jnp.concatenate([kv[ones, :HEAD], kv[twos, :HEAD]], 0)
        vals = jnp.concatenate([kv[ones, HEAD:], kv[twos, HEAD:]], 0)
        scores = jnp.dot(keys, q_cols[t], preferred_element_type=f32)
        probs = jnp.exp2(scores * (SCALE * LOG2E) - lse_rows[t])
        if allowed is not None:
            probs = jnp.concatenate([jnp.where(allowed, probs[:TILE], 0.0), probs[TILE:]], 0)
        dprobs = jnp.dot(vals, g_cols[t], preferred_element_type=f32)
        dscore = (probs * (dprobs - delta[t])).astype(bf16)
        probs = probs.astype(bf16)
        dkeys = jnp.dot(dscore, q_rows[t], preferred_element_type=f32)
        dvals = jnp.dot(probs, g_rows[t], preferred_element_type=f32)
        dqs = jnp.dot(keys.T, dscore, preferred_element_type=f32)
        return t, ones, twos, dkeys, dvals, dqs

    def add(t, ones, twos, dkeys, dvals, dqs):
        dq[t] += dqs
        dkv[ones, :HEAD] += dkeys[:TILE]
        dkv[ones, HEAD:] += dvals[:TILE]
        dkv[twos, :HEAD] += dkeys[TILE:]
        dkv[twos, HEAD:] += dvals[TILE:]

    most = jnp.maximum(counts[0], counts[1])

    def fill(i, carry):
        for t in range(2):

            @pl.when(i >= counts[t])
            def _():
                lists[t, i] = TILES

        return carry

    lax.fori_loop(jnp.minimum(counts[0], counts[1]), most + 1, fill, 0)
    causal = lax.broadcasted_iota(jnp.int32, (TILE, TILE), 0) <= (
        lax.broadcasted_iota(jnp.int32, (TILE, TILE), 1)
    )
    terms = []
    for t in range(2):
        row = jnp.broadcast_to(seg[q_tile + t], (TILE, TILE)).astype(f32)
        listed = jnp.where(mask[q_tile + t, q_tile + t] > 0, 1.0, 0.0)
        one = jnp.where((row.T == row) & causal, 1.0, 0.0) * listed
        terms.append(two_tiles(t, t, lists[t, 1], jnp.concatenate([one] * GROUPS, 1) > 0.5))
    for term in terms:
        add(*term)

    def rest(i, carry):
        terms = [two_tiles(t, lists[t, 2 * i], lists[t, 2 * i + 1], None) for t in range(2)]
        for term in terms:
            add(*term)
        return carry

    lax.fori_loop(1, lax.shift_right_logical(most + 1, 1), rest, 0)

    for (source, dest, away, first_slot, slots), start in zip(groups, starts):

        def give(j, carry):
            @pl.when(flags[start + j] > 0)
            def _():
                here = pl.ds(pl.multiple_of(j * TILE, TILE), TILE)
                there = pl.ds(pl.multiple_of((start + j) * TILE, TILE), TILE)
                dest[here, :] = dkv[there, :].astype(bf16)

            return carry

        lax.fori_loop(0, 2 * slots, give, 0)

    for t in range(2):
        tok = pl.ds(t * TILE, TILE)
        c, s = cos[tok, :].T, sin[tok, :].T
        for h in range(GROUPS):
            g = dq[t, :, pl.ds(h * TILE, TILE)] * SCALE
            u = g * s
            half = HEAD // 2
            turned = jnp.concatenate([u[half:], -u[:half]], 0)
            qg[pl.ds(h * HEAD, HEAD), tok] = (g * c + turned).astype(bf16)


def vmem(n):
    return [pl.BlockSpec(memory_space=pltpu.VMEM)] * n


def prep(joined, cos, sin):
    s = jax.ShapeDtypeStruct
    return pl.pallas_call(
        prep_kernel,
        out_shape=(
            s((2, ROWS, HEAD), bf16),
            s((2, HEAD, ROWS), bf16),
            s((2, ROWS, HEAD), bf16),
            s((2, HEAD, ROWS), bf16),
            s((2, 1, ROWS), f32),
        ),
        in_specs=vmem(3),
        out_specs=tuple(vmem(5)),
        compiler_params=pltpu.CompilerParams(vmem_limit_bytes=12 << 20),
        cost_estimate=pl.CostEstimate(flops=1000000, bytes_accessed=10000, transcendentals=0),
        name="prep",
    )(joined, cos, sin)


def attention(mask, info, *operands):
    s = jax.ShapeDtypeStruct
    early, late = (s((n * TOK, 2 * HEAD), bf16) for n in (EARLY, 8 - EARLY))
    return pl.pallas_call(
        attention_kernel,
        out_shape=(early, early, late, late, s((ROWS, TOK), bf16)),
        in_specs=[pl.BlockSpec(memory_space=pltpu.SMEM)] * 2 + vmem(len(operands)),
        out_specs=tuple(vmem(5)),
        scratch_shapes=[
            pltpu.VMEM(((TILES + 1) * TILE, 2 * HEAD), bf16),
            pltpu.VMEM(((TILES + 1) * TILE, 2 * HEAD), f32),
            pltpu.VMEM((2, HEAD, ROWS), f32),
            pltpu.VMEM((2, 1, ROWS), f32),
            pltpu.SMEM((2, TILES + 1), jnp.int32),
            pltpu.SMEM((2,), jnp.int32),
            pltpu.SMEM((TILES,), jnp.int32),
        ],
        compiler_params=pltpu.CompilerParams(vmem_limit_bytes=16 << 20),
        cost_estimate=pl.CostEstimate(
            flops=2000000000, bytes_accessed=8000000, transcendentals=1000000
        ),
        name="attention",
    )(mask, info, *operands)


def make_block(key, value, positions):
    s = jax.ShapeDtypeStruct
    inverse = jnp.asarray(np.concatenate([INVERSE, INVERSE])[None, :])
    return pl.pallas_call(
        block_kernel,
        out_shape=(s((TOK, HEAD), f32), s((TOK, HEAD), f32), s((TOK, 2 * HEAD), bf16)),
        in_specs=vmem(4),
        out_specs=tuple(vmem(3)),
        cost_estimate=pl.CostEstimate(flops=5000000, bytes_accessed=700000, transcendentals=60000),
        name="block",
    )(key, value, positions.reshape(2, 1, TILE), inverse)


STEP_ROWS = 640


ORDERS = (
    ((0, 1), (1, 1), (2, 1), (3, 1), (0, 0), (1, 0), (2, 0), (3, 0)),
    ((1, 0), (1, 1), (3, 0), (3, 1), (0, 0), (0, 1), (2, 0), (2, 1)),
)


def by_core(offsets):
    pairs = []
    for core, offset in enumerate(offsets):
        if offset is not None:
            for x in range(4):
                for zl in range(2):
                    to = (core * 4 + (x + offset[0]) % 4) * 2 + (zl + offset[1]) % 2
                    pairs.append(((core * 4 + x) * 2 + zl, to))
    return pairs


def send(x, *offsets):
    return lax.ppermute(x, ("core", "x", "zl"), by_core(offsets))


def first_kernel(
    tp, core, own, across, near1, near2, near3, cos, sin, qg, wk, wv, wq,
    out1, out2, kept, out3, grads, weights, sem,
):
    x, zl = lax.shift_right_logical(tp[0], 1), tp[0] & 1
    places = []
    for (x0, z0), (x1, z1) in zip(*ORDERS):
        to_x = (x + jnp.where(core[0] == 0, x0, x1)) & 3
        to_z = zl ^ jnp.where(core[0] == 0, z0, z1)
        start = pl.multiple_of((2 * to_x + to_z) * STEP_ROWS, STEP_ROWS)
        places.append(pl.ds(start, STEP_ROWS))
    copies = [
        pltpu.make_async_copy(wq.at[places[i], :], weights.at[i % 3], sem.at[i % 3])
        for i in range(8)
    ]
    for copy in copies[:3]:
        copy.start()
    total = own[...].astype(f32) + across[...].astype(f32)
    for near in (near1, near2, near3):
        total += near[...].astype(f32)
    sign = half_sign((TOK, HEAD), 1)
    g = total[:, :HEAD] * SCALE
    key_grad = g * cos[...] - pltpu.roll(g * sin[...], HEAD // 2, 1) * sign
    grads[:ROWS, :] = qg[...]
    grads[ROWS : ROWS + HEAD, :] = key_grad.T.astype(bf16)
    grads[ROWS + HEAD :, :] = total[:, HEAD:].T.astype(bf16)
    for i in range(8):
        copies[i].wait()
        joined = jnp.concatenate([weights[i % 3], wk[places[i], :], wv[places[i], :]], 1)
        block = jnp.dot(joined, grads[...], preferred_element_type=f32)
        (out1, out2, kept, out3)[i // 2][i % 2] = block.astype(bf16)
        if i + 3 < 8:
            copies[i + 3].start()


def middle_kernel(core, kept, more, got1, got2, got3, base, out1, out2, out3):
    @pl.when(core[0] == 0)
    def _():
        base[...] = kept[0].astype(f32) + got1[0].astype(f32)
        out1[...] = (kept[1].astype(f32) + got1[1].astype(f32)).astype(bf16)
        out2[...] = (more[0].astype(f32) + got2[0].astype(f32)).astype(bf16)
        out3[...] = (more[1].astype(f32) + got2[1].astype(f32)).astype(bf16)

    @pl.when(core[0] != 0)
    def _():
        total = []
        for i in range(2):
            arrived = got1[i].astype(f32) + got2[i].astype(f32) + got3[i].astype(f32)
            total.append(kept[i].astype(f32) + arrived)
        base[...] = total[0]
        out1[...] = total[1].astype(bf16)
        out2[...] = jnp.zeros_like(out2)
        out3[...] = jnp.zeros_like(out3)


def last_kernel(core, base, got1, got2, got3, out):
    @pl.when(core[0] == 0)
    def _():
        total = base[...] + got1[...].astype(f32) + got2[...].astype(f32)
        out[...] = (total + got3[...].astype(f32)).astype(bf16)

    @pl.when(core[0] != 0)
    def _():
        out[...] = (base[...] + got1[...].astype(f32)).astype(bf16)


def whole_call(kernel, name, outs, scalars, *operands, large=(), scratch=(), cost=(1300000, 3000000)):
    outs = tuple(jax.ShapeDtypeStruct(shape, dtype) for shape, dtype in outs)
    return pl.pallas_call(
        kernel,
        out_shape=outs,
        in_specs=[pl.BlockSpec(memory_space=pltpu.SMEM)] * len(scalars)
        + vmem(len(operands))
        + [pl.BlockSpec(memory_space=pl.ANY)] * len(large),
        out_specs=tuple(vmem(len(outs))),
        scratch_shapes=scratch,
        compiler_params=pltpu.CompilerParams(vmem_limit_bytes=(44 if large else 16) << 20),
        cost_estimate=pl.CostEstimate(
            flops=cost[0], bytes_accessed=cost[1], transcendentals=0
        ),
        name=name,
    )(*scalars, *operands, *large)


def project_and_sum(own, across, near, cos, sin, qg, wq, wk, wv):
    tp = lax.axis_index(TP).reshape(1)
    core = lax.axis_index("core").reshape(1)
    one, two = (STEP_ROWS, TOK), (2, STEP_ROWS, TOK)
    first, second, kept, third = whole_call(
        first_kernel,
        "first",
        [(two, bf16)] * 4,
        (tp, core),
        own, across, *near, cos, sin, qg, wk, wv,
        large=(wq,),
        scratch=[
            pltpu.VMEM((ROWS + 2 * HEAD, TOK), bf16),
            pltpu.VMEM((3, STEP_ROWS, ROWS), bf16),
            pltpu.SemaphoreType.DMA((3,)),
        ],
        cost=(2350000000, 12000000),
    )
    got1 = send(first, (0, 1), (1, 0))
    got2 = send(second, (0, 1), (3, 0))
    got3 = send(third, None, (2, 0))
    base, out1, out2, out3 = whole_call(
        middle_kernel,
        "middle",
        [(one, f32), (one, bf16), (one, bf16), (one, bf16)],
        (core,),
        kept, third, got1, got2, got3,
    )
    got1 = send(out1, (1, 0), (0, 1))
    got2 = send(out2, (2, 0), None)
    got3 = send(out3, (3, 0), None)
    return whole_call(last_kernel, "last", [(one, bf16)], (core,), base, got1, got2, got3)[0]


def local(
    query, key, value, att, grad, lse, block_mask, positions, segments, w_query, key_weight,
    value_weight,
):
    me = lax.axis_index(CTX)
    cos, sin, block = make_block(key, value, positions)

    across = swap_zh(block)
    joined = jnp.concatenate([query, grad, att], 1)
    joined, again = lax.optimization_barrier((joined, block))
    near = [shift_y(again, k) for k in (1, 2, 3)]
    across, joined = lax.optimization_barrier((across, joined))
    far = [shift_y(across, k) for k in (1, 2, 3)]
    q_rows, q_cols, g_rows, g_cols, delta = prep(joined, cos, sin)
    early = jnp.concatenate([block] + near + [across], 0)
    late = jnp.concatenate(far, 0)

    early_mine, early_other, late_mine, late_other, query_grad = attention(
        block_mask, me.reshape(1), segments.reshape(TILES, 1, TILE), lse, delta, cos, sin, q_rows,
        q_cols, g_rows, g_cols, early, swap_core(early), late, swap_core(late),
    )

    late = late_mine.astype(f32) + swap_core(late_other).astype(f32)
    early = early_mine.astype(f32) + swap_core(early_other).astype(f32)
    own, across = early[:TOK], early[4 * TOK :]
    parts = [early[k * TOK : (k + 1) * TOK].astype(bf16) for k in (1, 2, 3)]
    parts += [late[k * TOK : (k + 1) * TOK].astype(bf16) for k in range(3)]
    own, across, parts = lax.optimization_barrier((own, across, parts))
    far = [shift_y(parts[2 + k], -k) for k in (1, 2, 3)]
    near = [shift_y(parts[k - 1], -k) for k in (1, 2, 3)]
    across = across + sum(p.astype(f32) for p in far)
    across = swap_zh(lax.optimization_barrier(across.astype(bf16)))
    return project_and_sum(
        own, across, near, cos, sin, query_grad, w_query, key_weight, value_weight
    )


def solution(mesh):
    fine = Mesh(mesh.devices.reshape(4, 2, 2, 4, 2), ("y", "zh", "core", "x", "zl"))
    in_specs = (
        P(CTX, TP),
        P(CTX, TP),
        P(CTX, TP),
        P(CTX, TP),
        P(CTX, TP),
        P(TP, CTX),
        P(),
        P(CTX),
        P(),
        P(None, TP),
        P(None, TP),
        P(None, TP),
    )
    return jax.shard_map(
        local, mesh=fine, in_specs=in_specs, out_specs=P(TP, CTX), check_vma=False
    )
```

```python
import numpy as np
import jax
import jax.numpy as jnp
from jax import lax
from jax.experimental import pallas as pl
from jax.experimental.pallas import tpu as pltpu
from jax.sharding import Mesh, PartitionSpec as P

HEAD = 128
TILE = 128
GROUPS = 5
TOK = 256
TILES = 32
ROWS = GROUPS * TILE
SCALE = HEAD**-0.5
ROPE_BASE = 1000000.0
LOG2E = 1.4426950408889634
CTX = ("y", "zh", "core")
TP = ("x", "zl")

f32 = jnp.float32
bf16 = jnp.bfloat16


def shift(x, axes, sizes, offs):
    perm = []
    for source in np.ndindex(*sizes):
        dest = tuple((a + o) % s for a, o, s in zip(source, offs, sizes))
        perm.append(
            (int(np.ravel_multi_index(source, sizes)), int(np.ravel_multi_index(dest, sizes)))
        )
    return lax.ppermute(x, axes, perm)


def shift_y(x, k):
    return shift(x, ("y",), (4,), (k % 4,))


def swap_zh(x):
    return shift(x, ("zh",), (2,), (1,))


def swap_core(x):
    return shift(x, ("core",), (2,), (1,))


INVERSE = np.power(np.float64(ROPE_BASE), -np.arange(HEAD // 2) * (2.0 / HEAD)).astype(np.float32)


def half_sign(shape, axis):
    return jnp.where(lax.broadcasted_iota(jnp.int32, shape, axis) < HEAD // 2, -1.0, 1.0).astype(f32)


def block_kernel(key, value, positions, inverse, cos, sin, block):
    sign = half_sign((TILE, HEAD), 1)
    for t in range(2):
        tok = pl.ds(t * TILE, TILE)
        place = jnp.broadcast_to(positions[t].astype(f32), (TILE, TILE)).T
        angles = place * inverse[...]
        c, s = jnp.cos(angles), jnp.sin(angles)
        cos[tok, :] = c
        sin[tok, :] = s
        x = key[tok, :].astype(f32)
        block[tok, :HEAD] = (x * c + pltpu.roll(x, HEAD // 2, 1) * (s * sign)).astype(bf16)
        block[tok, HEAD:] = value[tok, :]


def prep_kernel(joined, cos, sin, q_rows, q_cols, g_rows, g_cols, delta):
    sign = half_sign((TILE, HEAD), 1)
    for t in range(2):
        tok = pl.ds(t * TILE, TILE)
        c, s = cos[tok, :], sin[tok, :] * sign
        for h in range(GROUPS):
            feat = pl.ds(h * HEAD, HEAD)
            lane = pl.ds(h * TILE, TILE)
            x = joined[tok, feat].astype(f32)
            rot = (x * c + pltpu.roll(x, HEAD // 2, 1) * s).astype(bf16)
            q_rows[t, lane, :] = rot
            q_cols[t, :, lane] = rot.T
            g = joined[tok, pl.ds(ROWS + h * HEAD, HEAD)]
            g_rows[t, lane, :] = g
            g_cols[t, :, lane] = g.T
            prod = g.astype(f32) * joined[tok, pl.ds(2 * ROWS + h * HEAD, HEAD)].astype(f32)
            delta[t, :, lane] = jnp.sum(prod.T, axis=0, keepdims=True)


EARLY = 5


def attention_kernel(
    mask, info, seg, lse, delta, cos, sin, q_rows, q_cols, g_rows, g_cols,
    early_mine, early_other, late_mine, late_other,
    d_early_mine, d_early_other, d_late_mine, d_late_other, qg,
    kv, dkv, dq, lse_rows, lists, counts, flags,
):
    dq[...] = jnp.zeros_like(dq)
    for t in range(2):
        for h in range(GROUPS):
            row = lse[h : h + 1, t * TILE : (t + 1) * TILE]
            lse_rows[t, :, pl.ds(h * TILE, TILE)] = row * LOG2E
    me = info[0]
    q_tile = 2 * me
    groups = (
        (early_mine, d_early_mine, 0, 0, EARLY),
        (early_other, d_early_other, 1, 0, EARLY),
        (late_mine, d_late_mine, 0, EARLY, 8 - EARLY),
        (late_other, d_late_other, 1, EARLY, 8 - EARLY),
    )
    starts = (0, 2 * EARLY, 4 * EARLY, 4 * EARLY + 2 * (8 - EARLY))

    def needs(j, away, first_slot):
        slot = lax.shift_right_logical(j, 1) + first_slot
        back_y = (lax.shift_right_logical(me, 2) - slot) & 3
        back_zh = (me ^ (lax.shift_right_logical(slot, 1) & 2)) & 2
        tile = 2 * (4 * back_y + back_zh + ((me ^ away) & 1)) + (j & 1)
        return mask[q_tile, tile] > 0, mask[q_tile + 1, tile] > 0

    for t in range(2):
        lists[t, 0] = t
        counts[t] = 1
    kv[pl.ds(TILES * TILE, TILE), :] = jnp.zeros((TILE, 2 * HEAD), bf16)
    dkv[pl.ds(TILES * TILE, TILE), :] = jnp.zeros((TILE, 2 * HEAD), f32)
    for (source, dest, away, first_slot, slots), start in zip(groups, starts):

        def collect(j, carry):
            needed = needs(j, away, first_slot)
            flags[start + j] = jnp.where(needed[0] | needed[1], 1, 0)
            here = pl.ds(pl.multiple_of(j * TILE, TILE), TILE)
            there = pl.ds(pl.multiple_of((start + j) * TILE, TILE), TILE)

            @pl.when(needed[0] | needed[1])
            def _():
                kv[there, :] = source[here, :]
                dkv[there, :] = jnp.zeros((TILE, 2 * HEAD), f32)

            @pl.when(jnp.logical_not(needed[0] | needed[1]))
            def _():
                dest[here, :] = jnp.zeros((TILE, 2 * HEAD), bf16)

            for t in range(2):
                add = needed[t]
                if start == 0:
                    add = add & (j != t)

                @pl.when(add)
                def _():
                    count = counts[t]
                    lists[t, count] = start + j
                    counts[t] = count + 1

            return carry

        lax.fori_loop(0, 2 * slots, collect, 0)

    def two_tiles(t, first, second, allowed):
        ones = pl.ds(pl.multiple_of(first * TILE, TILE), TILE)
        twos = pl.ds(pl.multiple_of(second * TILE, TILE), TILE)
        keys = jnp.concatenate([kv[ones, :HEAD], kv[twos, :HEAD]], 0)
        vals = jnp.concatenate([kv[ones, HEAD:], kv[twos, HEAD:]], 0)
        scores = jnp.dot(keys, q_cols[t], preferred_element_type=f32)
        probs = jnp.exp2(scores * (SCALE * LOG2E) - lse_rows[t])
        if allowed is not None:
            probs = jnp.concatenate([jnp.where(allowed, probs[:TILE], 0.0), probs[TILE:]], 0)
        dprobs = jnp.dot(vals, g_cols[t], preferred_element_type=f32)
        dscore = (probs * (dprobs - delta[t])).astype(bf16)
        probs = probs.astype(bf16)
        dkeys = jnp.dot(dscore, q_rows[t], preferred_element_type=f32)
        dvals = jnp.dot(probs, g_rows[t], preferred_element_type=f32)
        dqs = jnp.dot(keys.T, dscore, preferred_element_type=f32)
        return t, ones, twos, dkeys, dvals, dqs

    def add(t, ones, twos, dkeys, dvals, dqs):
        dq[t] += dqs
        dkv[ones, :HEAD] += dkeys[:TILE]
        dkv[ones, HEAD:] += dvals[:TILE]
        dkv[twos, :HEAD] += dkeys[TILE:]
        dkv[twos, HEAD:] += dvals[TILE:]

    most = jnp.maximum(counts[0], counts[1])

    def fill(i, carry):
        for t in range(2):

            @pl.when(i >= counts[t])
            def _():
                lists[t, i] = TILES

        return carry

    lax.fori_loop(jnp.minimum(counts[0], counts[1]), most + 1, fill, 0)
    causal = lax.broadcasted_iota(jnp.int32, (TILE, TILE), 0) <= (
        lax.broadcasted_iota(jnp.int32, (TILE, TILE), 1)
    )
    terms = []
    for t in range(2):
        row = jnp.broadcast_to(seg[q_tile + t], (TILE, TILE)).astype(f32)
        listed = jnp.where(mask[q_tile + t, q_tile + t] > 0, 1.0, 0.0)
        one = jnp.where((row.T == row) & causal, 1.0, 0.0) * listed
        terms.append(two_tiles(t, t, lists[t, 1], jnp.concatenate([one] * GROUPS, 1) > 0.5))
    for term in terms:
        add(*term)

    def rest(i, carry):
        terms = [two_tiles(t, lists[t, 2 * i], lists[t, 2 * i + 1], None) for t in range(2)]
        for term in terms:
            add(*term)
        return carry

    lax.fori_loop(1, lax.shift_right_logical(most + 1, 1), rest, 0)

    for (source, dest, away, first_slot, slots), start in zip(groups, starts):

        def give(j, carry):
            @pl.when(flags[start + j] > 0)
            def _():
                here = pl.ds(pl.multiple_of(j * TILE, TILE), TILE)
                there = pl.ds(pl.multiple_of((start + j) * TILE, TILE), TILE)
                dest[here, :] = dkv[there, :].astype(bf16)

            return carry

        lax.fori_loop(0, 2 * slots, give, 0)

    for t in range(2):
        tok = pl.ds(t * TILE, TILE)
        c, s = cos[tok, :].T, sin[tok, :].T
        for h in range(GROUPS):
            g = dq[t, :, pl.ds(h * TILE, TILE)] * SCALE
            u = g * s
            half = HEAD // 2
            turned = jnp.concatenate([u[half:], -u[:half]], 0)
            qg[pl.ds(h * HEAD, HEAD), tok] = (g * c + turned).astype(bf16)


def vmem(n):
    return [pl.BlockSpec(memory_space=pltpu.VMEM)] * n


def prep(joined, cos, sin):
    s = jax.ShapeDtypeStruct
    return pl.pallas_call(
        prep_kernel,
        out_shape=(
            s((2, ROWS, HEAD), bf16),
            s((2, HEAD, ROWS), bf16),
            s((2, ROWS, HEAD), bf16),
            s((2, HEAD, ROWS), bf16),
            s((2, 1, ROWS), f32),
        ),
        in_specs=vmem(3),
        out_specs=tuple(vmem(5)),
        compiler_params=pltpu.CompilerParams(vmem_limit_bytes=12 << 20),
        cost_estimate=pl.CostEstimate(flops=1000000, bytes_accessed=10000, transcendentals=0),
        name="prep",
    )(joined, cos, sin)


def attention(mask, info, *operands):
    s = jax.ShapeDtypeStruct
    early, late = (s((n * TOK, 2 * HEAD), bf16) for n in (EARLY, 8 - EARLY))
    return pl.pallas_call(
        attention_kernel,
        out_shape=(early, early, late, late, s((ROWS, TOK), bf16)),
        in_specs=[pl.BlockSpec(memory_space=pltpu.SMEM)] * 2 + vmem(len(operands)),
        out_specs=tuple(vmem(5)),
        scratch_shapes=[
            pltpu.VMEM(((TILES + 1) * TILE, 2 * HEAD), bf16),
            pltpu.VMEM(((TILES + 1) * TILE, 2 * HEAD), f32),
            pltpu.VMEM((2, HEAD, ROWS), f32),
            pltpu.VMEM((2, 1, ROWS), f32),
            pltpu.SMEM((2, TILES + 1), jnp.int32),
            pltpu.SMEM((2,), jnp.int32),
            pltpu.SMEM((TILES,), jnp.int32),
        ],
        compiler_params=pltpu.CompilerParams(vmem_limit_bytes=16 << 20),
        cost_estimate=pl.CostEstimate(
            flops=2000000000, bytes_accessed=8000000, transcendentals=1000000
        ),
        name="attention",
    )(mask, info, *operands)


def make_block(key, value, positions):
    s = jax.ShapeDtypeStruct
    inverse = jnp.asarray(np.concatenate([INVERSE, INVERSE])[None, :])
    return pl.pallas_call(
        block_kernel,
        out_shape=(s((TOK, HEAD), f32), s((TOK, HEAD), f32), s((TOK, 2 * HEAD), bf16)),
        in_specs=vmem(4),
        out_specs=tuple(vmem(3)),
        cost_estimate=pl.CostEstimate(flops=5000000, bytes_accessed=700000, transcendentals=60000),
        name="block",
    )(key, value, positions.reshape(2, 1, TILE), inverse)


WIDTH = 5120
STEP_ROWS = 640


def query_part_kernel(qg, wq, out):
    def step(i, carry):
        rows = pl.ds(pl.multiple_of(i * STEP_ROWS, STEP_ROWS), STEP_ROWS)
        out[rows, :] = jnp.dot(wq[rows, :], qg[...], preferred_element_type=f32).astype(bf16)
        return carry

    lax.fori_loop(0, WIDTH // STEP_ROWS, step, 0)


def query_part(qg, wq):
    return pl.pallas_call(
        query_part_kernel,
        out_shape=jax.ShapeDtypeStruct((WIDTH, TOK), bf16),
        in_specs=vmem(2),
        out_specs=vmem(1)[0],
        compiler_params=pltpu.CompilerParams(vmem_limit_bytes=16 << 20),
        cost_estimate=pl.CostEstimate(
            flops=1700000000, bytes_accessed=9000000, transcendentals=0
        ),
        name="query_part",
    )(qg, wq)


def project_kernel(part, own, across, near1, near2, near3, cos, sin, wk, wv, out, grads):
    total = own[...].astype(f32) + across[...].astype(f32)
    for near in (near1, near2, near3):
        total += near[...].astype(f32)
    sign = half_sign((TOK, HEAD), 1)
    g = total[:, :HEAD] * SCALE
    key_grad = g * cos[...] - pltpu.roll(g * sin[...], HEAD // 2, 1) * sign
    grads[:HEAD, :] = key_grad.T.astype(bf16)
    grads[HEAD:, :] = total[:, HEAD:].T.astype(bf16)

    def step(i, carry):
        rows = pl.ds(pl.multiple_of(i * STEP_ROWS, STEP_ROWS), STEP_ROWS)
        weights = jnp.concatenate([wk[rows, :], wv[rows, :]], 1)
        result = jnp.dot(weights, grads[...], preferred_element_type=f32)
        out[rows, :] = (part[rows, :].astype(f32) + result).astype(bf16)
        return carry

    lax.fori_loop(0, WIDTH // STEP_ROWS, step, 0)


def project(part, own, across, near, cos, sin, wk, wv):
    return pl.pallas_call(
        project_kernel,
        out_shape=jax.ShapeDtypeStruct((WIDTH, TOK), bf16),
        in_specs=vmem(10),
        out_specs=vmem(1)[0],
        scratch_shapes=[pltpu.VMEM((2 * HEAD, TOK), bf16)],
        compiler_params=pltpu.CompilerParams(vmem_limit_bytes=16 << 20),
        cost_estimate=pl.CostEstimate(
            flops=700000000, bytes_accessed=6000000, transcendentals=0
        ),
        name="project",
    )(part, own, across, *near, cos, sin, wk, wv)


def last_kernel(parts, out):
    def step(i, carry):
        rows = pl.ds(pl.multiple_of(i * TILE, TILE), TILE)
        total = parts[0, rows, :].astype(f32)
        for k in range(1, 8):
            total += parts[k, rows, :].astype(f32)
        out[rows, :] = total.astype(bf16)
        return carry

    lax.fori_loop(0, 5, step, 0)


def last_sum(parts):
    return pl.pallas_call(
        last_kernel,
        out_shape=jax.ShapeDtypeStruct((640, TOK), bf16),
        in_specs=vmem(1),
        out_specs=vmem(1)[0],
        compiler_params=pltpu.CompilerParams(vmem_limit_bytes=16 << 20),
        cost_estimate=pl.CostEstimate(flops=1300000, bytes_accessed=3000000, transcendentals=0),
        name="last_sum",
    )(parts)


def local(
    query, key, value, att, grad, lse, block_mask, positions, segments, w_query, key_weight,
    value_weight,
):
    me = lax.axis_index(CTX)
    cos, sin, block = make_block(key, value, positions)

    across = swap_zh(block)
    joined = jnp.concatenate([query, grad, att], 1)
    joined, again = lax.optimization_barrier((joined, block))
    near = [shift_y(again, k) for k in (1, 2, 3)]
    across, joined = lax.optimization_barrier((across, joined))
    far = [shift_y(across, k) for k in (1, 2, 3)]
    q_rows, q_cols, g_rows, g_cols, delta = prep(joined, cos, sin)
    early = jnp.concatenate([block] + near + [across], 0)
    late = jnp.concatenate(far, 0)

    early_mine, early_other, late_mine, late_other, query_grad = attention(
        block_mask, me.reshape(1), segments.reshape(TILES, 1, TILE), lse, delta, cos, sin, q_rows,
        q_cols, g_rows, g_cols, early, swap_core(early), late, swap_core(late),
    )

    late = late_mine.astype(f32) + swap_core(late_other).astype(f32)
    early = early_mine.astype(f32) + swap_core(early_other).astype(f32)
    own, across = early[:TOK], early[4 * TOK :]
    parts = [early[k * TOK : (k + 1) * TOK].astype(bf16) for k in (1, 2, 3)]
    parts += [late[k * TOK : (k + 1) * TOK].astype(bf16) for k in range(3)]
    own, across, parts = lax.optimization_barrier((own, across, parts))
    far = [shift_y(parts[2 + k], -k) for k in (1, 2, 3)]
    near = [shift_y(parts[k - 1], -k) for k in (1, 2, 3)]
    across = across + sum(p.astype(f32) for p in far)
    across, query_grad = lax.optimization_barrier((across.astype(bf16), query_grad))
    across = swap_zh(across)
    part, near = lax.optimization_barrier((query_part(query_grad, w_query), near))
    send = project(part, own, across, near, cos, sin, key_weight, value_weight)
    return last_sum(lax.all_to_all(send.reshape(8, 640, TOK), TP, 0, 0))


def solution(mesh):
    fine = Mesh(mesh.devices.reshape(4, 2, 2, 4, 2), ("y", "zh", "core", "x", "zl"))
    in_specs = (
        P(CTX, TP),
        P(CTX, TP),
        P(CTX, TP),
        P(CTX, TP),
        P(CTX, TP),
        P(TP, CTX),
        P(),
        P(CTX),
        P(),
        P(None, TP),
        P(None, TP),
        P(None, TP),
    )
    return jax.shard_map(
        local, mesh=fine, in_specs=in_specs, out_specs=P(TP, CTX), check_vma=False
    )
```

```python
import numpy as np
import jax
import jax.numpy as jnp
from jax import lax
from jax.experimental import pallas as pl
from jax.experimental.pallas import tpu as pltpu
from jax.sharding import Mesh, PartitionSpec as P

HEAD = 128
TILE = 128
GROUPS = 5
TOK = 256
TILES = 32
ROWS = GROUPS * TILE
SCALE = HEAD**-0.5
ROPE_BASE = 1000000.0
LOG2E = 1.4426950408889634
CTX = ("y", "zh", "core")
TP = ("x", "zl")

f32 = jnp.float32
bf16 = jnp.bfloat16


def shift(x, axes, sizes, offs):
    perm = []
    for source in np.ndindex(*sizes):
        dest = tuple((a + o) % s for a, o, s in zip(source, offs, sizes))
        perm.append(
            (int(np.ravel_multi_index(source, sizes)), int(np.ravel_multi_index(dest, sizes)))
        )
    return lax.ppermute(x, axes, perm)


def shift_y(x, k):
    return shift(x, ("y",), (4,), (k % 4,))


def swap_zh(x):
    return shift(x, ("zh",), (2,), (1,))


def swap_core(x):
    return shift(x, ("core",), (2,), (1,))


INVERSE = np.power(np.float64(ROPE_BASE), -np.arange(HEAD // 2) * (2.0 / HEAD)).astype(np.float32)


def half_sign(shape, axis):
    return jnp.where(lax.broadcasted_iota(jnp.int32, shape, axis) < HEAD // 2, -1.0, 1.0).astype(f32)


def block_kernel(key, value, positions, inverse, cos, sin, block):
    sign = half_sign((TILE, HEAD), 1)
    low = lax.broadcasted_iota(jnp.int32, (TILE, HEAD), 1) < HEAD // 2
    places = [jnp.broadcast_to(positions[t].astype(f32), (TILE, TILE)).T for t in range(2)]
    angles = jnp.where(low, places[0], places[1]) * inverse[...]
    both_cos, both_sin = jnp.cos(angles), jnp.sin(angles)
    for t in range(2):
        tok = pl.ds(t * TILE, TILE)
        mine = low if t == 0 else jnp.logical_not(low)
        c = jnp.where(mine, both_cos, pltpu.roll(both_cos, HEAD // 2, 1))
        s = jnp.where(mine, both_sin, pltpu.roll(both_sin, HEAD // 2, 1))
        cos[tok, :] = c
        sin[tok, :] = s
        x = key[tok, :].astype(f32)
        block[tok, :HEAD] = (x * c + pltpu.roll(x, HEAD // 2, 1) * (s * sign)).astype(bf16)
        block[tok, HEAD:] = value[tok, :]


def prep_kernel(query, grad, att, cos, sin, q_rows, q_cols, g_rows, g_cols, delta):
    sign = half_sign((TILE, HEAD), 1)
    for t in range(2):
        tok = pl.ds(t * TILE, TILE)
        c, s = cos[tok, :], sin[tok, :] * sign
        for h in range(GROUPS):
            feat = pl.ds(h * HEAD, HEAD)
            lane = pl.ds(h * TILE, TILE)
            x = query[tok, feat].astype(f32)
            rot = (x * c + pltpu.roll(x, HEAD // 2, 1) * s).astype(bf16)
            q_rows[t, lane, :] = rot
            q_cols[t, :, lane] = rot.T
            g = grad[tok, feat]
            g_rows[t, lane, :] = g
            g_cols[t, :, lane] = g.T
            prod = g.astype(f32) * att[tok, feat].astype(f32)
            delta[t, :, lane] = jnp.sum(prod.T, axis=0, keepdims=True)


EARLY = 5


def attention_kernel(
    mask, info, seg, lse, delta, cos, sin, q_rows, q_cols, g_rows, g_cols,
    early_mine, early_other, late_mine, late_other,
    d_early_mine, d_early_other, d_late_mine, d_late_other, qg,
    kv, dkv, dq, lse_rows, lists, counts, flags,
):
    dq[...] = jnp.zeros_like(dq)
    for t in range(2):
        for h in range(GROUPS):
            row = lse[h : h + 1, t * TILE : (t + 1) * TILE]
            lse_rows[t, :, pl.ds(h * TILE, TILE)] = row * LOG2E
    me = info[0]
    q_tile = 2 * me
    groups = (
        (early_mine, d_early_mine, 0, 0, EARLY),
        (early_other, d_early_other, 1, 0, EARLY),
        (late_mine, d_late_mine, 0, EARLY, 8 - EARLY),
        (late_other, d_late_other, 1, EARLY, 8 - EARLY),
    )
    starts = (0, 2 * EARLY, 4 * EARLY, 4 * EARLY + 2 * (8 - EARLY))

    def needs(j, away, first_slot):
        slot = lax.shift_right_logical(j, 1) + first_slot
        back_y = (lax.shift_right_logical(me, 2) - slot) & 3
        back_zh = (me ^ (lax.shift_right_logical(slot, 1) & 2)) & 2
        tile = 2 * (4 * back_y + back_zh + ((me ^ away) & 1)) + (j & 1)
        return mask[q_tile, tile] > 0, mask[q_tile + 1, tile] > 0

    for t in range(2):
        lists[t, 0] = t
        counts[t] = 1
    kv[pl.ds(TILES * TILE, TILE), :] = jnp.zeros((TILE, 2 * HEAD), bf16)
    dkv[pl.ds(TILES * TILE, TILE), :] = jnp.zeros((TILE, 2 * HEAD), f32)
    for (source, dest, away, first_slot, slots), start in zip(groups, starts):

        def collect(j, carry):
            needed = needs(j, away, first_slot)
            flags[start + j] = jnp.where(needed[0] | needed[1], 1, 0)
            here = pl.ds(pl.multiple_of(j * TILE, TILE), TILE)
            there = pl.ds(pl.multiple_of((start + j) * TILE, TILE), TILE)

            @pl.when(needed[0] | needed[1])
            def _():
                kv[there, :] = source[here, :]
                dkv[there, :] = jnp.zeros((TILE, 2 * HEAD), f32)

            @pl.when(jnp.logical_not(needed[0] | needed[1]))
            def _():
                dest[here, :] = jnp.zeros((TILE, 2 * HEAD), bf16)

            for t in range(2):
                add = needed[t]
                if start == 0:
                    add = add & (j != t)

                @pl.when(add)
                def _():
                    count = counts[t]
                    lists[t, count] = start + j
                    counts[t] = count + 1

            return carry

        lax.fori_loop(0, 2 * slots, collect, 0)

    def two_tiles(t, first, second, allowed):
        ones = pl.ds(pl.multiple_of(first * TILE, TILE), TILE)
        twos = pl.ds(pl.multiple_of(second * TILE, TILE), TILE)
        keys = jnp.concatenate([kv[ones, :HEAD], kv[twos, :HEAD]], 0)
        vals = jnp.concatenate([kv[ones, HEAD:], kv[twos, HEAD:]], 0)
        scores = jnp.dot(keys, q_cols[t], preferred_element_type=f32)
        probs = jnp.exp2(scores * (SCALE * LOG2E) - lse_rows[t])
        if allowed is not None:
            probs = jnp.concatenate([jnp.where(allowed, probs[:TILE], 0.0), probs[TILE:]], 0)
        dprobs = jnp.dot(vals, g_cols[t], preferred_element_type=f32)
        dscore = (probs * (dprobs - delta[t])).astype(bf16)
        probs = probs.astype(bf16)
        dkeys = jnp.dot(dscore, q_rows[t], preferred_element_type=f32)
        dvals = jnp.dot(probs, g_rows[t], preferred_element_type=f32)
        dqs = jnp.dot(keys.T, dscore, preferred_element_type=f32)
        return t, ones, twos, dkeys, dvals, dqs

    def add(t, ones, twos, dkeys, dvals, dqs):
        dq[t] += dqs
        dkv[ones, :HEAD] += dkeys[:TILE]
        dkv[ones, HEAD:] += dvals[:TILE]
        dkv[twos, :HEAD] += dkeys[TILE:]
        dkv[twos, HEAD:] += dvals[TILE:]

    most = jnp.maximum(counts[0], counts[1])

    def fill(i, carry):
        for t in range(2):

            @pl.when(i >= counts[t])
            def _():
                lists[t, i] = TILES

        return carry

    lax.fori_loop(jnp.minimum(counts[0], counts[1]), most + 1, fill, 0)
    causal = lax.broadcasted_iota(jnp.int32, (TILE, TILE), 0) <= (
        lax.broadcasted_iota(jnp.int32, (TILE, TILE), 1)
    )
    terms = []
    for t in range(2):
        row = jnp.broadcast_to(seg[q_tile + t], (TILE, TILE)).astype(f32)
        listed = jnp.where(mask[q_tile + t, q_tile + t] > 0, 1.0, 0.0)
        one = jnp.where((row.T == row) & causal, 1.0, 0.0) * listed
        terms.append(two_tiles(t, t, lists[t, 1], jnp.concatenate([one] * GROUPS, 1) > 0.5))
    for term in terms:
        add(*term)

    def rest(i, carry):
        terms = [two_tiles(t, lists[t, 2 * i], lists[t, 2 * i + 1], None) for t in range(2)]
        for term in terms:
            add(*term)
        return carry

    lax.fori_loop(1, lax.shift_right_logical(most + 1, 1), rest, 0)

    for (source, dest, away, first_slot, slots), start in zip(groups, starts):

        def give(j, carry):
            @pl.when(flags[start + j] > 0)
            def _():
                here = pl.ds(pl.multiple_of(j * TILE, TILE), TILE)
                there = pl.ds(pl.multiple_of((start + j) * TILE, TILE), TILE)
                dest[here, :] = dkv[there, :].astype(bf16)

            return carry

        lax.fori_loop(0, 2 * slots, give, 0)

    for t in range(2):
        tok = pl.ds(t * TILE, TILE)
        c, s = cos[tok, :].T, sin[tok, :].T
        for h in range(GROUPS):
            g = dq[t, :, pl.ds(h * TILE, TILE)]
            u = g * s
            half = HEAD // 2
            turned = jnp.concatenate([u[half:], -u[:half]], 0)
            qg[pl.ds(h * HEAD, HEAD), tok] = (g * c + turned).astype(bf16)


def vmem(n):
    return [pl.BlockSpec(memory_space=pltpu.VMEM)] * n


def prep(query, grad, att, cos, sin):
    s = jax.ShapeDtypeStruct
    return pl.pallas_call(
        prep_kernel,
        out_shape=(
            s((2, ROWS, HEAD), bf16),
            s((2, HEAD, ROWS), bf16),
            s((2, ROWS, HEAD), bf16),
            s((2, HEAD, ROWS), bf16),
            s((2, 1, ROWS), f32),
        ),
        in_specs=vmem(5),
        out_specs=tuple(vmem(5)),
        compiler_params=pltpu.CompilerParams(vmem_limit_bytes=12 << 20),
        cost_estimate=pl.CostEstimate(flops=1000000, bytes_accessed=10000, transcendentals=0),
        name="prep",
    )(query, grad, att, cos, sin)


def attention(mask, info, *operands):
    s = jax.ShapeDtypeStruct
    early, late = (s((n * TOK, 2 * HEAD), bf16) for n in (EARLY, 8 - EARLY))
    return pl.pallas_call(
        attention_kernel,
        out_shape=(early, early, late, late, s((ROWS, TOK), bf16)),
        in_specs=[pl.BlockSpec(memory_space=pltpu.SMEM)] * 2 + vmem(len(operands)),
        out_specs=tuple(vmem(5)),
        scratch_shapes=[
            pltpu.VMEM(((TILES + 1) * TILE, 2 * HEAD), bf16),
            pltpu.VMEM(((TILES + 1) * TILE, 2 * HEAD), f32),
            pltpu.VMEM((2, HEAD, ROWS), f32),
            pltpu.VMEM((2, 1, ROWS), f32),
            pltpu.SMEM((2, TILES + 1), jnp.int32),
            pltpu.SMEM((2,), jnp.int32),
            pltpu.SMEM((TILES,), jnp.int32),
        ],
        compiler_params=pltpu.CompilerParams(vmem_limit_bytes=16 << 20),
        cost_estimate=pl.CostEstimate(
            flops=2000000000, bytes_accessed=8000000, transcendentals=1000000
        ),
        name="attention",
    )(mask, info, *operands)


def make_block(key, value, positions):
    s = jax.ShapeDtypeStruct
    inverse = jnp.asarray(np.concatenate([INVERSE, INVERSE])[None, :])
    return pl.pallas_call(
        block_kernel,
        out_shape=(s((TOK, HEAD), f32), s((TOK, HEAD), f32), s((TOK, 2 * HEAD), bf16)),
        in_specs=vmem(4),
        out_specs=tuple(vmem(3)),
        cost_estimate=pl.CostEstimate(flops=5000000, bytes_accessed=700000, transcendentals=60000),
        name="block",
    )(key, value, positions.reshape(2, 1, TILE), inverse)


WIDTH = 5120
STEP_ROWS = 640


def query_part_kernel(qg, wq, out):
    def step(i, carry):
        rows = pl.ds(pl.multiple_of(i * STEP_ROWS, STEP_ROWS), STEP_ROWS)
        out[rows, :] = jnp.dot(wq[rows, :], qg[...], preferred_element_type=f32).astype(bf16)
        return carry

    lax.fori_loop(0, WIDTH // STEP_ROWS, step, 0)


def query_part(qg, wq):
    return pl.pallas_call(
        query_part_kernel,
        out_shape=jax.ShapeDtypeStruct((WIDTH, TOK), bf16),
        in_specs=vmem(2),
        out_specs=vmem(1)[0],
        compiler_params=pltpu.CompilerParams(vmem_limit_bytes=16 << 20),
        cost_estimate=pl.CostEstimate(
            flops=1700000000, bytes_accessed=9000000, transcendentals=0
        ),
        name="query_part",
    )(qg, wq)


def project_kernel(part, own, across, near1, near2, near3, cos, sin, wk, wv, out, grads):
    total = own[...].astype(f32) + across[...].astype(f32)
    for near in (near1, near2, near3):
        total += near[...].astype(f32)
    sign = half_sign((TOK, HEAD), 1)
    g = total[:, :HEAD] * SCALE
    key_grad = g * cos[...] - pltpu.roll(g * sin[...], HEAD // 2, 1) * sign
    grads[:HEAD, :] = key_grad.T.astype(bf16)
    grads[HEAD:, :] = total[:, HEAD:].T.astype(bf16)

    def step(i, carry):
        rows = pl.ds(pl.multiple_of(i * STEP_ROWS, STEP_ROWS), STEP_ROWS)
        weights = jnp.concatenate([wk[rows, :], wv[rows, :]], 1)
        result = jnp.dot(weights, grads[...], preferred_element_type=f32)
        out[rows, :] = (part[rows, :].astype(f32) + result).astype(bf16)
        return carry

    lax.fori_loop(0, WIDTH // STEP_ROWS, step, 0)


def project(part, own, across, near, cos, sin, wk, wv):
    return pl.pallas_call(
        project_kernel,
        out_shape=jax.ShapeDtypeStruct((WIDTH, TOK), bf16),
        in_specs=vmem(10),
        out_specs=vmem(1)[0],
        scratch_shapes=[pltpu.VMEM((2 * HEAD, TOK), bf16)],
        compiler_params=pltpu.CompilerParams(vmem_limit_bytes=16 << 20),
        cost_estimate=pl.CostEstimate(
            flops=700000000, bytes_accessed=6000000, transcendentals=0
        ),
        name="project",
    )(part, own, across, *near, cos, sin, wk, wv)


def last_kernel(parts, out):
    def step(i, carry):
        rows = pl.ds(pl.multiple_of(i * TILE, TILE), TILE)
        total = parts[0, rows, :].astype(f32)
        for k in range(1, 8):
            total += parts[k, rows, :].astype(f32)
        out[rows, :] = total.astype(bf16)
        return carry

    lax.fori_loop(0, 5, step, 0)


def last_sum(parts):
    return pl.pallas_call(
        last_kernel,
        out_shape=jax.ShapeDtypeStruct((640, TOK), bf16),
        in_specs=vmem(1),
        out_specs=vmem(1)[0],
        compiler_params=pltpu.CompilerParams(vmem_limit_bytes=16 << 20),
        cost_estimate=pl.CostEstimate(flops=1300000, bytes_accessed=3000000, transcendentals=0),
        name="last_sum",
    )(parts)


def local(
    query, key, value, att, grad, lse, block_mask, positions, segments, w_query, key_weight,
    value_weight,
):
    me = lax.axis_index(CTX)
    cos, sin, block = make_block(key, value, positions)

    across = swap_zh(block)
    scaled, again = lax.optimization_barrier(((cos * SCALE, sin * SCALE), block))
    near = [shift_y(again, k) for k in (1, 2, 3)]
    across, query, grad, att = lax.optimization_barrier((across, query, grad, att))
    far = [shift_y(across, k) for k in (1, 2, 3)]
    q_rows, q_cols, g_rows, g_cols, delta = prep(query, grad, att, cos, sin)
    early = jnp.concatenate([block] + near + [across], 0)
    late = jnp.concatenate(far, 0)

    early_mine, early_other, late_mine, late_other, query_grad = attention(
        block_mask, me.reshape(1), segments.reshape(TILES, 1, TILE), lse, delta, *scaled, q_rows,
        q_cols, g_rows, g_cols, early, swap_core(early), late, swap_core(late),
    )

    late = late_mine.astype(f32) + swap_core(late_other).astype(f32)
    early = early_mine.astype(f32) + swap_core(early_other).astype(f32)
    own, across = early[:TOK], early[4 * TOK :]
    parts = [early[k * TOK : (k + 1) * TOK].astype(bf16) for k in (1, 2, 3)]
    parts += [late[k * TOK : (k + 1) * TOK].astype(bf16) for k in range(3)]
    own, across, parts = lax.optimization_barrier((own, across, parts))
    far = [shift_y(parts[2 + k], -k) for k in (1, 2, 3)]
    near = [shift_y(parts[k - 1], -k) for k in (1, 2, 3)]
    across = across + sum(p.astype(f32) for p in far)
    across, query_grad = lax.optimization_barrier((across.astype(bf16), query_grad))
    across = swap_zh(across)
    part, near = lax.optimization_barrier((query_part(query_grad, w_query), near))
    send = project(part, own, across, near, cos, sin, key_weight, value_weight)
    return last_sum(lax.all_to_all(send.reshape(8, 640, TOK), TP, 0, 0))


def solution(mesh):
    fine = Mesh(mesh.devices.reshape(4, 2, 2, 4, 2), ("y", "zh", "core", "x", "zl"))
    in_specs = (
        P(CTX, TP),
        P(CTX, TP),
        P(CTX, TP),
        P(CTX, TP),
        P(CTX, TP),
        P(TP, CTX),
        P(),
        P(CTX),
        P(),
        P(None, TP),
        P(None, TP),
        P(None, TP),
    )
    return jax.shard_map(
        local, mesh=fine, in_specs=in_specs, out_specs=P(TP, CTX), check_vma=False
    )
```

```python
import numpy as np
import jax
import jax.numpy as jnp
from jax import lax
from jax.experimental import pallas as pl
from jax.experimental.pallas import tpu as pltpu
from jax.sharding import Mesh, PartitionSpec as P

HEAD = 128
TILE = 128
GROUPS = 5
TOK = 256
TILES = 32
ROWS = GROUPS * TILE
SCALE = HEAD**-0.5
ROPE_BASE = 1000000.0
LOG2E = 1.4426950408889634
CTX = ("y", "zh", "core")
TP = ("x", "zl")

f32 = jnp.float32
bf16 = jnp.bfloat16


def shift(x, axes, sizes, offs):
    perm = []
    for source in np.ndindex(*sizes):
        dest = tuple((a + o) % s for a, o, s in zip(source, offs, sizes))
        perm.append(
            (int(np.ravel_multi_index(source, sizes)), int(np.ravel_multi_index(dest, sizes)))
        )
    return lax.ppermute(x, axes, perm)


def shift_y(x, k):
    return shift(x, ("y",), (4,), (k % 4,))


def swap_zh(x):
    return shift(x, ("zh",), (2,), (1,))


def swap_core(x):
    return shift(x, ("core",), (2,), (1,))


INVERSE = np.power(np.float64(ROPE_BASE), -np.arange(HEAD // 2) * (2.0 / HEAD)).astype(np.float32)


def half_sign(shape, axis):
    return jnp.where(lax.broadcasted_iota(jnp.int32, shape, axis) < HEAD // 2, -1.0, 1.0).astype(f32)


def block_kernel(key, value, positions, inverse, cos, sin, block):
    sign = half_sign((TILE, HEAD), 1)
    low = lax.broadcasted_iota(jnp.int32, (TILE, HEAD), 1) < HEAD // 2
    places = [jnp.broadcast_to(positions[t].astype(f32), (TILE, TILE)).T for t in range(2)]
    angles = jnp.where(low, places[0], places[1]) * inverse[...]
    both_cos, both_sin = jnp.cos(angles), jnp.sin(angles)
    for t in range(2):
        tok = pl.ds(t * TILE, TILE)
        mine = low if t == 0 else jnp.logical_not(low)
        c = jnp.where(mine, both_cos, pltpu.roll(both_cos, HEAD // 2, 1))
        s = jnp.where(mine, both_sin, pltpu.roll(both_sin, HEAD // 2, 1))
        cos[tok, :] = c
        sin[tok, :] = s
        x = key[tok, :].astype(f32)
        block[tok, :HEAD] = (x * c + pltpu.roll(x, HEAD // 2, 1) * (s * sign)).astype(bf16)
        block[tok, HEAD:] = value[tok, :]


def prep_kernel(query, grad, att, cos, sin, small, q_rows, q_cols, g_rows, g_cols, delta):
    sign = half_sign((TILE, HEAD), 1)
    for t in range(2):
        tok = pl.ds(t * TILE, TILE)
        c, s = cos[tok, :], sin[tok, :] * sign
        for h in range(GROUPS):
            feat = pl.ds(h * HEAD, HEAD)
            lane = pl.ds(h * TILE, TILE)
            x = query[tok, feat].astype(f32)
            rot = (x * c + pltpu.roll(x, HEAD // 2, 1) * s).astype(bf16)
            q_rows[t, lane, :] = rot
            q_cols[t, :, lane] = rot.T
            g = grad[tok, feat]
            g_rows[t, lane, :] = g
            g_cols[t, :, lane] = g.T
            prod = g.astype(f32) * att[tok, feat].astype(f32)
            delta[t, :, lane] = jnp.sum(prod.T, axis=0, keepdims=True)


EARLY = 5


def attention_kernel(
    mask, info, seg, lse, delta, cos, sin, q_rows, q_cols, g_rows, g_cols,
    early_mine, early_other, late_mine, late_other,
    d_early_mine, d_early_other, d_late_mine, d_late_other, qg,
    kv, dkv, dq, lse_rows, lists, counts, flags,
):
    dq[...] = jnp.zeros_like(dq)
    for t in range(2):
        for h in range(GROUPS):
            row = lse[h : h + 1, t * TILE : (t + 1) * TILE]
            lse_rows[t, :, pl.ds(h * TILE, TILE)] = row * LOG2E
    me = info[0]
    q_tile = 2 * me
    groups = (
        (early_mine, d_early_mine, 0, 0, EARLY),
        (early_other, d_early_other, 1, 0, EARLY),
        (late_mine, d_late_mine, 0, EARLY, 8 - EARLY),
        (late_other, d_late_other, 1, EARLY, 8 - EARLY),
    )
    starts = (0, 2 * EARLY, 4 * EARLY, 4 * EARLY + 2 * (8 - EARLY))

    def needs(j, away, first_slot):
        slot = lax.shift_right_logical(j, 1) + first_slot
        back_y = (lax.shift_right_logical(me, 2) - slot) & 3
        back_zh = (me ^ (lax.shift_right_logical(slot, 1) & 2)) & 2
        tile = 2 * (4 * back_y + back_zh + ((me ^ away) & 1)) + (j & 1)
        return mask[q_tile, tile] > 0, mask[q_tile + 1, tile] > 0

    for t in range(2):
        lists[t, 0] = t
        counts[t] = 1
    kv[pl.ds(TILES * TILE, TILE), :] = jnp.zeros((TILE, 2 * HEAD), bf16)
    dkv[pl.ds(TILES * TILE, TILE), :] = jnp.zeros((TILE, 2 * HEAD), f32)
    for (source, dest, away, first_slot, slots), start in zip(groups, starts):

        def collect(j, carry):
            needed = needs(j, away, first_slot)
            flags[start + j] = jnp.where(needed[0] | needed[1], 1, 0)
            here = pl.ds(pl.multiple_of(j * TILE, TILE), TILE)
            there = pl.ds(pl.multiple_of((start + j) * TILE, TILE), TILE)

            @pl.when(needed[0] | needed[1])
            def _():
                kv[there, :] = source[here, :]
                dkv[there, :] = jnp.zeros((TILE, 2 * HEAD), f32)

            @pl.when(jnp.logical_not(needed[0] | needed[1]))
            def _():
                dest[here, :] = jnp.zeros((TILE, 2 * HEAD), bf16)

            for t in range(2):
                add = needed[t]
                if start == 0:
                    add = add & (j != t)

                @pl.when(add)
                def _():
                    count = counts[t]
                    lists[t, count] = start + j
                    counts[t] = count + 1

            return carry

        lax.fori_loop(0, 2 * slots, collect, 0)

    def two_tiles(t, first, second, allowed):
        ones = pl.ds(pl.multiple_of(first * TILE, TILE), TILE)
        twos = pl.ds(pl.multiple_of(second * TILE, TILE), TILE)
        keys = jnp.concatenate([kv[ones, :HEAD], kv[twos, :HEAD]], 0)
        vals = jnp.concatenate([kv[ones, HEAD:], kv[twos, HEAD:]], 0)
        scores = jnp.dot(keys, q_cols[t], preferred_element_type=f32)
        probs = jnp.exp2(scores * (SCALE * LOG2E) - lse_rows[t])
        if allowed is not None:
            probs = jnp.concatenate([jnp.where(allowed, probs[:TILE], 0.0), probs[TILE:]], 0)
        dprobs = jnp.dot(vals, g_cols[t], preferred_element_type=f32)
        dscore = (probs * (dprobs - delta[t])).astype(bf16)
        probs = probs.astype(bf16)
        dkeys = jnp.dot(dscore, q_rows[t], preferred_element_type=f32)
        dvals = jnp.dot(probs, g_rows[t], preferred_element_type=f32)
        dqs = jnp.dot(keys.T, dscore, preferred_element_type=f32)
        return t, ones, twos, dkeys, dvals, dqs

    def add(t, ones, twos, dkeys, dvals, dqs):
        dq[t] += dqs
        dkv[ones, :HEAD] += dkeys[:TILE]
        dkv[ones, HEAD:] += dvals[:TILE]
        dkv[twos, :HEAD] += dkeys[TILE:]
        dkv[twos, HEAD:] += dvals[TILE:]

    most = jnp.maximum(counts[0], counts[1])

    def fill(i, carry):
        for t in range(2):

            @pl.when(i >= counts[t])
            def _():
                lists[t, i] = TILES

        return carry

    lax.fori_loop(jnp.minimum(counts[0], counts[1]), most + 1, fill, 0)
    causal = lax.broadcasted_iota(jnp.int32, (TILE, TILE), 0) <= (
        lax.broadcasted_iota(jnp.int32, (TILE, TILE), 1)
    )
    terms = []
    for t in range(2):
        row = jnp.broadcast_to(seg[q_tile + t], (TILE, TILE)).astype(f32)
        listed = jnp.where(mask[q_tile + t, q_tile + t] > 0, 1.0, 0.0)
        one = jnp.where((row.T == row) & causal, 1.0, 0.0) * listed
        terms.append(two_tiles(t, t, lists[t, 1], jnp.concatenate([one] * GROUPS, 1) > 0.5))
    for term in terms:
        add(*term)

    def rest(i, carry):
        terms = [two_tiles(t, lists[t, 2 * i], lists[t, 2 * i + 1], None) for t in range(2)]
        for term in terms:
            add(*term)
        return carry

    lax.fori_loop(1, lax.shift_right_logical(most + 1, 1), rest, 0)

    for (source, dest, away, first_slot, slots), start in zip(groups, starts):

        def give(j, carry):
            @pl.when(flags[start + j] > 0)
            def _():
                here = pl.ds(pl.multiple_of(j * TILE, TILE), TILE)
                there = pl.ds(pl.multiple_of((start + j) * TILE, TILE), TILE)
                dest[here, :] = dkv[there, :].astype(bf16)

            return carry

        lax.fori_loop(0, 2 * slots, give, 0)

    for t in range(2):
        tok = pl.ds(t * TILE, TILE)
        c, s = cos[tok, :].T, sin[tok, :].T
        for h in range(GROUPS):
            g = dq[t, :, pl.ds(h * TILE, TILE)] * SCALE
            u = g * s
            half = HEAD // 2
            turned = jnp.concatenate([u[half:], -u[:half]], 0)
            qg[pl.ds(h * HEAD, HEAD), tok] = (g * c + turned).astype(bf16)


def vmem(n):
    return [pl.BlockSpec(memory_space=pltpu.VMEM)] * n


def prep(query, grad, att, cos, sin, small):
    s = jax.ShapeDtypeStruct
    return pl.pallas_call(
        prep_kernel,
        out_shape=(
            s((2, ROWS, HEAD), bf16),
            s((2, HEAD, ROWS), bf16),
            s((2, ROWS, HEAD), bf16),
            s((2, HEAD, ROWS), bf16),
            s((2, 1, ROWS), f32),
        ),
        in_specs=vmem(6),
        out_specs=tuple(vmem(5)),
        compiler_params=pltpu.CompilerParams(vmem_limit_bytes=12 << 20),
        cost_estimate=pl.CostEstimate(flops=1000000, bytes_accessed=10000, transcendentals=0),
        name="prep",
    )(query, grad, att, cos, sin, small)


def attention(mask, info, *operands):
    s = jax.ShapeDtypeStruct
    early, late = (s((n * TOK, 2 * HEAD), bf16) for n in (EARLY, 8 - EARLY))
    return pl.pallas_call(
        attention_kernel,
        out_shape=(early, early, late, late, s((ROWS, TOK), bf16)),
        in_specs=[pl.BlockSpec(memory_space=pltpu.SMEM)] * 2 + vmem(len(operands)),
        out_specs=tuple(vmem(5)),
        scratch_shapes=[
            pltpu.VMEM(((TILES + 1) * TILE, 2 * HEAD), bf16),
            pltpu.VMEM(((TILES + 1) * TILE, 2 * HEAD), f32),
            pltpu.VMEM((2, HEAD, ROWS), f32),
            pltpu.VMEM((2, 1, ROWS), f32),
            pltpu.SMEM((2, TILES + 1), jnp.int32),
            pltpu.SMEM((2,), jnp.int32),
            pltpu.SMEM((TILES,), jnp.int32),
        ],
        compiler_params=pltpu.CompilerParams(vmem_limit_bytes=16 << 20),
        cost_estimate=pl.CostEstimate(
            flops=2000000000, bytes_accessed=8000000, transcendentals=1000000
        ),
        name="attention",
    )(mask, info, *operands)


def make_block(key, value, positions):
    s = jax.ShapeDtypeStruct
    inverse = jnp.asarray(np.concatenate([INVERSE, INVERSE])[None, :])
    return pl.pallas_call(
        block_kernel,
        out_shape=(s((TOK, HEAD), f32), s((TOK, HEAD), f32), s((TOK, 2 * HEAD), bf16)),
        in_specs=vmem(4),
        out_specs=tuple(vmem(3)),
        cost_estimate=pl.CostEstimate(flops=5000000, bytes_accessed=700000, transcendentals=60000),
        name="block",
    )(key, value, positions.reshape(2, 1, TILE), inverse)


WIDTH = 5120
STEP_ROWS = 640


def query_part_kernel(qg, wq, out):
    def step(i, carry):
        rows = pl.ds(pl.multiple_of(i * STEP_ROWS, STEP_ROWS), STEP_ROWS)
        out[rows, :] = jnp.dot(wq[rows, :], qg[...], preferred_element_type=f32).astype(bf16)
        return carry

    lax.fori_loop(0, WIDTH // STEP_ROWS, step, 0)


def query_part(qg, wq):
    return pl.pallas_call(
        query_part_kernel,
        out_shape=jax.ShapeDtypeStruct((WIDTH, TOK), bf16),
        in_specs=vmem(2),
        out_specs=vmem(1)[0],
        compiler_params=pltpu.CompilerParams(vmem_limit_bytes=16 << 20),
        cost_estimate=pl.CostEstimate(
            flops=1700000000, bytes_accessed=9000000, transcendentals=0
        ),
        name="query_part",
    )(qg, wq)


def project_kernel(part, own, across, near1, near2, near3, cos, sin, wk, wv, out, grads):
    total = own[...].astype(f32) + across[...].astype(f32)
    for near in (near1, near2, near3):
        total += near[...].astype(f32)
    sign = half_sign((TOK, HEAD), 1)
    g = total[:, :HEAD] * SCALE
    key_grad = g * cos[...] - pltpu.roll(g * sin[...], HEAD // 2, 1) * sign
    grads[:HEAD, :] = key_grad.T.astype(bf16)
    grads[HEAD:, :] = total[:, HEAD:].T.astype(bf16)

    def step(i, carry):
        rows = pl.ds(pl.multiple_of(i * STEP_ROWS, STEP_ROWS), STEP_ROWS)
        weights = jnp.concatenate([wk[rows, :], wv[rows, :]], 1)
        result = jnp.dot(weights, grads[...], preferred_element_type=f32)
        out[rows, :] = (part[rows, :].astype(f32) + result).astype(bf16)
        return carry

    lax.fori_loop(0, WIDTH // STEP_ROWS, step, 0)


def project(part, own, across, near, cos, sin, wk, wv):
    return pl.pallas_call(
        project_kernel,
        out_shape=jax.ShapeDtypeStruct((WIDTH, TOK), bf16),
        in_specs=vmem(10),
        out_specs=vmem(1)[0],
        scratch_shapes=[pltpu.VMEM((2 * HEAD, TOK), bf16)],
        compiler_params=pltpu.CompilerParams(vmem_limit_bytes=16 << 20),
        cost_estimate=pl.CostEstimate(
            flops=700000000, bytes_accessed=6000000, transcendentals=0
        ),
        name="project",
    )(part, own, across, *near, cos, sin, wk, wv)


def last_kernel(parts, out):
    def step(i, carry):
        rows = pl.ds(pl.multiple_of(i * TILE, TILE), TILE)
        total = parts[0, rows, :].astype(f32)
        for k in range(1, 8):
            total += parts[k, rows, :].astype(f32)
        out[rows, :] = total.astype(bf16)
        return carry

    lax.fori_loop(0, 5, step, 0)


def last_sum(parts):
    return pl.pallas_call(
        last_kernel,
        out_shape=jax.ShapeDtypeStruct((640, TOK), bf16),
        in_specs=vmem(1),
        out_specs=vmem(1)[0],
        compiler_params=pltpu.CompilerParams(vmem_limit_bytes=16 << 20),
        cost_estimate=pl.CostEstimate(flops=1300000, bytes_accessed=3000000, transcendentals=0),
        name="last_sum",
    )(parts)


def local(
    query, key, value, att, grad, lse, block_mask, positions, segments, w_query, key_weight,
    value_weight,
):
    me = lax.axis_index(CTX)
    cos, sin, block = make_block(key, value, positions)

    across = swap_zh(block)
    small, again = lax.optimization_barrier((cos[:8] * SCALE, block))
    near = [shift_y(again, k) for k in (1, 2, 3)]
    across, query, grad, att = lax.optimization_barrier((across, query, grad, att))
    far = [shift_y(across, k) for k in (1, 2, 3)]
    q_rows, q_cols, g_rows, g_cols, delta = prep(query, grad, att, cos, sin, small)
    early = jnp.concatenate([block] + near + [across], 0)
    late = jnp.concatenate(far, 0)

    early_mine, early_other, late_mine, late_other, query_grad = attention(
        block_mask, me.reshape(1), segments.reshape(TILES, 1, TILE), lse, delta, cos, sin, q_rows,
        q_cols, g_rows, g_cols, early, swap_core(early), late, swap_core(late),
    )

    late = late_mine.astype(f32) + swap_core(late_other).astype(f32)
    early = early_mine.astype(f32) + swap_core(early_other).astype(f32)
    own, across = early[:TOK], early[4 * TOK :]
    parts = [early[k * TOK : (k + 1) * TOK].astype(bf16) for k in (1, 2, 3)]
    parts += [late[k * TOK : (k + 1) * TOK].astype(bf16) for k in range(3)]
    own, across, parts = lax.optimization_barrier((own, across, parts))
    far = [shift_y(parts[2 + k], -k) for k in (1, 2, 3)]
    near = [shift_y(parts[k - 1], -k) for k in (1, 2, 3)]
    across = across + sum(p.astype(f32) for p in far)
    across, query_grad = lax.optimization_barrier((across.astype(bf16), query_grad))
    across = swap_zh(across)
    part, near = lax.optimization_barrier((query_part(query_grad, w_query), near))
    send = project(part, own, across, near, cos, sin, key_weight, value_weight)
    return last_sum(lax.all_to_all(send.reshape(8, 640, TOK), TP, 0, 0))


def solution(mesh):
    fine = Mesh(mesh.devices.reshape(4, 2, 2, 4, 2), ("y", "zh", "core", "x", "zl"))
    in_specs = (
        P(CTX, TP),
        P(CTX, TP),
        P(CTX, TP),
        P(CTX, TP),
        P(CTX, TP),
        P(TP, CTX),
        P(),
        P(CTX),
        P(),
        P(None, TP),
        P(None, TP),
        P(None, TP),
    )
    return jax.shard_map(
        local, mesh=fine, in_specs=in_specs, out_specs=P(TP, CTX), check_vma=False
    )
```

```python
import numpy as np
import jax
import jax.numpy as jnp
from jax import lax
from jax.experimental import pallas as pl
from jax.experimental.pallas import tpu as pltpu
from jax.sharding import Mesh, PartitionSpec as P

HEAD = 128
TILE = 128
GROUPS = 5
TOK = 256
TILES = 32
ROWS = GROUPS * TILE
SCALE = HEAD**-0.5
ROPE_BASE = 1000000.0
LOG2E = 1.4426950408889634
CTX = ("y", "zh", "core")
TP = ("x", "zl")

f32 = jnp.float32
bf16 = jnp.bfloat16


def shift(x, axes, sizes, offs):
    perm = []
    for source in np.ndindex(*sizes):
        dest = tuple((a + o) % s for a, o, s in zip(source, offs, sizes))
        perm.append(
            (int(np.ravel_multi_index(source, sizes)), int(np.ravel_multi_index(dest, sizes)))
        )
    return lax.ppermute(x, axes, perm)


def shift_y(x, k):
    return shift(x, ("y",), (4,), (k % 4,))


def swap_zh(x):
    return shift(x, ("zh",), (2,), (1,))


def swap_core(x):
    return shift(x, ("core",), (2,), (1,))


INVERSE = np.power(np.float64(ROPE_BASE), -np.arange(HEAD // 2) * (2.0 / HEAD)).astype(np.float32)


def half_sign(shape, axis):
    return jnp.where(lax.broadcasted_iota(jnp.int32, shape, axis) < HEAD // 2, -1.0, 1.0).astype(f32)


def block_kernel(key, value, positions, inverse, cos, sin, block):
    sign = half_sign((TILE, HEAD), 1)
    low = lax.broadcasted_iota(jnp.int32, (TILE, HEAD), 1) < HEAD // 2
    places = [jnp.broadcast_to(positions[t].astype(f32), (TILE, TILE)).T for t in range(2)]
    angles = jnp.where(low, places[0], places[1]) * inverse[...]
    both_cos, both_sin = jnp.cos(angles), jnp.sin(angles)
    for t in range(2):
        tok = pl.ds(t * TILE, TILE)
        mine = low if t == 0 else jnp.logical_not(low)
        c = jnp.where(mine, both_cos, pltpu.roll(both_cos, HEAD // 2, 1))
        s = jnp.where(mine, both_sin, pltpu.roll(both_sin, HEAD // 2, 1))
        cos[tok, :] = c
        sin[tok, :] = s
        x = key[tok, :].astype(f32)
        block[tok, :HEAD] = (x * c + pltpu.roll(x, HEAD // 2, 1) * (s * sign)).astype(bf16)
        block[tok, HEAD:] = value[tok, :]


def prep_kernel(query, grad, att, cos, sin, small, q_rows, q_cols, g_rows, g_cols, delta):
    sign = half_sign((TILE, HEAD), 1)
    for t in range(2):
        tok = pl.ds(t * TILE, TILE)
        c, s = cos[tok, :], sin[tok, :] * sign
        for h in range(GROUPS):
            feat = pl.ds(h * HEAD, HEAD)
            lane = pl.ds(h * TILE, TILE)
            x = query[tok, feat].astype(f32)
            rot = (x * c + pltpu.roll(x, HEAD // 2, 1) * s).astype(bf16)
            q_rows[t, lane, :] = rot
            q_cols[t, :, lane] = rot.T
            g = grad[tok, feat]
            g_rows[t, lane, :] = g
            g_cols[t, :, lane] = g.T
            prod = g.astype(f32) * att[tok, feat].astype(f32)
            delta[t, :, lane] = jnp.sum(prod.T, axis=0, keepdims=True)


EARLY = 5


def attention_kernel(
    mask, info, seg, lse, delta, cos, sin, q_rows, q_cols, g_rows, g_cols,
    early_mine, early_other, late_mine, late_other,
    d_early_mine, d_early_other, d_late_mine, d_late_other, qg,
    kv, dkv, dq, lse_rows, lists, counts, flags,
):
    dq[...] = jnp.zeros_like(dq)
    for t in range(2):
        for h in range(GROUPS):
            row = lse[h : h + 1, t * TILE : (t + 1) * TILE]
            lse_rows[t, :, pl.ds(h * TILE, TILE)] = row * LOG2E
    me = info[0]
    q_tile = 2 * me
    groups = (
        (early_mine, d_early_mine, 0, 0, EARLY),
        (early_other, d_early_other, 1, 0, EARLY),
        (late_mine, d_late_mine, 0, EARLY, 8 - EARLY),
        (late_other, d_late_other, 1, EARLY, 8 - EARLY),
    )
    starts = (0, 2 * EARLY, 4 * EARLY, 4 * EARLY + 2 * (8 - EARLY))

    def needs(j, away, first_slot):
        slot = lax.shift_right_logical(j, 1) + first_slot
        back_y = (lax.shift_right_logical(me, 2) - slot) & 3
        back_zh = (me ^ (lax.shift_right_logical(slot, 1) & 2)) & 2
        tile = 2 * (4 * back_y + back_zh + ((me ^ away) & 1)) + (j & 1)
        return mask[q_tile, tile] > 0, mask[q_tile + 1, tile] > 0

    for t in range(2):
        lists[t, 0] = t
        counts[t] = 1
    kv[pl.ds(TILES * TILE, TILE), :] = jnp.zeros((TILE, 2 * HEAD), bf16)
    dkv[pl.ds(TILES * TILE, TILE), :] = jnp.zeros((TILE, 2 * HEAD), f32)
    for (source, dest, away, first_slot, slots), start in zip(groups, starts):

        def collect(j, carry):
            needed = needs(j, away, first_slot)
            flags[start + j] = jnp.where(needed[0] | needed[1], 1, 0)
            here = pl.ds(pl.multiple_of(j * TILE, TILE), TILE)
            there = pl.ds(pl.multiple_of((start + j) * TILE, TILE), TILE)

            @pl.when(needed[0] | needed[1])
            def _():
                kv[there, :] = source[here, :]
                dkv[there, :] = jnp.zeros((TILE, 2 * HEAD), f32)

            @pl.when(jnp.logical_not(needed[0] | needed[1]))
            def _():
                dest[here, :] = jnp.zeros((TILE, 2 * HEAD), bf16)

            for t in range(2):
                add = needed[t]
                if start == 0:
                    add = add & (j != t)

                @pl.when(add)
                def _():
                    count = counts[t]
                    lists[t, count] = start + j
                    counts[t] = count + 1

            return carry

        lax.fori_loop(0, 2 * slots, collect, 0, unroll=True)

    def two_tiles(t, first, second, allowed):
        ones = pl.ds(pl.multiple_of(first * TILE, TILE), TILE)
        twos = pl.ds(pl.multiple_of(second * TILE, TILE), TILE)
        keys = jnp.concatenate([kv[ones, :HEAD], kv[twos, :HEAD]], 0)
        vals = jnp.concatenate([kv[ones, HEAD:], kv[twos, HEAD:]], 0)
        scores = jnp.dot(keys, q_cols[t], preferred_element_type=f32)
        probs = jnp.exp2(scores * (SCALE * LOG2E) - lse_rows[t])
        if allowed is not None:
            probs = jnp.concatenate([jnp.where(allowed, probs[:TILE], 0.0), probs[TILE:]], 0)
        dprobs = jnp.dot(vals, g_cols[t], preferred_element_type=f32)
        dscore = (probs * (dprobs - delta[t])).astype(bf16)
        probs = probs.astype(bf16)
        dkeys = jnp.dot(dscore, q_rows[t], preferred_element_type=f32)
        dvals = jnp.dot(probs, g_rows[t], preferred_element_type=f32)
        dqs = jnp.dot(keys.T, dscore, preferred_element_type=f32)
        return t, ones, twos, dkeys, dvals, dqs

    def add(t, ones, twos, dkeys, dvals, dqs):
        dq[t] += dqs
        dkv[ones, :HEAD] += dkeys[:TILE]
        dkv[ones, HEAD:] += dvals[:TILE]
        dkv[twos, :HEAD] += dkeys[TILE:]
        dkv[twos, HEAD:] += dvals[TILE:]

    most = jnp.maximum(counts[0], counts[1])

    def fill(i, carry):
        for t in range(2):

            @pl.when(i >= counts[t])
            def _():
                lists[t, i] = TILES

        return carry

    lax.fori_loop(jnp.minimum(counts[0], counts[1]), most + 1, fill, 0)
    causal = lax.broadcasted_iota(jnp.int32, (TILE, TILE), 0) <= (
        lax.broadcasted_iota(jnp.int32, (TILE, TILE), 1)
    )
    terms = []
    for t in range(2):
        row = jnp.broadcast_to(seg[q_tile + t], (TILE, TILE)).astype(f32)
        listed = jnp.where(mask[q_tile + t, q_tile + t] > 0, 1.0, 0.0)
        one = jnp.where((row.T == row) & causal, 1.0, 0.0) * listed
        terms.append(two_tiles(t, t, lists[t, 1], jnp.concatenate([one] * GROUPS, 1) > 0.5))
    for term in terms:
        add(*term)

    def rest(i, carry):
        terms = [two_tiles(t, lists[t, 2 * i], lists[t, 2 * i + 1], None) for t in range(2)]
        for term in terms:
            add(*term)
        return carry

    lax.fori_loop(1, lax.shift_right_logical(most + 1, 1), rest, 0)

    for (source, dest, away, first_slot, slots), start in zip(groups, starts):

        def give(j, carry):
            @pl.when(flags[start + j] > 0)
            def _():
                here = pl.ds(pl.multiple_of(j * TILE, TILE), TILE)
                there = pl.ds(pl.multiple_of((start + j) * TILE, TILE), TILE)
                dest[here, :] = dkv[there, :].astype(bf16)

            return carry

        lax.fori_loop(0, 2 * slots, give, 0, unroll=True)

    for t in range(2):
        tok = pl.ds(t * TILE, TILE)
        c, s = cos[tok, :].T, sin[tok, :].T
        for h in range(GROUPS):
            g = dq[t, :, pl.ds(h * TILE, TILE)] * SCALE
            u = g * s
            half = HEAD // 2
            turned = jnp.concatenate([u[half:], -u[:half]], 0)
            qg[pl.ds(h * HEAD, HEAD), tok] = (g * c + turned).astype(bf16)


def vmem(n):
    return [pl.BlockSpec(memory_space=pltpu.VMEM)] * n


def prep(query, grad, att, cos, sin, small):
    s = jax.ShapeDtypeStruct
    return pl.pallas_call(
        prep_kernel,
        out_shape=(
            s((2, ROWS, HEAD), bf16),
            s((2, HEAD, ROWS), bf16),
            s((2, ROWS, HEAD), bf16),
            s((2, HEAD, ROWS), bf16),
            s((2, 1, ROWS), f32),
        ),
        in_specs=vmem(6),
        out_specs=tuple(vmem(5)),
        compiler_params=pltpu.CompilerParams(vmem_limit_bytes=12 << 20),
        cost_estimate=pl.CostEstimate(flops=1000000, bytes_accessed=10000, transcendentals=0),
        name="prep",
    )(query, grad, att, cos, sin, small)


def attention(mask, info, *operands):
    s = jax.ShapeDtypeStruct
    early, late = (s((n * TOK, 2 * HEAD), bf16) for n in (EARLY, 8 - EARLY))
    return pl.pallas_call(
        attention_kernel,
        out_shape=(early, early, late, late, s((ROWS, TOK), bf16)),
        in_specs=[pl.BlockSpec(memory_space=pltpu.SMEM)] * 2 + vmem(len(operands)),
        out_specs=tuple(vmem(5)),
        scratch_shapes=[
            pltpu.VMEM(((TILES + 1) * TILE, 2 * HEAD), bf16),
            pltpu.VMEM(((TILES + 1) * TILE, 2 * HEAD), f32),
            pltpu.VMEM((2, HEAD, ROWS), f32),
            pltpu.VMEM((2, 1, ROWS), f32),
            pltpu.SMEM((2, TILES + 1), jnp.int32),
            pltpu.SMEM((2,), jnp.int32),
            pltpu.SMEM((TILES,), jnp.int32),
        ],
        compiler_params=pltpu.CompilerParams(vmem_limit_bytes=16 << 20),
        cost_estimate=pl.CostEstimate(
            flops=2000000000, bytes_accessed=8000000, transcendentals=1000000
        ),
        name="attention",
    )(mask, info, *operands)


def make_block(key, value, positions):
    s = jax.ShapeDtypeStruct
    inverse = jnp.asarray(np.concatenate([INVERSE, INVERSE])[None, :])
    return pl.pallas_call(
        block_kernel,
        out_shape=(s((TOK, HEAD), f32), s((TOK, HEAD), f32), s((TOK, 2 * HEAD), bf16)),
        in_specs=vmem(4),
        out_specs=tuple(vmem(3)),
        cost_estimate=pl.CostEstimate(flops=5000000, bytes_accessed=700000, transcendentals=60000),
        name="block",
    )(key, value, positions.reshape(2, 1, TILE), inverse)


WIDTH = 5120
STEP_ROWS = 640


def query_part_kernel(qg, wq, out):
    def step(i, carry):
        rows = pl.ds(pl.multiple_of(i * STEP_ROWS, STEP_ROWS), STEP_ROWS)
        out[rows, :] = jnp.dot(wq[rows, :], qg[...], preferred_element_type=f32).astype(bf16)
        return carry

    lax.fori_loop(0, WIDTH // STEP_ROWS, step, 0)


def query_part(qg, wq):
    return pl.pallas_call(
        query_part_kernel,
        out_shape=jax.ShapeDtypeStruct((WIDTH, TOK), bf16),
        in_specs=vmem(2),
        out_specs=vmem(1)[0],
        compiler_params=pltpu.CompilerParams(vmem_limit_bytes=16 << 20),
        cost_estimate=pl.CostEstimate(
            flops=1700000000, bytes_accessed=9000000, transcendentals=0
        ),
        name="query_part",
    )(qg, wq)


def project_kernel(part, own, across, near1, near2, near3, cos, sin, wk, wv, out, grads):
    total = own[...].astype(f32) + across[...].astype(f32)
    for near in (near1, near2, near3):
        total += near[...].astype(f32)
    sign = half_sign((TOK, HEAD), 1)
    g = total[:, :HEAD] * SCALE
    key_grad = g * cos[...] - pltpu.roll(g * sin[...], HEAD // 2, 1) * sign
    grads[:HEAD, :] = key_grad.T.astype(bf16)
    grads[HEAD:, :] = total[:, HEAD:].T.astype(bf16)

    def step(i, carry):
        rows = pl.ds(pl.multiple_of(i * STEP_ROWS, STEP_ROWS), STEP_ROWS)
        weights = jnp.concatenate([wk[rows, :], wv[rows, :]], 1)
        result = jnp.dot(weights, grads[...], preferred_element_type=f32)
        out[rows, :] = (part[rows, :].astype(f32) + result).astype(bf16)
        return carry

    lax.fori_loop(0, WIDTH // STEP_ROWS, step, 0)


def project(part, own, across, near, cos, sin, wk, wv):
    return pl.pallas_call(
        project_kernel,
        out_shape=jax.ShapeDtypeStruct((WIDTH, TOK), bf16),
        in_specs=vmem(10),
        out_specs=vmem(1)[0],
        scratch_shapes=[pltpu.VMEM((2 * HEAD, TOK), bf16)],
        compiler_params=pltpu.CompilerParams(vmem_limit_bytes=16 << 20),
        cost_estimate=pl.CostEstimate(
            flops=700000000, bytes_accessed=6000000, transcendentals=0
        ),
        name="project",
    )(part, own, across, *near, cos, sin, wk, wv)


def last_kernel(parts, out):
    def step(i, carry):
        rows = pl.ds(pl.multiple_of(i * TILE, TILE), TILE)
        total = parts[0, rows, :].astype(f32)
        for k in range(1, 8):
            total += parts[k, rows, :].astype(f32)
        out[rows, :] = total.astype(bf16)
        return carry

    lax.fori_loop(0, 5, step, 0)


def last_sum(parts):
    return pl.pallas_call(
        last_kernel,
        out_shape=jax.ShapeDtypeStruct((640, TOK), bf16),
        in_specs=vmem(1),
        out_specs=vmem(1)[0],
        compiler_params=pltpu.CompilerParams(vmem_limit_bytes=16 << 20),
        cost_estimate=pl.CostEstimate(flops=1300000, bytes_accessed=3000000, transcendentals=0),
        name="last_sum",
    )(parts)


def local(
    query, key, value, att, grad, lse, block_mask, positions, segments, w_query, key_weight,
    value_weight,
):
    me = lax.axis_index(CTX)
    cos, sin, block = make_block(key, value, positions)

    across = swap_zh(block)
    small, again = lax.optimization_barrier((cos[:8] * SCALE, block))
    near = [shift_y(again, k) for k in (1, 2, 3)]
    across, query, grad, att = lax.optimization_barrier((across, query, grad, att))
    far = [shift_y(across, k) for k in (1, 2, 3)]
    q_rows, q_cols, g_rows, g_cols, delta = prep(query, grad, att, cos, sin, small)
    early = jnp.concatenate([block] + near + [across], 0)
    late = jnp.concatenate(far, 0)

    early_mine, early_other, late_mine, late_other, query_grad = attention(
        block_mask, me.reshape(1), segments.reshape(TILES, 1, TILE), lse, delta, cos, sin, q_rows,
        q_cols, g_rows, g_cols, early, swap_core(early), late, swap_core(late),
    )

    late = late_mine.astype(f32) + swap_core(late_other).astype(f32)
    early = early_mine.astype(f32) + swap_core(early_other).astype(f32)
    own, across = early[:TOK], early[4 * TOK :]
    parts = [early[k * TOK : (k + 1) * TOK].astype(bf16) for k in (1, 2, 3)]
    parts += [late[k * TOK : (k + 1) * TOK].astype(bf16) for k in range(3)]
    own, across, parts = lax.optimization_barrier((own, across, parts))
    far = [shift_y(parts[2 + k], -k) for k in (1, 2, 3)]
    near = [shift_y(parts[k - 1], -k) for k in (1, 2, 3)]
    across = across + sum(p.astype(f32) for p in far)
    across, query_grad = lax.optimization_barrier((across.astype(bf16), query_grad))
    across = swap_zh(across)
    part, near = lax.optimization_barrier((query_part(query_grad, w_query), near))
    send = project(part, own, across, near, cos, sin, key_weight, value_weight)
    return last_sum(lax.all_to_all(send.reshape(8, 640, TOK), TP, 0, 0))


def solution(mesh):
    fine = Mesh(mesh.devices.reshape(4, 2, 2, 4, 2), ("y", "zh", "core", "x", "zl"))
    in_specs = (
        P(CTX, TP),
        P(CTX, TP),
        P(CTX, TP),
        P(CTX, TP),
        P(CTX, TP),
        P(TP, CTX),
        P(),
        P(CTX),
        P(),
        P(None, TP),
        P(None, TP),
        P(None, TP),
    )
    return jax.shard_map(
        local, mesh=fine, in_specs=in_specs, out_specs=P(TP, CTX), check_vma=False
    )
```

```python
import numpy as np
import jax
import jax.numpy as jnp
from jax import lax
from jax.experimental import pallas as pl
from jax.experimental.pallas import tpu as pltpu
from jax.sharding import Mesh, PartitionSpec as P

HEAD = 128
TILE = 128
GROUPS = 5
TOK = 256
TILES = 32
ROWS = GROUPS * TILE
SCALE = HEAD**-0.5
ROPE_BASE = 1000000.0
LOG2E = 1.4426950408889634
CTX = ("y", "zh", "core")
TP = ("x", "zl")

f32 = jnp.float32
bf16 = jnp.bfloat16


def shift(x, axes, sizes, offs):
    perm = []
    for source in np.ndindex(*sizes):
        dest = tuple((a + o) % s for a, o, s in zip(source, offs, sizes))
        perm.append(
            (int(np.ravel_multi_index(source, sizes)), int(np.ravel_multi_index(dest, sizes)))
        )
    return lax.ppermute(x, axes, perm)


def shift_y(x, k):
    return shift(x, ("y",), (4,), (k % 4,))


def swap_zh(x):
    return shift(x, ("zh",), (2,), (1,))


def swap_core(x):
    return shift(x, ("core",), (2,), (1,))


INVERSE = np.power(np.float64(ROPE_BASE), -np.arange(HEAD // 2) * (2.0 / HEAD)).astype(np.float32)


def half_sign(shape, axis):
    return jnp.where(lax.broadcasted_iota(jnp.int32, shape, axis) < HEAD // 2, -1.0, 1.0).astype(f32)


def block_kernel(key, value, positions, inverse, cos, sin, block):
    sign = half_sign((TILE, HEAD), 1)
    low = lax.broadcasted_iota(jnp.int32, (TILE, HEAD), 1) < HEAD // 2
    places = [jnp.broadcast_to(positions[t].astype(f32), (TILE, TILE)).T for t in range(2)]
    angles = jnp.where(low, places[0], places[1]) * inverse[...]
    both_cos, both_sin = jnp.cos(angles), jnp.sin(angles)
    for t in range(2):
        tok = pl.ds(t * TILE, TILE)
        mine = low if t == 0 else jnp.logical_not(low)
        c = jnp.where(mine, both_cos, pltpu.roll(both_cos, HEAD // 2, 1))
        s = jnp.where(mine, both_sin, pltpu.roll(both_sin, HEAD // 2, 1))
        cos[tok, :] = c
        sin[tok, :] = s
        x = key[tok, :].astype(f32)
        block[tok, :HEAD] = (x * c + pltpu.roll(x, HEAD // 2, 1) * (s * sign)).astype(bf16)
        block[tok, HEAD:] = value[tok, :]


def prep_kernel(query, grad, att, cos, sin, small, q_rows, q_cols, g_rows, g_cols, delta):
    sign = half_sign((TILE, HEAD), 1)
    for t in range(2):
        tok = pl.ds(t * TILE, TILE)
        c, s = cos[tok, :], sin[tok, :] * sign
        for h in range(GROUPS):
            feat = pl.ds(h * HEAD, HEAD)
            lane = pl.ds(h * TILE, TILE)
            x = query[tok, feat].astype(f32)
            rot = (x * c + pltpu.roll(x, HEAD // 2, 1) * s).astype(bf16)
            q_rows[t, lane, :] = rot
            q_cols[t, :, lane] = rot.T
            g = grad[tok, feat]
            g_rows[t, lane, :] = g
            g_cols[t, :, lane] = g.T
            prod = g.astype(f32) * att[tok, feat].astype(f32)
            delta[t, :, lane] = jnp.sum(prod.T, axis=0, keepdims=True)


EARLY = 5


def attention_kernel(
    mask, info, seg, lse, delta, cos, sin, q_rows, q_cols, g_rows, g_cols,
    early_mine, early_other, late_mine, late_other,
    d_early_mine, d_early_other, d_late_mine, d_late_other, qg,
    kv, dkv, dq, lse_rows, lists, counts, flags,
):
    dq[...] = jnp.zeros_like(dq)
    for t in range(2):
        for h in range(GROUPS):
            row = lse[h : h + 1, t * TILE : (t + 1) * TILE]
            lse_rows[t, :, pl.ds(h * TILE, TILE)] = row * LOG2E
    me = info[0]
    q_tile = 2 * me
    groups = (
        (early_mine, d_early_mine, 0, 0, EARLY),
        (early_other, d_early_other, 1, 0, EARLY),
        (late_mine, d_late_mine, 0, EARLY, 8 - EARLY),
        (late_other, d_late_other, 1, EARLY, 8 - EARLY),
    )
    starts = (0, 2 * EARLY, 4 * EARLY, 4 * EARLY + 2 * (8 - EARLY))

    def needs(j, away, first_slot):
        slot = lax.shift_right_logical(j, 1) + first_slot
        back_y = (lax.shift_right_logical(me, 2) - slot) & 3
        back_zh = (me ^ (lax.shift_right_logical(slot, 1) & 2)) & 2
        tile = 2 * (4 * back_y + back_zh + ((me ^ away) & 1)) + (j & 1)
        return mask[q_tile, tile] > 0, mask[q_tile + 1, tile] > 0

    for t in range(2):
        lists[t, 0] = t
        counts[t] = 1
    kv[pl.ds(TILES * TILE, TILE), :] = jnp.zeros((TILE, 2 * HEAD), bf16)
    dkv[pl.ds(TILES * TILE, TILE), :] = jnp.zeros((TILE, 2 * HEAD), f32)
    for (source, dest, away, first_slot, slots), start in zip(groups, starts):

        def collect(j, carry):
            needed = needs(j, away, first_slot)
            flags[start + j] = jnp.where(needed[0] | needed[1], 1, 0)
            here = pl.ds(pl.multiple_of(j * TILE, TILE), TILE)
            there = pl.ds(pl.multiple_of((start + j) * TILE, TILE), TILE)

            @pl.when(needed[0] | needed[1])
            def _():
                kv[there, :] = source[here, :]
                dkv[there, :] = jnp.zeros((TILE, 2 * HEAD), f32)

            @pl.when(jnp.logical_not(needed[0] | needed[1]))
            def _():
                dest[here, :] = jnp.zeros((TILE, 2 * HEAD), bf16)

            for t in range(2):
                add = needed[t]
                if start == 0:
                    add = add & (j != t)

                @pl.when(add)
                def _():
                    count = counts[t]
                    lists[t, count] = start + j
                    counts[t] = count + 1

            return carry

        lax.fori_loop(0, 2 * slots, collect, 0, unroll=True)

    def two_tiles(t, first, second, allowed):
        ones = pl.ds(pl.multiple_of(first * TILE, TILE), TILE)
        twos = pl.ds(pl.multiple_of(second * TILE, TILE), TILE)
        keys = jnp.concatenate([kv[ones, :HEAD], kv[twos, :HEAD]], 0)
        vals = jnp.concatenate([kv[ones, HEAD:], kv[twos, HEAD:]], 0)
        scores = jnp.dot(keys, q_cols[t], preferred_element_type=f32)
        probs = jnp.exp2(scores * (SCALE * LOG2E) - lse_rows[t])
        if allowed is not None:
            probs = jnp.concatenate([jnp.where(allowed, probs[:TILE], 0.0), probs[TILE:]], 0)
        dprobs = jnp.dot(vals, g_cols[t], preferred_element_type=f32)
        dscore = (probs * (dprobs - delta[t])).astype(bf16)
        probs = probs.astype(bf16)
        dkeys = jnp.dot(dscore, q_rows[t], preferred_element_type=f32)
        dvals = jnp.dot(probs, g_rows[t], preferred_element_type=f32)
        dqs = jnp.dot(keys.T, dscore, preferred_element_type=f32)
        return t, ones, twos, dkeys, dvals, dqs

    def add(t, ones, twos, dkeys, dvals, dqs):
        dq[t] += dqs
        dkv[ones, :HEAD] += dkeys[:TILE]
        dkv[ones, HEAD:] += dvals[:TILE]
        dkv[twos, :HEAD] += dkeys[TILE:]
        dkv[twos, HEAD:] += dvals[TILE:]

    most = jnp.maximum(counts[0], counts[1])

    def fill(i, carry):
        for t in range(2):

            @pl.when(i >= counts[t])
            def _():
                lists[t, i] = TILES

        return carry

    lax.fori_loop(jnp.minimum(counts[0], counts[1]), most + 1, fill, 0)
    causal = lax.broadcasted_iota(jnp.int32, (TILE, TILE), 0) <= (
        lax.broadcasted_iota(jnp.int32, (TILE, TILE), 1)
    )
    terms = []
    for t in range(2):
        row = jnp.broadcast_to(seg[q_tile + t], (TILE, TILE)).astype(f32)
        listed = jnp.where(mask[q_tile + t, q_tile + t] > 0, 1.0, 0.0)
        one = jnp.where((row.T == row) & causal, 1.0, 0.0) * listed
        terms.append(two_tiles(t, t, lists[t, 1], jnp.concatenate([one] * GROUPS, 1) > 0.5))
    for term in terms:
        add(*term)

    def rest(i, carry):
        terms = [two_tiles(t, lists[t, 2 * i], lists[t, 2 * i + 1], None) for t in range(2)]
        for term in terms:
            add(*term)
        return carry

    lax.fori_loop(1, lax.shift_right_logical(most + 1, 1), rest, 0)

    for (source, dest, away, first_slot, slots), start in zip(groups, starts):

        def give(j, carry):
            @pl.when(flags[start + j] > 0)
            def _():
                here = pl.ds(pl.multiple_of(j * TILE, TILE), TILE)
                there = pl.ds(pl.multiple_of((start + j) * TILE, TILE), TILE)
                dest[here, :] = dkv[there, :].astype(bf16)

            return carry

        lax.fori_loop(0, 2 * slots, give, 0, unroll=True)

    for t in range(2):
        tok = pl.ds(t * TILE, TILE)
        c, s = cos[tok, :].T, sin[tok, :].T
        for h in range(GROUPS):
            g = dq[t, :, pl.ds(h * TILE, TILE)] * SCALE
            u = g * s
            half = HEAD // 2
            turned = jnp.concatenate([u[half:], -u[:half]], 0)
            qg[pl.ds(h * HEAD, HEAD), tok] = (g * c + turned).astype(bf16)


def vmem(n):
    return [pl.BlockSpec(memory_space=pltpu.VMEM)] * n


def prep(query, grad, att, cos, sin, small):
    s = jax.ShapeDtypeStruct
    return pl.pallas_call(
        prep_kernel,
        out_shape=(
            s((2, ROWS, HEAD), bf16),
            s((2, HEAD, ROWS), bf16),
            s((2, ROWS, HEAD), bf16),
            s((2, HEAD, ROWS), bf16),
            s((2, 1, ROWS), f32),
        ),
        in_specs=vmem(6),
        out_specs=tuple(vmem(5)),
        compiler_params=pltpu.CompilerParams(vmem_limit_bytes=12 << 20),
        cost_estimate=pl.CostEstimate(flops=1000000, bytes_accessed=10000, transcendentals=0),
        name="prep",
    )(query, grad, att, cos, sin, small)


def attention(mask, info, *operands):
    s = jax.ShapeDtypeStruct
    early, late = (s((n * TOK, 2 * HEAD), bf16) for n in (EARLY, 8 - EARLY))
    return pl.pallas_call(
        attention_kernel,
        out_shape=(early, early, late, late, s((ROWS, TOK), bf16)),
        in_specs=[pl.BlockSpec(memory_space=pltpu.SMEM)] * 2 + vmem(len(operands)),
        out_specs=tuple(vmem(5)),
        scratch_shapes=[
            pltpu.VMEM(((TILES + 1) * TILE, 2 * HEAD), bf16),
            pltpu.VMEM(((TILES + 1) * TILE, 2 * HEAD), f32),
            pltpu.VMEM((2, HEAD, ROWS), f32),
            pltpu.VMEM((2, 1, ROWS), f32),
            pltpu.SMEM((2, TILES + 1), jnp.int32),
            pltpu.SMEM((2,), jnp.int32),
            pltpu.SMEM((TILES,), jnp.int32),
        ],
        compiler_params=pltpu.CompilerParams(vmem_limit_bytes=16 << 20),
        cost_estimate=pl.CostEstimate(
            flops=2000000000, bytes_accessed=8000000, transcendentals=1000000
        ),
        name="attention",
    )(mask, info, *operands)


def make_block(key, value, positions):
    s = jax.ShapeDtypeStruct
    inverse = jnp.asarray(np.concatenate([INVERSE, INVERSE])[None, :])
    return pl.pallas_call(
        block_kernel,
        out_shape=(s((TOK, HEAD), f32), s((TOK, HEAD), f32), s((TOK, 2 * HEAD), bf16)),
        in_specs=vmem(4),
        out_specs=tuple(vmem(3)),
        cost_estimate=pl.CostEstimate(flops=5000000, bytes_accessed=700000, transcendentals=60000),
        name="block",
    )(key, value, positions.reshape(2, 1, TILE), inverse)


WIDTH = 5120
STEP_ROWS = 640


def query_part_kernel(qg, wq, out):
    def step(i, carry):
        rows = pl.ds(pl.multiple_of(i * STEP_ROWS, STEP_ROWS), STEP_ROWS)
        out[rows, :] = jnp.dot(wq[rows, :], qg[...], preferred_element_type=f32).astype(bf16)
        return carry

    lax.fori_loop(0, WIDTH // STEP_ROWS, step, 0)


def query_part(qg, wq):
    return pl.pallas_call(
        query_part_kernel,
        out_shape=jax.ShapeDtypeStruct((WIDTH, TOK), bf16),
        in_specs=vmem(2),
        out_specs=vmem(1)[0],
        compiler_params=pltpu.CompilerParams(vmem_limit_bytes=16 << 20),
        cost_estimate=pl.CostEstimate(
            flops=1700000000, bytes_accessed=9000000, transcendentals=0
        ),
        name="query_part",
    )(qg, wq)


def project_kernel(part, own, across, near1, near2, near3, cos, sin, wk, wv, out, grads):
    total = own[...].astype(f32) + across[...].astype(f32)
    for near in (near1, near2, near3):
        total += near[...].astype(f32)
    sign = half_sign((TOK, HEAD), 1)
    g = total[:, :HEAD] * SCALE
    key_grad = g * cos[...] - pltpu.roll(g * sin[...], HEAD // 2, 1) * sign
    grads[:HEAD, :] = key_grad.T.astype(bf16)
    grads[HEAD:, :] = total[:, HEAD:].T.astype(bf16)

    def step(i, carry):
        rows = pl.ds(pl.multiple_of(i * STEP_ROWS, STEP_ROWS), STEP_ROWS)
        weights = jnp.concatenate([wk[rows, :], wv[rows, :]], 1)
        result = jnp.dot(weights, grads[...], preferred_element_type=f32)
        out[rows, :] = (part[rows, :].astype(f32) + result).astype(bf16)
        return carry

    lax.fori_loop(0, WIDTH // STEP_ROWS, step, 0, unroll=True)


def project(part, own, across, near, cos, sin, wk, wv):
    return pl.pallas_call(
        project_kernel,
        out_shape=jax.ShapeDtypeStruct((WIDTH, TOK), bf16),
        in_specs=vmem(10),
        out_specs=vmem(1)[0],
        scratch_shapes=[pltpu.VMEM((2 * HEAD, TOK), bf16)],
        compiler_params=pltpu.CompilerParams(vmem_limit_bytes=16 << 20),
        cost_estimate=pl.CostEstimate(
            flops=700000000, bytes_accessed=6000000, transcendentals=0
        ),
        name="project",
    )(part, own, across, *near, cos, sin, wk, wv)


def last_kernel(parts, out):
    def step(i, carry):
        rows = pl.ds(pl.multiple_of(i * TILE, TILE), TILE)
        total = parts[0, rows, :].astype(f32)
        for k in range(1, 8):
            total += parts[k, rows, :].astype(f32)
        out[rows, :] = total.astype(bf16)
        return carry

    lax.fori_loop(0, 5, step, 0, unroll=True)


def last_sum(parts):
    return pl.pallas_call(
        last_kernel,
        out_shape=jax.ShapeDtypeStruct((640, TOK), bf16),
        in_specs=vmem(1),
        out_specs=vmem(1)[0],
        compiler_params=pltpu.CompilerParams(vmem_limit_bytes=16 << 20),
        cost_estimate=pl.CostEstimate(flops=1300000, bytes_accessed=3000000, transcendentals=0),
        name="last_sum",
    )(parts)


def local(
    query, key, value, att, grad, lse, block_mask, positions, segments, w_query, key_weight,
    value_weight,
):
    me = lax.axis_index(CTX)
    cos, sin, block = make_block(key, value, positions)

    across = swap_zh(block)
    small, again = lax.optimization_barrier((cos[:8] * SCALE, block))
    near = [shift_y(again, k) for k in (1, 2, 3)]
    across, query, grad, att = lax.optimization_barrier((across, query, grad, att))
    far = [shift_y(across, k) for k in (1, 2, 3)]
    q_rows, q_cols, g_rows, g_cols, delta = prep(query, grad, att, cos, sin, small)
    early = jnp.concatenate([block] + near + [across], 0)
    late = jnp.concatenate(far, 0)

    early_mine, early_other, late_mine, late_other, query_grad = attention(
        block_mask, me.reshape(1), segments.reshape(TILES, 1, TILE), lse, delta, cos, sin, q_rows,
        q_cols, g_rows, g_cols, early, swap_core(early), late, swap_core(late),
    )

    late = late_mine.astype(f32) + swap_core(late_other).astype(f32)
    early = early_mine.astype(f32) + swap_core(early_other).astype(f32)
    own, across = early[:TOK], early[4 * TOK :]
    parts = [early[k * TOK : (k + 1) * TOK].astype(bf16) for k in (1, 2, 3)]
    parts += [late[k * TOK : (k + 1) * TOK].astype(bf16) for k in range(3)]
    own, across, parts = lax.optimization_barrier((own, across, parts))
    far = [shift_y(parts[2 + k], -k) for k in (1, 2, 3)]
    near = [shift_y(parts[k - 1], -k) for k in (1, 2, 3)]
    across = across + sum(p.astype(f32) for p in far)
    across, query_grad = lax.optimization_barrier((across.astype(bf16), query_grad))
    across = swap_zh(across)
    part, near = lax.optimization_barrier((query_part(query_grad, w_query), near))
    send = project(part, own, across, near, cos, sin, key_weight, value_weight)
    return last_sum(lax.all_to_all(send.reshape(8, 640, TOK), TP, 0, 0))


def solution(mesh):
    fine = Mesh(mesh.devices.reshape(4, 2, 2, 4, 2), ("y", "zh", "core", "x", "zl"))
    in_specs = (
        P(CTX, TP),
        P(CTX, TP),
        P(CTX, TP),
        P(CTX, TP),
        P(CTX, TP),
        P(TP, CTX),
        P(),
        P(CTX),
        P(),
        P(None, TP),
        P(None, TP),
        P(None, TP),
    )
    return jax.shard_map(
        local, mesh=fine, in_specs=in_specs, out_specs=P(TP, CTX), check_vma=False
    )
```

```python
import numpy as np
import jax
import jax.numpy as jnp
from jax import lax
from jax.experimental import pallas as pl
from jax.experimental.pallas import tpu as pltpu
from jax.sharding import Mesh, PartitionSpec as P

HEAD = 128
TILE = 128
GROUPS = 5
TOK = 256
TILES = 32
ROWS = GROUPS * TILE
SCALE = HEAD**-0.5
ROPE_BASE = 1000000.0
LOG2E = 1.4426950408889634
CTX = ("y", "zh", "core")
TP = ("x", "zl")

f32 = jnp.float32
bf16 = jnp.bfloat16


def shift(x, axes, sizes, offs):
    perm = []
    for source in np.ndindex(*sizes):
        dest = tuple((a + o) % s for a, o, s in zip(source, offs, sizes))
        perm.append(
            (int(np.ravel_multi_index(source, sizes)), int(np.ravel_multi_index(dest, sizes)))
        )
    return lax.ppermute(x, axes, perm)


def shift_y(x, k):
    return shift(x, ("y",), (4,), (k % 4,))


def swap_zh(x):
    return shift(x, ("zh",), (2,), (1,))


def swap_core(x):
    return shift(x, ("core",), (2,), (1,))


INVERSE = np.power(np.float64(ROPE_BASE), -np.arange(HEAD // 2) * (2.0 / HEAD)).astype(np.float32)


def half_sign(shape, axis):
    return jnp.where(lax.broadcasted_iota(jnp.int32, shape, axis) < HEAD // 2, -1.0, 1.0).astype(f32)


def block_kernel(key, value, positions, inverse, cos, sin, block):
    sign = half_sign((TILE, HEAD), 1)
    low = lax.broadcasted_iota(jnp.int32, (TILE, HEAD), 1) < HEAD // 2
    places = [jnp.broadcast_to(positions[t].astype(f32), (TILE, TILE)).T for t in range(2)]
    angles = jnp.where(low, places[0], places[1]) * inverse[...]
    both_cos, both_sin = jnp.cos(angles), jnp.sin(angles)
    for t in range(2):
        tok = pl.ds(t * TILE, TILE)
        mine = low if t == 0 else jnp.logical_not(low)
        c = jnp.where(mine, both_cos, pltpu.roll(both_cos, HEAD // 2, 1))
        s = jnp.where(mine, both_sin, pltpu.roll(both_sin, HEAD // 2, 1))
        cos[tok, :] = c
        sin[tok, :] = s
        x = key[tok, :].astype(f32)
        block[tok, :HEAD] = (x * c + pltpu.roll(x, HEAD // 2, 1) * (s * sign)).astype(bf16)
        block[tok, HEAD:] = value[tok, :]


def prep_kernel(query, grad, att, cos, sin, small, q_rows, q_cols, g_rows, g_cols, delta):
    sign = half_sign((TILE, HEAD), 1)
    for t in range(2):
        tok = pl.ds(t * TILE, TILE)
        c, s = cos[tok, :], sin[tok, :] * sign
        for h in range(GROUPS):
            feat = pl.ds(h * HEAD, HEAD)
            lane = pl.ds(h * TILE, TILE)
            x = query[tok, feat].astype(f32)
            rot = (x * c + pltpu.roll(x, HEAD // 2, 1) * s).astype(bf16)
            q_rows[t, lane, :] = rot
            q_cols[t, :, lane] = rot.T
            g = grad[tok, feat]
            g_rows[t, lane, :] = g
            g_cols[t, :, lane] = g.T
            prod = g.astype(f32) * att[tok, feat].astype(f32)
            delta[t, :, lane] = jnp.sum(prod.T, axis=0, keepdims=True)


EARLY = 5


def attention_kernel(
    mask, info, seg, lse, delta, cos, sin, q_rows, q_cols, g_rows, g_cols,
    early_mine, early_other, late_mine, late_other,
    d_early_mine, d_early_other, d_late_mine, d_late_other, qg,
    kv, dkv, dq, lse_rows, lists, counts, flags,
):
    dq[...] = jnp.zeros_like(dq)
    for t in range(2):
        for h in range(GROUPS):
            row = lse[h : h + 1, t * TILE : (t + 1) * TILE]
            lse_rows[t, :, pl.ds(h * TILE, TILE)] = row * LOG2E
    me = info[0]
    q_tile = 2 * me
    groups = (
        (early_mine, d_early_mine, 0, 0, EARLY),
        (early_other, d_early_other, 1, 0, EARLY),
        (late_mine, d_late_mine, 0, EARLY, 8 - EARLY),
        (late_other, d_late_other, 1, EARLY, 8 - EARLY),
    )
    starts = (0, 2 * EARLY, 4 * EARLY, 4 * EARLY + 2 * (8 - EARLY))

    def needs(j, away, first_slot):
        slot = lax.shift_right_logical(j, 1) + first_slot
        back_y = (lax.shift_right_logical(me, 2) - slot) & 3
        back_zh = (me ^ (lax.shift_right_logical(slot, 1) & 2)) & 2
        tile = 2 * (4 * back_y + back_zh + ((me ^ away) & 1)) + (j & 1)
        return mask[q_tile, tile] > 0, mask[q_tile + 1, tile] > 0

    for t in range(2):
        lists[t, 0] = t
        counts[t] = 1
    kv[pl.ds(TILES * TILE, TILE), :] = jnp.zeros((TILE, 2 * HEAD), bf16)
    dkv[pl.ds(TILES * TILE, TILE), :] = jnp.zeros((TILE, 2 * HEAD), f32)
    for (source, dest, away, first_slot, slots), start in zip(groups, starts):

        def collect(j, carry):
            needed = needs(j, away, first_slot)
            flags[start + j] = jnp.where(needed[0] | needed[1], 1, 0)
            here = pl.ds(pl.multiple_of(j * TILE, TILE), TILE)
            there = pl.ds(pl.multiple_of((start + j) * TILE, TILE), TILE)

            @pl.when(needed[0] | needed[1])
            def _():
                kv[there, :] = source[here, :]
                dkv[there, :] = jnp.zeros((TILE, 2 * HEAD), f32)

            @pl.when(jnp.logical_not(needed[0] | needed[1]))
            def _():
                dest[here, :] = jnp.zeros((TILE, 2 * HEAD), bf16)

            for t in range(2):
                add = needed[t]
                if start == 0:
                    add = add & (j != t)

                @pl.when(add)
                def _():
                    count = counts[t]
                    lists[t, count] = start + j
                    counts[t] = count + 1

            return carry

        lax.fori_loop(0, 2 * slots, collect, 0, unroll=True)

    def two_tiles(t, first, second, allowed):
        ones = pl.ds(pl.multiple_of(first * TILE, TILE), TILE)
        twos = pl.ds(pl.multiple_of(second * TILE, TILE), TILE)
        keys = jnp.concatenate([kv[ones, :HEAD], kv[twos, :HEAD]], 0)
        vals = jnp.concatenate([kv[ones, HEAD:], kv[twos, HEAD:]], 0)
        scores = jnp.dot(keys, q_cols[t], preferred_element_type=f32)
        probs = jnp.exp2(scores * (SCALE * LOG2E) - lse_rows[t])
        if allowed is not None:
            probs = jnp.concatenate([jnp.where(allowed, probs[:TILE], 0.0), probs[TILE:]], 0)
        dprobs = jnp.dot(vals, g_cols[t], preferred_element_type=f32)
        dscore = (probs * (dprobs - delta[t])).astype(bf16)
        probs = probs.astype(bf16)
        dkeys = jnp.dot(dscore, q_rows[t], preferred_element_type=f32)
        dvals = jnp.dot(probs, g_rows[t], preferred_element_type=f32)
        dqs = jnp.dot(keys.T, dscore, preferred_element_type=f32)
        return t, ones, twos, dkeys, dvals, dqs

    def add(t, ones, twos, dkeys, dvals, dqs):
        dq[t] += dqs
        dkv[ones, :HEAD] += dkeys[:TILE]
        dkv[ones, HEAD:] += dvals[:TILE]
        dkv[twos, :HEAD] += dkeys[TILE:]
        dkv[twos, HEAD:] += dvals[TILE:]

    most = jnp.maximum(counts[0], counts[1])

    def fill(i, carry):
        for t in range(2):

            @pl.when(i >= counts[t])
            def _():
                lists[t, i] = TILES

        return carry

    lax.fori_loop(jnp.minimum(counts[0], counts[1]), most + 1, fill, 0)
    causal = lax.broadcasted_iota(jnp.int32, (TILE, TILE), 0) <= (
        lax.broadcasted_iota(jnp.int32, (TILE, TILE), 1)
    )
    terms = []
    for t in range(2):
        row = jnp.broadcast_to(seg[q_tile + t], (TILE, TILE)).astype(f32)
        listed = jnp.where(mask[q_tile + t, q_tile + t] > 0, 1.0, 0.0)
        one = jnp.where((row.T == row) & causal, 1.0, 0.0) * listed
        terms.append(two_tiles(t, t, lists[t, 1], jnp.concatenate([one] * GROUPS, 1) > 0.5))
    for term in terms:
        add(*term)

    def rest(i, carry):
        terms = [two_tiles(t, lists[t, 2 * i], lists[t, 2 * i + 1], None) for t in range(2)]
        for term in terms:
            add(*term)
        return carry

    lax.fori_loop(1, lax.shift_right_logical(most + 1, 1), rest, 0)

    for (source, dest, away, first_slot, slots), start in zip(groups, starts):

        def give(j, carry):
            @pl.when(flags[start + j] > 0)
            def _():
                here = pl.ds(pl.multiple_of(j * TILE, TILE), TILE)
                there = pl.ds(pl.multiple_of((start + j) * TILE, TILE), TILE)
                dest[here, :] = dkv[there, :].astype(bf16)

            return carry

        lax.fori_loop(0, 2 * slots, give, 0, unroll=True)

    for t in range(2):
        tok = pl.ds(t * TILE, TILE)
        c, s = cos[tok, :].T, sin[tok, :].T
        for h in range(GROUPS):
            g = dq[t, :, pl.ds(h * TILE, TILE)] * SCALE
            u = g * s
            half = HEAD // 2
            turned = jnp.concatenate([u[half:], -u[:half]], 0)
            qg[pl.ds(h * HEAD, HEAD), tok] = (g * c + turned).astype(bf16)


def vmem(n):
    return [pl.BlockSpec(memory_space=pltpu.VMEM)] * n


def prep(query, grad, att, cos, sin, small):
    s = jax.ShapeDtypeStruct
    return pl.pallas_call(
        prep_kernel,
        out_shape=(
            s((2, ROWS, HEAD), bf16),
            s((2, HEAD, ROWS), bf16),
            s((2, ROWS, HEAD), bf16),
            s((2, HEAD, ROWS), bf16),
            s((2, 1, ROWS), f32),
        ),
        in_specs=vmem(6),
        out_specs=tuple(vmem(5)),
        compiler_params=pltpu.CompilerParams(vmem_limit_bytes=12 << 20),
        cost_estimate=pl.CostEstimate(flops=1000000, bytes_accessed=10000, transcendentals=0),
        name="prep",
    )(query, grad, att, cos, sin, small)


def attention(mask, info, *operands):
    s = jax.ShapeDtypeStruct
    early, late = (s((n * TOK, 2 * HEAD), bf16) for n in (EARLY, 8 - EARLY))
    return pl.pallas_call(
        attention_kernel,
        out_shape=(early, early, late, late, s((ROWS, TOK), bf16)),
        in_specs=[pl.BlockSpec(memory_space=pltpu.SMEM)] * 2 + vmem(len(operands)),
        out_specs=tuple(vmem(5)),
        scratch_shapes=[
            pltpu.VMEM(((TILES + 1) * TILE, 2 * HEAD), bf16),
            pltpu.VMEM(((TILES + 1) * TILE, 2 * HEAD), f32),
            pltpu.VMEM((2, HEAD, ROWS), f32),
            pltpu.VMEM((2, 1, ROWS), f32),
            pltpu.SMEM((2, TILES + 1), jnp.int32),
            pltpu.SMEM((2,), jnp.int32),
            pltpu.SMEM((TILES,), jnp.int32),
        ],
        compiler_params=pltpu.CompilerParams(vmem_limit_bytes=16 << 20),
        cost_estimate=pl.CostEstimate(
            flops=2000000000, bytes_accessed=8000000, transcendentals=1000000
        ),
        name="attention",
    )(mask, info, *operands)


def make_block(key, value, positions):
    s = jax.ShapeDtypeStruct
    inverse = jnp.asarray(np.concatenate([INVERSE, INVERSE])[None, :])
    return pl.pallas_call(
        block_kernel,
        out_shape=(s((TOK, HEAD), f32), s((TOK, HEAD), f32), s((TOK, 2 * HEAD), bf16)),
        in_specs=vmem(4),
        out_specs=tuple(vmem(3)),
        cost_estimate=pl.CostEstimate(flops=5000000, bytes_accessed=700000, transcendentals=60000),
        name="block",
    )(key, value, positions.reshape(2, 1, TILE), inverse)


WIDTH = 5120
STEP_ROWS = 640


def query_part_kernel(qg, wq, out):
    def step(i, carry):
        rows = pl.ds(pl.multiple_of(i * STEP_ROWS, STEP_ROWS), STEP_ROWS)
        out[rows, :] = jnp.dot(wq[rows, :], qg[...], preferred_element_type=f32).astype(bf16)
        return carry

    lax.fori_loop(0, WIDTH // STEP_ROWS, step, 0, unroll=True)


def query_part(qg, wq):
    return pl.pallas_call(
        query_part_kernel,
        out_shape=jax.ShapeDtypeStruct((WIDTH, TOK), bf16),
        in_specs=vmem(2),
        out_specs=vmem(1)[0],
        compiler_params=pltpu.CompilerParams(vmem_limit_bytes=16 << 20),
        cost_estimate=pl.CostEstimate(
            flops=1700000000, bytes_accessed=9000000, transcendentals=0
        ),
        name="query_part",
    )(qg, wq)


def project_kernel(part, own, across, near1, near2, near3, cos, sin, wk, wv, out, grads):
    total = own[...].astype(f32) + across[...].astype(f32)
    for near in (near1, near2, near3):
        total += near[...].astype(f32)
    sign = half_sign((TOK, HEAD), 1)
    g = total[:, :HEAD] * SCALE
    key_grad = g * cos[...] - pltpu.roll(g * sin[...], HEAD // 2, 1) * sign
    grads[:HEAD, :] = key_grad.T.astype(bf16)
    grads[HEAD:, :] = total[:, HEAD:].T.astype(bf16)

    def step(i, carry):
        rows = pl.ds(pl.multiple_of(i * STEP_ROWS, STEP_ROWS), STEP_ROWS)
        weights = jnp.concatenate([wk[rows, :], wv[rows, :]], 1)
        result = jnp.dot(weights, grads[...], preferred_element_type=f32)
        out[rows, :] = (part[rows, :].astype(f32) + result).astype(bf16)
        return carry

    lax.fori_loop(0, WIDTH // STEP_ROWS, step, 0, unroll=True)


def project(part, own, across, near, cos, sin, wk, wv):
    return pl.pallas_call(
        project_kernel,
        out_shape=jax.ShapeDtypeStruct((WIDTH, TOK), bf16),
        in_specs=vmem(10),
        out_specs=vmem(1)[0],
        scratch_shapes=[pltpu.VMEM((2 * HEAD, TOK), bf16)],
        compiler_params=pltpu.CompilerParams(vmem_limit_bytes=16 << 20),
        cost_estimate=pl.CostEstimate(
            flops=700000000, bytes_accessed=6000000, transcendentals=0
        ),
        name="project",
    )(part, own, across, *near, cos, sin, wk, wv)


def last_kernel(parts, out):
    def step(i, carry):
        rows = pl.ds(pl.multiple_of(i * TILE, TILE), TILE)
        total = parts[0, rows, :].astype(f32)
        for k in range(1, 8):
            total += parts[k, rows, :].astype(f32)
        out[rows, :] = total.astype(bf16)
        return carry

    lax.fori_loop(0, 5, step, 0, unroll=True)


def last_sum(parts):
    return pl.pallas_call(
        last_kernel,
        out_shape=jax.ShapeDtypeStruct((640, TOK), bf16),
        in_specs=vmem(1),
        out_specs=vmem(1)[0],
        compiler_params=pltpu.CompilerParams(vmem_limit_bytes=16 << 20),
        cost_estimate=pl.CostEstimate(flops=1300000, bytes_accessed=3000000, transcendentals=0),
        name="last_sum",
    )(parts)


def local(
    query, key, value, att, grad, lse, block_mask, positions, segments, w_query, key_weight,
    value_weight,
):
    me = lax.axis_index(CTX)
    cos, sin, block = make_block(key, value, positions)

    across = swap_zh(block)
    small, again = lax.optimization_barrier((cos[:8] * SCALE, block))
    near = [shift_y(again, k) for k in (1, 2, 3)]
    across, query, grad, att = lax.optimization_barrier((across, query, grad, att))
    far = [shift_y(across, k) for k in (1, 2, 3)]
    q_rows, q_cols, g_rows, g_cols, delta = prep(query, grad, att, cos, sin, small)
    early = jnp.concatenate([block] + near + [across], 0)
    late = jnp.concatenate(far, 0)

    early_mine, early_other, late_mine, late_other, query_grad = attention(
        block_mask, me.reshape(1), segments.reshape(TILES, 1, TILE), lse, delta, cos, sin, q_rows,
        q_cols, g_rows, g_cols, early, swap_core(early), late, swap_core(late),
    )

    late = late_mine.astype(f32) + swap_core(late_other).astype(f32)
    early = early_mine.astype(f32) + swap_core(early_other).astype(f32)
    own, across = early[:TOK], early[4 * TOK :]
    parts = [early[k * TOK : (k + 1) * TOK].astype(bf16) for k in (1, 2, 3)]
    parts += [late[k * TOK : (k + 1) * TOK].astype(bf16) for k in range(3)]
    own, across, parts = lax.optimization_barrier((own, across, parts))
    far = [shift_y(parts[2 + k], -k) for k in (1, 2, 3)]
    near = [shift_y(parts[k - 1], -k) for k in (1, 2, 3)]
    across = across + sum(p.astype(f32) for p in far)
    across, query_grad = lax.optimization_barrier((across.astype(bf16), query_grad))
    across = swap_zh(across)
    part, near = lax.optimization_barrier((query_part(query_grad, w_query), near))
    send = project(part, own, across, near, cos, sin, key_weight, value_weight)
    return last_sum(lax.all_to_all(send.reshape(8, 640, TOK), TP, 0, 0))


def solution(mesh):
    fine = Mesh(mesh.devices.reshape(4, 2, 2, 4, 2), ("y", "zh", "core", "x", "zl"))
    in_specs = (
        P(CTX, TP),
        P(CTX, TP),
        P(CTX, TP),
        P(CTX, TP),
        P(CTX, TP),
        P(TP, CTX),
        P(),
        P(CTX),
        P(),
        P(None, TP),
        P(None, TP),
        P(None, TP),
    )
    return jax.shard_map(
        local, mesh=fine, in_specs=in_specs, out_specs=P(TP, CTX), check_vma=False
    )
```

```python
import numpy as np
import jax
import jax.numpy as jnp
from jax import lax
from jax.experimental import pallas as pl
from jax.experimental.pallas import tpu as pltpu
from jax.sharding import Mesh, PartitionSpec as P

HEAD = 128
TILE = 128
GROUPS = 5
TOK = 256
TILES = 32
ROWS = GROUPS * TILE
SCALE = HEAD**-0.5
ROPE_BASE = 1000000.0
LOG2E = 1.4426950408889634
CTX = ("y", "zh", "core")
TP = ("x", "zl")

f32 = jnp.float32
bf16 = jnp.bfloat16


def shift(x, axes, sizes, offs):
    perm = []
    for source in np.ndindex(*sizes):
        dest = tuple((a + o) % s for a, o, s in zip(source, offs, sizes))
        perm.append(
            (int(np.ravel_multi_index(source, sizes)), int(np.ravel_multi_index(dest, sizes)))
        )
    return lax.ppermute(x, axes, perm)


def shift_y(x, k):
    return shift(x, ("y",), (4,), (k % 4,))


def swap_zh(x):
    return shift(x, ("zh",), (2,), (1,))


def swap_core(x):
    return shift(x, ("core",), (2,), (1,))


INVERSE = np.power(np.float64(ROPE_BASE), -np.arange(HEAD // 2) * (2.0 / HEAD)).astype(np.float32)


def half_sign(shape, axis):
    return jnp.where(lax.broadcasted_iota(jnp.int32, shape, axis) < HEAD // 2, -1.0, 1.0).astype(f32)


def block_kernel(key, value, positions, inverse, cos, sin, block):
    sign = half_sign((TILE, HEAD), 1)
    low = lax.broadcasted_iota(jnp.int32, (TILE, HEAD), 1) < HEAD // 2
    places = [jnp.broadcast_to(positions[t].astype(f32), (TILE, TILE)).T for t in range(2)]
    angles = jnp.where(low, places[0], places[1]) * inverse[...]
    both_cos, both_sin = jnp.cos(angles), jnp.sin(angles)
    for t in range(2):
        tok = pl.ds(t * TILE, TILE)
        mine = low if t == 0 else jnp.logical_not(low)
        c = jnp.where(mine, both_cos, pltpu.roll(both_cos, HEAD // 2, 1))
        s = jnp.where(mine, both_sin, pltpu.roll(both_sin, HEAD // 2, 1))
        cos[tok, :] = c
        sin[tok, :] = s
        x = key[tok, :].astype(f32)
        block[tok, :HEAD] = (x * c + pltpu.roll(x, HEAD // 2, 1) * (s * sign)).astype(bf16)
        block[tok, HEAD:] = value[tok, :]


def prep_kernel(query, grad, att, cos, sin, small, q_rows, q_cols, g_rows, g_cols, delta):
    sign = half_sign((TILE, HEAD), 1)
    for t in range(2):
        tok = pl.ds(t * TILE, TILE)
        c, s = cos[tok, :], sin[tok, :] * sign
        for h in range(GROUPS):
            feat = pl.ds(h * HEAD, HEAD)
            lane = pl.ds(h * TILE, TILE)
            x = query[tok, feat].astype(f32)
            rot = (x * c + pltpu.roll(x, HEAD // 2, 1) * s).astype(bf16)
            q_rows[t, lane, :] = rot
            q_cols[t, :, lane] = rot.T
            g = grad[tok, feat]
            g_rows[t, lane, :] = g
            g_cols[t, :, lane] = g.T
            prod = g.astype(f32) * att[tok, feat].astype(f32)
            delta[t, :, lane] = jnp.sum(prod.T, axis=0, keepdims=True)


EARLY = 5


def attention_kernel(
    mask, info, seg, lse, delta, cos, sin, q_rows, q_cols, g_rows, g_cols,
    early_mine, early_other, late_mine, late_other,
    d_early_mine, d_early_other, d_late_mine, d_late_other, qg,
    kv, dkv, dq, lse_rows, lists, counts, flags,
):
    dq[...] = jnp.zeros_like(dq)
    for t in range(2):
        for h in range(GROUPS):
            row = lse[h : h + 1, t * TILE : (t + 1) * TILE]
            lse_rows[t, :, pl.ds(h * TILE, TILE)] = row * LOG2E
    me = info[0]
    q_tile = 2 * me
    groups = (
        (early_mine, d_early_mine, 0, 0, EARLY),
        (early_other, d_early_other, 1, 0, EARLY),
        (late_mine, d_late_mine, 0, EARLY, 8 - EARLY),
        (late_other, d_late_other, 1, EARLY, 8 - EARLY),
    )
    starts = (0, 2 * EARLY, 4 * EARLY, 4 * EARLY + 2 * (8 - EARLY))

    def needs(j, away, first_slot):
        slot = lax.shift_right_logical(j, 1) + first_slot
        back_y = (lax.shift_right_logical(me, 2) - slot) & 3
        back_zh = (me ^ (lax.shift_right_logical(slot, 1) & 2)) & 2
        tile = 2 * (4 * back_y + back_zh + ((me ^ away) & 1)) + (j & 1)
        return mask[q_tile, tile] > 0, mask[q_tile + 1, tile] > 0

    for t in range(2):
        lists[t, 0] = t
        counts[t] = 1
    kv[pl.ds(TILES * TILE, TILE), :] = jnp.zeros((TILE, 2 * HEAD), bf16)
    dkv[pl.ds(TILES * TILE, TILE), :] = jnp.zeros((TILE, 2 * HEAD), f32)
    for (source, dest, away, first_slot, slots), start in zip(groups, starts):

        def collect(j, carry):
            needed = needs(j, away, first_slot)
            flags[start + j] = jnp.where(needed[0] | needed[1], 1, 0)
            here = pl.ds(pl.multiple_of(j * TILE, TILE), TILE)
            there = pl.ds(pl.multiple_of((start + j) * TILE, TILE), TILE)

            @pl.when(needed[0] | needed[1])
            def _():
                kv[there, :] = source[here, :]
                dkv[there, :] = jnp.zeros((TILE, 2 * HEAD), f32)

            @pl.when(jnp.logical_not(needed[0] | needed[1]))
            def _():
                dest[here, :] = jnp.zeros((TILE, 2 * HEAD), bf16)

            for t in range(2):
                add = needed[t]
                if start == 0:
                    add = add & (j != t)

                @pl.when(add)
                def _():
                    count = counts[t]
                    lists[t, count] = start + j
                    counts[t] = count + 1

            return carry

        lax.fori_loop(0, 2 * slots, collect, 0, unroll=True)

    def two_tiles(t, first, second, allowed):
        ones = pl.ds(pl.multiple_of(first * TILE, TILE), TILE)
        twos = pl.ds(pl.multiple_of(second * TILE, TILE), TILE)
        keys = jnp.concatenate([kv[ones, :HEAD], kv[twos, :HEAD]], 0)
        vals = jnp.concatenate([kv[ones, HEAD:], kv[twos, HEAD:]], 0)
        scores = jnp.dot(keys, q_cols[t], preferred_element_type=f32)
        probs = jnp.exp2(scores * (SCALE * LOG2E) - lse_rows[t])
        if allowed is not None:
            probs = jnp.concatenate([jnp.where(allowed, probs[:TILE], 0.0), probs[TILE:]], 0)
        dprobs = jnp.dot(vals, g_cols[t], preferred_element_type=f32)
        dscore = (probs * (dprobs - delta[t])).astype(bf16)
        probs = probs.astype(bf16)
        dkeys = jnp.dot(dscore, q_rows[t], preferred_element_type=f32)
        dvals = jnp.dot(probs, g_rows[t], preferred_element_type=f32)
        dqs = jnp.dot(keys.T, dscore, preferred_element_type=f32)
        return t, ones, twos, dkeys, dvals, dqs

    def add(t, ones, twos, dkeys, dvals, dqs):
        dq[t] += dqs
        dkv[ones, :HEAD] += dkeys[:TILE]
        dkv[ones, HEAD:] += dvals[:TILE]
        dkv[twos, :HEAD] += dkeys[TILE:]
        dkv[twos, HEAD:] += dvals[TILE:]

    most = jnp.maximum(counts[0], counts[1])

    def fill(i, carry):
        for t in range(2):

            @pl.when(i >= counts[t])
            def _():
                lists[t, i] = TILES

        return carry

    lax.fori_loop(jnp.minimum(counts[0], counts[1]), most + 1, fill, 0)
    causal = lax.broadcasted_iota(jnp.int32, (TILE, TILE), 0) <= (
        lax.broadcasted_iota(jnp.int32, (TILE, TILE), 1)
    )
    terms = []
    for t in range(2):
        row = jnp.broadcast_to(seg[q_tile + t], (TILE, TILE)).astype(f32)
        listed = jnp.where(mask[q_tile + t, q_tile + t] > 0, 1.0, 0.0)
        one = jnp.where((row.T == row) & causal, 1.0, 0.0) * listed
        terms.append(two_tiles(t, t, lists[t, 1], jnp.concatenate([one] * GROUPS, 1) > 0.5))
    for term in terms:
        add(*term)

    def rest(i, carry):
        terms = [two_tiles(t, lists[t, 2 * i], lists[t, 2 * i + 1], None) for t in range(2)]
        for term in terms:
            add(*term)
        return carry

    lax.fori_loop(1, lax.shift_right_logical(most + 1, 1), rest, 0)

    for (source, dest, away, first_slot, slots), start in zip(groups, starts):

        def give(j, carry):
            @pl.when(flags[start + j] > 0)
            def _():
                here = pl.ds(pl.multiple_of(j * TILE, TILE), TILE)
                there = pl.ds(pl.multiple_of((start + j) * TILE, TILE), TILE)
                dest[here, :] = dkv[there, :].astype(bf16)

            return carry

        lax.fori_loop(0, 2 * slots, give, 0, unroll=True)

    for t in range(2):
        tok = pl.ds(t * TILE, TILE)
        c, s = cos[tok, :].T, sin[tok, :].T
        for h in range(GROUPS):
            g = dq[t, :, pl.ds(h * TILE, TILE)] * SCALE
            u = g * s
            half = HEAD // 2
            turned = jnp.concatenate([u[half:], -u[:half]], 0)
            qg[pl.ds(h * HEAD, HEAD), tok] = (g * c + turned).astype(bf16)


def vmem(n):
    return [pl.BlockSpec(memory_space=pltpu.VMEM)] * n


def prep(query, grad, att, cos, sin, small):
    s = jax.ShapeDtypeStruct
    return pl.pallas_call(
        prep_kernel,
        out_shape=(
            s((2, ROWS, HEAD), bf16),
            s((2, HEAD, ROWS), bf16),
            s((2, ROWS, HEAD), bf16),
            s((2, HEAD, ROWS), bf16),
            s((2, 1, ROWS), f32),
        ),
        in_specs=vmem(6),
        out_specs=tuple(vmem(5)),
        compiler_params=pltpu.CompilerParams(vmem_limit_bytes=12 << 20),
        cost_estimate=pl.CostEstimate(flops=1000000, bytes_accessed=10000, transcendentals=0),
        name="prep",
    )(query, grad, att, cos, sin, small)


def attention(mask, info, *operands):
    s = jax.ShapeDtypeStruct
    early, late = (s((n * TOK, 2 * HEAD), bf16) for n in (EARLY, 8 - EARLY))
    return pl.pallas_call(
        attention_kernel,
        out_shape=(early, early, late, late, s((ROWS, TOK), bf16)),
        in_specs=[pl.BlockSpec(memory_space=pltpu.SMEM)] * 2 + vmem(len(operands)),
        out_specs=tuple(vmem(5)),
        scratch_shapes=[
            pltpu.VMEM(((TILES + 1) * TILE, 2 * HEAD), bf16),
            pltpu.VMEM(((TILES + 1) * TILE, 2 * HEAD), f32),
            pltpu.VMEM((2, HEAD, ROWS), f32),
            pltpu.VMEM((2, 1, ROWS), f32),
            pltpu.SMEM((2, TILES + 1), jnp.int32),
            pltpu.SMEM((2,), jnp.int32),
            pltpu.SMEM((TILES,), jnp.int32),
        ],
        compiler_params=pltpu.CompilerParams(vmem_limit_bytes=16 << 20),
        cost_estimate=pl.CostEstimate(
            flops=2000000000, bytes_accessed=8000000, transcendentals=1000000
        ),
        name="attention",
    )(mask, info, *operands)


def make_block(key, value, positions):
    s = jax.ShapeDtypeStruct
    inverse = jnp.asarray(np.concatenate([INVERSE, INVERSE])[None, :])
    return pl.pallas_call(
        block_kernel,
        out_shape=(s((TOK, HEAD), f32), s((TOK, HEAD), f32), s((TOK, 2 * HEAD), bf16)),
        in_specs=vmem(4),
        out_specs=tuple(vmem(3)),
        cost_estimate=pl.CostEstimate(flops=5000000, bytes_accessed=700000, transcendentals=60000),
        name="block",
    )(key, value, positions.reshape(2, 1, TILE), inverse)


WIDTH = 5120
STEP_ROWS = 640


def query_part_kernel(qg, wq, out):
    def step(i, carry):
        rows = pl.ds(pl.multiple_of(i * STEP_ROWS, STEP_ROWS), STEP_ROWS)
        out[rows, :] = jnp.dot(wq[rows, :], qg[...], preferred_element_type=f32).astype(bf16)
        return carry

    lax.fori_loop(0, WIDTH // STEP_ROWS, step, 0)


def query_part(qg, wq):
    return pl.pallas_call(
        query_part_kernel,
        out_shape=jax.ShapeDtypeStruct((WIDTH, TOK), bf16),
        in_specs=vmem(2),
        out_specs=vmem(1)[0],
        compiler_params=pltpu.CompilerParams(vmem_limit_bytes=16 << 20),
        cost_estimate=pl.CostEstimate(
            flops=1700000000, bytes_accessed=9000000, transcendentals=0
        ),
        name="query_part",
    )(qg, wq)


def project_kernel(part, own, across, near1, near2, near3, cos, sin, wk, wv, out, grads):
    total = own[...].astype(f32) + across[...].astype(f32)
    for near in (near1, near2, near3):
        total += near[...].astype(f32)
    sign = half_sign((TOK, HEAD), 1)
    g = total[:, :HEAD] * SCALE
    key_grad = g * cos[...] - pltpu.roll(g * sin[...], HEAD // 2, 1) * sign
    grads[:HEAD, :] = key_grad.T.astype(bf16)
    grads[HEAD:, :] = total[:, HEAD:].T.astype(bf16)

    def step(i, carry):
        rows = pl.ds(pl.multiple_of(i * STEP_ROWS, STEP_ROWS), STEP_ROWS)
        weights = jnp.concatenate([wk[rows, :], wv[rows, :]], 1)
        result = jnp.dot(weights, grads[...], preferred_element_type=f32)
        out[rows, :] = (part[rows, :].astype(f32) + result).astype(bf16)
        return carry

    lax.fori_loop(0, WIDTH // STEP_ROWS, step, 0, unroll=True)


def project(part, own, across, near, cos, sin, wk, wv):
    return pl.pallas_call(
        project_kernel,
        out_shape=jax.ShapeDtypeStruct((WIDTH, TOK), bf16),
        in_specs=vmem(10),
        out_specs=vmem(1)[0],
        scratch_shapes=[pltpu.VMEM((2 * HEAD, TOK), bf16)],
        compiler_params=pltpu.CompilerParams(vmem_limit_bytes=16 << 20),
        cost_estimate=pl.CostEstimate(
            flops=700000000, bytes_accessed=6000000, transcendentals=0
        ),
        name="project",
    )(part, own, across, *near, cos, sin, wk, wv)


def last_kernel(parts, out):
    def step(i, carry):
        rows = pl.ds(pl.multiple_of(i * TILE, TILE), TILE)
        terms = [parts[k, rows, :].astype(f32) for k in range(8)]
        while len(terms) > 1:
            terms = [p + q for p, q in zip(terms[::2], terms[1::2])]
        total = terms[0]
        out[rows, :] = total.astype(bf16)
        return carry

    lax.fori_loop(0, 5, step, 0, unroll=True)


def last_sum(parts):
    return pl.pallas_call(
        last_kernel,
        out_shape=jax.ShapeDtypeStruct((640, TOK), bf16),
        in_specs=vmem(1),
        out_specs=vmem(1)[0],
        compiler_params=pltpu.CompilerParams(vmem_limit_bytes=16 << 20),
        cost_estimate=pl.CostEstimate(flops=1300000, bytes_accessed=3000000, transcendentals=0),
        name="last_sum",
    )(parts)


def local(
    query, key, value, att, grad, lse, block_mask, positions, segments, w_query, key_weight,
    value_weight,
):
    me = lax.axis_index(CTX)
    cos, sin, block = make_block(key, value, positions)

    across = swap_zh(block)
    small, again = lax.optimization_barrier((cos[:8] * SCALE, block))
    near = [shift_y(again, k) for k in (1, 2, 3)]
    across, query, grad, att = lax.optimization_barrier((across, query, grad, att))
    far = [shift_y(across, k) for k in (1, 2, 3)]
    q_rows, q_cols, g_rows, g_cols, delta = prep(query, grad, att, cos, sin, small)
    early = jnp.concatenate([block] + near + [across], 0)
    late = jnp.concatenate(far, 0)

    early_mine, early_other, late_mine, late_other, query_grad = attention(
        block_mask, me.reshape(1), segments.reshape(TILES, 1, TILE), lse, delta, cos, sin, q_rows,
        q_cols, g_rows, g_cols, early, swap_core(early), late, swap_core(late),
    )

    late = late_mine.astype(f32) + swap_core(late_other).astype(f32)
    early = early_mine.astype(f32) + swap_core(early_other).astype(f32)
    own, across = early[:TOK], early[4 * TOK :]
    parts = [early[k * TOK : (k + 1) * TOK].astype(bf16) for k in (1, 2, 3)]
    parts += [late[k * TOK : (k + 1) * TOK].astype(bf16) for k in range(3)]
    own, across, parts = lax.optimization_barrier((own, across, parts))
    far = [shift_y(parts[2 + k], -k) for k in (1, 2, 3)]
    near = [shift_y(parts[k - 1], -k) for k in (1, 2, 3)]
    across = across + sum(p.astype(f32) for p in far)
    across, query_grad = lax.optimization_barrier((across.astype(bf16), query_grad))
    across = swap_zh(across)
    part, near = lax.optimization_barrier((query_part(query_grad, w_query), near))
    send = project(part, own, across, near, cos, sin, key_weight, value_weight)
    return last_sum(lax.all_to_all(send.reshape(8, 640, TOK), TP, 0, 0))


def solution(mesh):
    fine = Mesh(mesh.devices.reshape(4, 2, 2, 4, 2), ("y", "zh", "core", "x", "zl"))
    in_specs = (
        P(CTX, TP),
        P(CTX, TP),
        P(CTX, TP),
        P(CTX, TP),
        P(CTX, TP),
        P(TP, CTX),
        P(),
        P(CTX),
        P(),
        P(None, TP),
        P(None, TP),
        P(None, TP),
    )
    return jax.shard_map(
        local, mesh=fine, in_specs=in_specs, out_specs=P(TP, CTX), check_vma=False
    )
```
